512 devices in a mesh: tm: 128 (over y, x, z_lo), heads: 4 (over z_hi, core).
Axes of the slice: x: 4, y: 4, z: 16 (z_hi: 2, z_lo: 8; z = z_hi * 8 + z_lo), core: 2. Of those that a mesh axis runs over, the one named last changes fastest.
Arguments:
- queries: bfloat16 [32768, 1536], P('tm', 'heads'), may hold values from -30 to 30
- key_input: bfloat16 [32768, 1536], P('tm', 'heads'), may hold values from -30 to 30
- value_input: bfloat16 [32768, 1536], P('tm', 'heads'), may hold values from -6 to 6
- residual: bfloat16 [32768, 1536], P('tm', 'heads'), may hold values from -60 to 60
- out_weight: bfloat16 [1536, 1536], P('heads'), may hold values from -0.15625 to 0.15625
- norm_gain: float32 [1536], P('heads'), may hold values from 0.1 to 1.9
- conv_kernel: float32 [32, 1536], P(None, 'heads'), may hold values from -1 to 1
- cotangent: bfloat16 [32768, 1536], P('tm', 'heads'), may hold values from -6 to 6
- group_mask: int32 [128, 8], replicated, may hold values from 0 to 1, as said below
- group_len: int32 [128], replicated, may hold values from 128 to 256, as said below
Outputs:
- block_out: bfloat16 [32768, 1536], P('tm', 'heads')
- residual_grad: bfloat16 [32768, 1536], P('tm', 'heads')
- query_grad: bfloat16 [32768, 1536], P('tm', 'heads')
- key_grad: bfloat16 [32768, 1536], P('tm', 'heads')
- value_grad: bfloat16 [32768, 1536], P('tm', 'heads')
- gain_grad: float32 [1536], P('heads')
- kernel_grad: float32 [32, 1536], P(None, 'heads')
The draws below stay inside these ranges and needn't reach their ends.
Inputs may be any that keep to these rules, and one draw needn't show every extreme that they name: `group_mask`: entry [c, 0] is 1 for every group. `group_len`: at least one group is full.
All inputs are finite; a program needn't handle non-finite values.
Results may differ from the reference program's by a relative error of at most 0.014.
Values may be sent and summed in bfloat16 or wider, within the bound.
A program may use at most 128 MiB of HBM per device.

```python
import jax
import jax.numpy as jnp
from jax import lax

D = 1536
HEADS = 16
DH = 96
GROUP = 256
WIN = 8
KTAPS = 32
NCHUNK = 128
FRAMES = 32768


def draw_queries(key, part):
    key = jax.random.fold_in(key, 11)
    return jnp.clip(jax.random.normal(key, (FRAMES, D), jnp.float32), -6.0, 6.0).astype(jnp.bfloat16)


def draw_key_input(key, part):
    key = jax.random.fold_in(key, 12)
    return jnp.clip(jax.random.normal(key, (FRAMES, D), jnp.float32), -6.0, 6.0).astype(jnp.bfloat16)


def draw_residual(key, part):
    key = jax.random.fold_in(key, 13)
    key_base, key_rows, key_cols = jax.random.split(key, 3)
    base = jnp.clip(jax.random.normal(key_base, (FRAMES, D), jnp.float32), -6.0, 6.0)
    row_scale = jnp.exp(jax.random.uniform(key_rows, (FRAMES, 1), jnp.float32, -1.2, 1.1))
    col_scale = jnp.exp(jax.random.uniform(key_cols, (1, D), jnp.float32, -1.2, 1.1))
    return (base * row_scale * col_scale).astype(jnp.bfloat16)


def draw_group_mask(key, part):
    key = jax.random.fold_in(key, 21)
    key_level, key_coin = jax.random.split(key)
    level = jax.random.randint(key_level, (NCHUNK, 1), 0, 4)
    coin = jax.random.randint(key_coin, (NCHUNK, WIN), 0, 4)
    bits = (coin <= level).astype(jnp.int32)
    return bits.at[:, 0].set(1)


def draw_group_len(key, part):
    key = jax.random.fold_in(key, 22)
    key_len, key_full = jax.random.split(key)
    lengths = jax.random.randint(key_len, (NCHUNK,), GROUP // 2, GROUP + 1)
    full_at = jax.random.randint(key_full, (), 0, NCHUNK)
    return lengths.at[full_at].set(GROUP)


def steps_of(rng, shape, shards, smallest, top_value):
    def one(dim, blocks):
        draws = jax.random.uniform(jax.random.fold_in(jax.random.fold_in(rng, 6), dim), (blocks,), jnp.float32, smallest / len(shards), top_value / len(shards))
        return jnp.repeat(jnp.exp(draws), shape[dim] // blocks).reshape((-1,) + (1,) * (len(shape) - dim - 1))

    gain = one(*shards[0])
    for cut in shards[1:]:
        gain = gain * one(*cut)
    return gain


def centred(own_key, dims, deviation, bound, pieces=(), kind=jnp.bfloat16):
    entries = deviation * jax.random.normal(own_key, dims, jnp.float32)
    if pieces:
        entries = entries * steps_of(own_key, dims, pieces, -0.22, 0.18)
    return jnp.clip(entries, -bound, bound).astype(kind)


def setup_inputs(seed: int = 0) -> dict:
    streams_of = jax.random.split(jax.random.key(seed), 11)
    queries = draw_queries(jax.random.fold_in(streams_of[10], 71), 0)
    key_input = draw_key_input(jax.random.fold_in(streams_of[10], 71), 0)
    value_input = centred(streams_of[2], (FRAMES, D), 1.0, 6.0, ((0, 128), (1, 4)))
    residual = draw_residual(jax.random.fold_in(streams_of[10], 71), 0)
    out_weight = centred(streams_of[4], (D, D), D ** -0.5, 0.15625, ((0, 4),))
    norm_gain = jnp.clip(1.0 + 0.18 * jax.random.normal(streams_of[5], (D,), jnp.float32), 0.1, 1.9)
    conv_kernel = centred(streams_of[6], (KTAPS, D), KTAPS ** -0.5, 1.0, ((1, 4),), jnp.float32)
    cotangent = centred(streams_of[7], (FRAMES, D), 1.0, 6.0, ((0, 128), (1, 4)))
    group_mask = draw_group_mask(jax.random.fold_in(streams_of[10], 71), 0)
    group_len = draw_group_len(jax.random.fold_in(streams_of[10], 71), 0)
    return dict(queries=queries, key_input=key_input, value_input=value_input, residual=residual, out_weight=out_weight, norm_gain=norm_gain, conv_kernel=conv_kernel, cotangent=cotangent, group_mask=group_mask, group_len=group_len)


def key_allowed(group_mask, group_len, query_group, first_key, key_groups):
    group_total = group_mask.shape[0]
    key_group = first_key + jnp.arange(key_groups, dtype=jnp.int32)
    lag_groups = query_group - key_group
    row_bits = lax.dynamic_slice(group_mask, (jnp.clip(query_group, 0, group_total - 1).astype(jnp.int32), jnp.int32(0)), (1, WIN))[0]
    lag_bit = lax.optimization_barrier(jnp.sum(jnp.where(lag_groups[:, None] == jnp.arange(WIN, dtype=jnp.int32)[None, :], row_bits[None, :], 0), axis=1))
    key_len = lax.optimization_barrier(jnp.sum(jnp.where(key_group[:, None] == jnp.arange(group_total, dtype=jnp.int32)[None, :], group_len[None, :], 0), axis=1))
    usable = (key_group >= 0) & (lag_groups >= 0) & (lag_groups < WIN) & (query_group < group_total) & (lag_bit == 1)
    inside = jnp.arange(GROUP, dtype=jnp.int32)
    return (usable[:, None] & (inside[None, :] < key_len[:, None])).reshape(key_groups * GROUP)

def weights_from(scores, allowed):
    masked = jnp.where(allowed[None, None, :], scores, -1e+30)
    row_top = lax.optimization_barrier(jnp.max(masked, axis=2, keepdims=True))
    raised = jnp.where(allowed[None, None, :], jnp.exp(masked - row_top), 0.0)
    summed = lax.optimization_barrier(jnp.sum(raised, axis=2, keepdims=True))
    return (raised / summed, row_top, summed)

def rounded(array):
    return lax.optimization_barrier(array.astype(jnp.bfloat16)).astype(jnp.float32)

def reference(queries, key_input, value_input, residual, out_weight, norm_gain, conv_kernel, cotangent, group_mask, group_len):
    frames = queries.shape[0]
    group_count = frames // GROUP
    scaling = DH ** (-0.5)
    lead_rows = (WIN - 1) * GROUP
    query_heads = queries.astype(jnp.float32).reshape(frames, HEADS, DH)
    zero_lead = jnp.zeros((lead_rows, HEADS, DH), jnp.float32)
    key_heads = jnp.concatenate([zero_lead, key_input.astype(jnp.float32).reshape(frames, HEADS, DH)], axis=0)
    value_heads = jnp.concatenate([zero_lead, value_input.astype(jnp.float32).reshape(frames, HEADS, DH)], axis=0)

    def gather_window(block_index):
        query_block = lax.dynamic_slice_in_dim(query_heads, block_index * GROUP, GROUP, 0)
        key_block = lax.dynamic_slice_in_dim(key_heads, block_index * GROUP, WIN * GROUP, 0)
        value_block = lax.dynamic_slice_in_dim(value_heads, block_index * GROUP, WIN * GROUP, 0)
        allowed = key_allowed(group_mask, group_len, block_index, block_index - WIN + 1, WIN)
        scores = jnp.einsum('qhd,khd->hqk', query_block, key_block) * scaling
        weights, _, _ = weights_from(scores, allowed)
        return (query_block, key_block, value_block, weights)

    def forward_group(block_index):
        _, _, value_block, weights = gather_window(block_index)
        mixed_heads = jnp.einsum('hqk,khd->qhd', rounded(weights), value_block)
        return mixed_heads.astype(jnp.bfloat16).reshape(GROUP, D)
    indices = jnp.arange(group_count, dtype=jnp.int32)
    attended = lax.map(forward_group, indices).reshape(frames, D)
    mixed_rows = residual.astype(jnp.float32) + jnp.dot(attended, out_weight, preferred_element_type=jnp.float32)
    centre_row = lax.optimization_barrier(jnp.sum(mixed_rows, axis=1, keepdims=True)) / D
    inverse = lax.rsqrt(lax.optimization_barrier(jnp.sum(mixed_rows * mixed_rows, axis=1, keepdims=True)) / D - centre_row * centre_row + 1e-05)
    standard = (mixed_rows - centre_row) * inverse
    normed = (standard * norm_gain).astype(jnp.bfloat16)
    half_taps = KTAPS // 2
    padded_norm = jnp.pad(normed.astype(jnp.float32), ((half_taps, half_taps), (0, 0)))
    convolved = sum((conv_kernel[m] * padded_norm[m:m + frames] for m in range(KTAPS)))
    gating = jax.nn.sigmoid(convolved)
    block_out = (mixed_rows + convolved * gating).astype(jnp.bfloat16)
    incoming = cotangent.astype(jnp.float32)
    conv_grad = incoming * gating * (1.0 + convolved * (1.0 - gating))
    padded_grad = jnp.pad(conv_grad, ((half_taps, half_taps), (0, 0)))
    normed_grad = sum((conv_kernel[m] * padded_grad[2 * half_taps - m:2 * half_taps - m + frames] for m in range(KTAPS)))
    kernel_grad = jnp.stack([lax.optimization_barrier(jnp.sum(conv_grad * padded_norm[m:m + frames], axis=0)) for m in range(KTAPS)])
    gain_grad = lax.optimization_barrier(jnp.sum(normed_grad * standard, axis=0))
    scaled_grad = normed_grad * norm_gain
    grad_mean = lax.optimization_barrier(jnp.sum(scaled_grad, axis=1, keepdims=True))
    grad_proj = lax.optimization_barrier(jnp.sum(scaled_grad * standard, axis=1, keepdims=True))
    residual_grad = (incoming + inverse * (scaled_grad - grad_mean / D - standard * grad_proj / D)).astype(jnp.bfloat16)
    attended_grad = jnp.dot(residual_grad, out_weight.T, preferred_element_type=jnp.float32).astype(jnp.bfloat16)
    grad_heads = attended_grad.astype(jnp.float32).reshape(frames, HEADS, DH)

    def backward_group(state_pair, block_index):
        key_sum, value_sum = state_pair
        query_block, key_block, value_block, weights = gather_window(block_index)
        grad_block = lax.dynamic_slice_in_dim(grad_heads, block_index * GROUP, GROUP, 0)
        weight_grad = jnp.einsum('qhd,khd->hqk', grad_block, value_block)
        centre = lax.optimization_barrier(jnp.sum(weights * weight_grad, axis=2, keepdims=True))
        score_grad = rounded(weights * (weight_grad - centre))
        query_part = (jnp.einsum('hqk,khd->qhd', score_grad, key_block) * scaling).astype(jnp.bfloat16)
        key_part = jnp.einsum('hqk,qhd->khd', score_grad, query_block) * scaling
        value_part = jnp.einsum('hqk,qhd->khd', rounded(weights), grad_block)
        offset = block_index * GROUP
        key_sum = lax.dynamic_update_slice_in_dim(key_sum, lax.dynamic_slice_in_dim(key_sum, offset, WIN * GROUP, 0) + key_part, offset, 0)
        value_sum = lax.dynamic_update_slice_in_dim(value_sum, lax.dynamic_slice_in_dim(value_sum, offset, WIN * GROUP, 0) + value_part, offset, 0)
        return ((key_sum, value_sum), query_part.reshape(GROUP, D))
    zero_block = jnp.zeros((lead_rows + frames, HEADS, DH), jnp.float32)
    (key_sum, value_sum), query_parts = lax.scan(backward_group, (zero_block, zero_block), indices)
    query_grad = query_parts.reshape(frames, D)
    key_grad = key_sum[lead_rows:].reshape(frames, D).astype(jnp.bfloat16)
    value_grad = value_sum[lead_rows:].reshape(frames, D).astype(jnp.bfloat16)
    return (block_out, residual_grad, query_grad, key_grad, value_grad, gain_grad, kernel_grad)
```

```python
import functools

import jax
import jax.numpy as jnp
from jax import lax
from jax.experimental import pallas as pl
from jax.experimental.pallas import tpu as pltpu
from jax.sharding import PartitionSpec as P

D = 1536
DH = 96
GROUP = 256
WIN = 8
HEADS_HERE = 4
COLS = 384
RUN = 8
TAPS = 32
SCALE = DH ** (-0.5)
SCALE2 = SCALE * 1.4426950408889634
NEG = -1e30
F32 = jnp.float32
BF16 = jnp.bfloat16
VMEM_LIMIT = 50 * 1024 * 1024

TN = (((0,), (0,)), ((), ()))
NT = (((1,), (1,)), ((), ()))
NN = (((1,), (0,)), ((), ()))


def dot(a, b, dims):
    return lax.dot_general(a, b, dims, preferred_element_type=F32)


def remote(src, dst, send_sem, recv_sem, where):
    return pltpu.make_async_remote_copy(
        src_ref=src,
        dst_ref=dst,
        send_sem=send_sem,
        recv_sem=recv_sem,
        device_id=where,
        device_id_type=pl.DeviceIdType.MESH,
    )


def greet(places):
    barrier = pltpu.get_barrier_semaphore()
    for where in places:
        pl.semaphore_signal(barrier, inc=1, device_id=where, device_id_type=pl.DeviceIdType.MESH)
    pl.semaphore_wait(barrier, len(places))


def window_limit(gm_ref, gl_ref, t, b):
    source = jnp.maximum(t - b, 0)
    return jnp.where(t >= b, gm_ref[t, b] * gl_ref[source], 0)


def head_rows(h):
    return slice(h * DH, (h + 1) * DH)


def gather_attend(
    q_ref, k_ref, v_ref, gm_ref, gl_ref,
    att_ref, lse_ref, qt_ref, win_ref,
    kv, acc, m_s, l_s, send, xsend, recv, out_sem,
):
    t, hd = lax.axis_index("tm"), lax.axis_index("heads")
    n = lax.axis_size("tm")
    z = lax.rem(t, RUN)
    ring = [lax.rem(t + by, n) for by in (1, n - 1, RUN, n - RUN)]
    greet([(to, hd) for to in ring])

    kv[0, 0] = k_ref[...].T
    kv[0, 1] = v_ref[...].T
    for i in range(2):
        @pl.when(z >= 1)
        def _(i=i):
            remote(kv.at[0, i], kv.at[8, i], xsend.at[i], recv.at[8, i], (ring[2], hd)).start()

        @pl.when(z < RUN - 1)
        def _(i=i):
            remote(kv.at[0, i], kv.at[1, i], send.at[0, i], recv.at[1, i], (ring[0], hd)).start()

    qt_ref[...] = q_ref[...].T
    m_s[...] = jnp.full(m_s.shape, NEG, F32)
    l_s[...] = jnp.zeros(l_s.shape, F32)
    acc[...] = jnp.zeros(acc.shape, F32)

    def attend(b):
        limit = window_limit(gm_ref, gl_ref, t, b)
        for h in range(HEADS_HERE):
            rows = head_rows(h)
            s = dot(kv[b, 0, rows, :], qt_ref[rows, :], TN)
            inside = lax.broadcasted_iota(jnp.int32, s.shape, 0) < limit
            s = jnp.where(inside, s * SCALE2, NEG)
            m_old = m_s[h : h + 1, :]
            m_new = jnp.maximum(m_old, jnp.max(s, axis=0, keepdims=True))
            alpha = jnp.exp2(m_old - m_new)
            p = jnp.exp2(s - m_new)
            m_s[h : h + 1, :] = m_new
            l_s[h : h + 1, :] = l_s[h : h + 1, :] * alpha + jnp.sum(p, axis=0, keepdims=True)
            acc[rows, :] = acc[rows, :] * alpha + dot(kv[b, 1, rows, :], p.astype(BF16), NN)

    def forward(b, i):
        upward = b <= z
        to = jnp.where(upward, ring[0], ring[1])
        slot = jnp.where(upward, b + 1, b - 1)
        return remote(kv.at[b, i], kv.at[slot, i], send.at[b, i], recv.at[slot, i], (to, hd))

    def sends_on(b):
        return jnp.where(b <= z, z < RUN - 1, z >= 1)

    def arrive(b):
        for i in range(2):
            remote(kv.at[b, i], kv.at[b, i], send.at[b, i], recv.at[b, i], (ring[0], hd)).wait_recv()

            @pl.when(sends_on(b))
            def _(i=i):
                forward(b, i).start()

    attend(0)

    @pl.when(z >= 1)
    def _():
        arrive(8)

    few = jnp.minimum(z, RUN - 1 - z)

    def slot_of(j):
        pair = j // 2 + 1
        paired = jnp.where(lax.rem(j, 2) == 0, pair, 8 - pair)
        rest = j - few + 1
        single = jnp.where(2 * z > RUN - 1, rest, 8 - rest)
        return jnp.where(j < 2 * few, paired, single)

    def step(j, carry):
        b = slot_of(j)
        arrive(b)
        attend(b)
        return carry

    lax.fori_loop(0, 7, step, 0)
    keep = pltpu.make_async_copy(kv.at[pl.ds(0, WIN)], win_ref, out_sem)
    keep.start()
    for h in range(HEADS_HERE):
        rows = head_rows(h)
        att_ref[rows, :] = (acc[rows, :] / l_s[h : h + 1, :]).astype(BF16)
    lse_ref[...] = jnp.where(
        lax.broadcasted_iota(jnp.int32, lse_ref.shape, 0) < HEADS_HERE,
        m_s[...] + jnp.log2(jnp.maximum(l_s[...], 1e-30)),
        0.0,
    )
    for i in range(2):
        @pl.when(z >= 1)
        def _(i=i):
            remote(kv.at[0, i], kv.at[8, i], xsend.at[i], recv.at[8, i], (ring[2], hd)).wait_send()

        @pl.when(z < RUN - 1)
        def _(i=i):
            remote(kv.at[0, i], kv.at[1, i], send.at[0, i], recv.at[1, i], (ring[0], hd)).wait_send()

        @pl.when(z >= 1)
        def _(i=i):
            forward(8, i).wait_send()

    def drain(b, carry):
        for i in range(2):
            @pl.when(sends_on(b))
            def _(i=i):
                forward(b, i).wait_send()
        return carry

    lax.fori_loop(1, 8, drain, 0)
    keep.wait()


def middle(
    att_ref, w_ref, res_ref, gain_ref, ck_ref, cot_ref,
    out_ref, rg_ref, dot_ref, kg_ref,
    dsend, drecv, pfar, fsend, frecv, mixed, stats, stats2, turn, standard,
    hn, hc, pn, cg, cote, silu, ng, kacc, kpart, rz, rx, ry, rgall, racc,
    ssem, rsem, zs, zr, gs, gr, xs, xr, ys, yr,
):
    t, hd = lax.axis_index("tm"), lax.axis_index("heads")
    n = lax.axis_size("tm")
    zh, core = hd // 2, lax.rem(hd, 2)
    partner = hd + 1 - 2 * core
    far = lax.rem(hd + 2, 4)
    diag = lax.rem(partner + 2, 4)
    z, x, y = lax.rem(t, RUN), lax.rem(t // RUN, 4), t // (4 * RUN)
    after, before = lax.rem(t + 1, n), lax.rem(t + n - 1, n)

    def along_z(i):
        return ((t - z + i), hd)

    def along_x(i):
        return ((t + (i - x) * RUN), hd)

    def along_y(i):
        return ((t + (i - y) * 4 * RUN), hd)

    places = [(t, partner), (t, far), (t, diag), (after, hd), (before, hd)]
    places += [along_z(lax.rem(z + d, RUN)) for d in range(1, RUN)]
    places += [along_x(lax.rem(x + d, 4)) for d in range(1, 4)]
    places += [along_y(lax.rem(y + d, 4)) for d in range(1, 4)]
    greet(places)

    def cp(i, src, dst, where):
        return remote(src, dst, ssem.at[i], rsem.at[i], where)

    cot_up = cp(0, cot_ref.at[pl.ds(GROUP - 16, 16)], hc.at[0], (after, hd))
    cot_down = cp(1, cot_ref.at[pl.ds(0, 16)], hc.at[1], (before, hd))
    cot_up.start()
    cot_down.start()

    def project(j):
        cols = pl.ds(pl.multiple_of(j * COLS, 128), COLS)
        return dot(att_ref[...], w_ref[:, cols], TN)

    dsend[0] = project(diag)
    give_far = cp(2, dsend.at[0], drecv.at[0], (t, partner))
    give_far.start()
    pfar[...] = project(far)
    give_far.wait_recv()
    fsend[...] = (pfar[...] + drecv[0]).astype(BF16)
    cross = cp(3, fsend, frecv, (t, far))
    cross.start()
    dsend[1] = project(partner)
    give_near = cp(4, dsend.at[1], drecv.at[1], (t, partner))
    give_near.start()
    mixed[...] = project(hd) + res_ref[...].astype(F32)
    give_near.wait_recv()
    mixed[...] = mixed[...] + drecv[1]
    cot_up.wait_recv()
    cot_down.wait_recv()
    cote[16 : 16 + GROUP, :] = cot_ref[...].astype(F32)
    cote[0:16, :] = jnp.where(t > 0, hc[0].astype(F32), 0.0)
    cote[16 + GROUP :, :] = jnp.where(t < n - 1, hc[1].astype(F32), 0.0)
    cross.wait_recv()
    mixed[...] = mixed[...] + frecv[...].astype(F32)

    lane = lax.broadcasted_iota(jnp.int32, (GROUP, 128), 1)

    def over_heads(buf, first, a, b):
        both = jnp.where(lane == 0, a, jnp.where(lane == 1, b, 0.0))
        buf[pl.ds(hd, 1)] = both.T[0:8, :][None]
        copies = [
            cp(first + i, buf.at[hd], buf.at[hd], (t, lax.rem(hd + i + 1, 4))) for i in range(3)
        ]
        for c in copies:
            c.start()
        for c in copies:
            c.wait_recv()
        turn[...] = jnp.zeros(turn.shape, F32)
        turn[0:8, :] = buf[0] + buf[1] + buf[2] + buf[3]
        back = turn[...].T
        return copies, back[:, 0:1], back[:, 1:2]

    mx = mixed[...]
    stat_copies, row_sum, row_square = over_heads(
        stats, 5, jnp.sum(mx, axis=1, keepdims=True), jnp.sum(mx * mx, axis=1, keepdims=True)
    )
    centre = row_sum / D
    inverse = lax.rsqrt(row_square / D - centre * centre + 1e-05)
    standard[...] = (mixed[...] - centre) * inverse
    hn[2:, :, :] = (standard[...] * gain_ref[...]).astype(BF16).reshape(8, 32, COLS)
    norm_up = cp(8, hn.at[9], hn.at[0], (after, hd))
    norm_down = cp(9, hn.at[2], hn.at[1], (before, hd))
    norm_up.start()
    norm_down.start()
    pn[32 : 32 + GROUP, :] = hn[2:, :, :].astype(F32).reshape(GROUP, COLS)
    kacc[...] = jnp.zeros(kacc.shape, F32)
    norm_up.wait_recv()
    norm_down.wait_recv()
    pn[0:32, :] = jnp.where(t > 0, hn[0].astype(F32), 0.0)
    pn[32 + GROUP :, :] = jnp.where(t < n - 1, hn[1].astype(F32), 0.0)

    for cb in range(3):
        cols = slice(cb * 128, cb * 128 + 128)

        def convolve(i, carry, cols=cols):
            base = pl.multiple_of(i * 96, 32)
            rows = pn[pl.ds(base, 128), cols]
            total = jnp.zeros((96, 128), F32)
            for r in range(8):
                moved = rows[r : r + 120]
                for a in range(4):
                    m = 8 * a + r
                    total = total + ck_ref[m : m + 1, cols] * moved[8 * a : 8 * a + 96]
            gate = jax.nn.sigmoid(total)
            silu[pl.ds(base, 96), cols] = total * gate
            cg[pl.ds(base, 96), cols] = (
                cote[pl.ds(base, 96), cols] * gate * (1.0 + total * (1.0 - gate))
            )
            return carry

        lax.fori_loop(0, 3, convolve, 0)

    for cb in range(3):
        cols = slice(cb * 128, cb * 128 + 128)

        def backward(i, carry, cols=cols):
            base = pl.multiple_of(i * 64, 64)
            rows = cg[pl.ds(base, 96), cols]
            total = jnp.zeros((64, 128), F32)
            for r in range(8):
                moved = rows if r == 0 else rows[r : r + 88]
                for a in range(5 if r == 0 else 4):
                    u = 8 * a + r
                    if u == 0:
                        continue
                    m = 32 - u
                    total = total + ck_ref[m : m + 1, cols] * moved[8 * a : 8 * a + 64]
            ng[pl.ds(base, 64), cols] = total
            prod = total * standard[pl.ds(base, 64), cols]
            kacc[TAPS, :, cols] = kacc[TAPS, :, cols] + jnp.sum(prod.reshape(8, 8, 128), axis=0)
            grad = rows[16:80]
            normed = pn[pl.ds(base + 16, 96), cols]
            for r in range(8):
                moved = normed[r : r + 88]
                for a in range(4):
                    m = 8 * a + r
                    prod = grad * moved[8 * a : 8 * a + 64]
                    kacc[m, :, cols] = kacc[m, :, cols] + jnp.sum(prod.reshape(8, 8, 128), axis=0)
            return carry

        lax.fori_loop(0, 4, backward, 0)

    out_ref[...] = (mixed[...] + silu[16 : 16 + GROUP, :]).astype(BF16)

    kpart[...] = jnp.zeros(kpart.shape, F32)
    summed = jnp.sum(kacc[...], axis=1)
    for cb in range(3):
        kpart[cb * 40 : cb * 40 + 40, :] = summed[:, cb * 128 : cb * 128 + 128]

    def exchange(count, here, place, source, buf, ss, rs):
        def to(i):
            return remote(source(i), buf.at[here], ss.at[i], rs.at[here], place(i))

        for i in range(count):
            @pl.when(here != i)
            def _(i=i):
                to(i).start()

    def finish(count, here, place, source, buf, ss, rs):
        for i in range(count):
            @pl.when(here != i)
            def _(i=i):
                remote(source(i), buf.at[i], ss.at[i], rs.at[i], place(i)).wait()

    z_parts = (RUN, z, along_z, lambda i: kpart.at[pl.ds(16 * i, 16)], rz, zs, zr)
    exchange(*z_parts)
    rz[pl.ds(z, 1)] = kpart[pl.ds(pl.multiple_of(z * 16, 16), 16), :][None]

    sg = ng[...] * gain_ref[...]
    stat_copies2, grad_mean, grad_proj = over_heads(
        stats2, 10, jnp.sum(sg, axis=1, keepdims=True), jnp.sum(sg * standard[...], axis=1, keepdims=True)
    )
    grad = cote[16 : 16 + GROUP, :] + inverse * (
        ng[...] * gain_ref[...] - grad_mean / D - standard[...] * (grad_proj / D)
    )
    rgb = grad.astype(BF16)
    rg_ref[...] = rgb
    rgall[pl.ds(hd, 1)] = rgb[None]
    share_far = cp(13, rgall.at[hd], rgall.at[hd], (t, far))
    share_near = cp(14, rgall.at[hd], rgall.at[hd], (t, partner))
    share_far.start()
    share_near.start()

    def back(j):
        cols = pl.ds(pl.multiple_of(j * COLS, 128), COLS)
        rows = rgall[pl.ds(j, 1)].reshape(GROUP, COLS)
        return dot(w_ref[:, cols], rows, NT)

    racc[...] = back(hd)
    finish(*z_parts)
    rx[pl.ds(x, 1)] = sum((rz[i] for i in range(1, RUN)), rz[0])[None]
    x_parts = (4, x, along_x, lambda i: rx.at[x], rx, xs, xr)
    exchange(*x_parts)
    remote(rgall.at[partner], rgall.at[partner], ssem.at[14], rsem.at[14], (t, partner)).wait_recv()
    racc[...] = racc[...] + back(partner)
    finish(*x_parts)
    ry[pl.ds(y, 1)] = (rx[0] + rx[1] + rx[2] + rx[3])[None]
    y_parts = (4, y, along_y, lambda i: ry.at[y], ry, ys, yr)
    exchange(*y_parts)
    finish(*y_parts)
    total = ry[0] + ry[1] + ry[2] + ry[3]
    rz_all = kg_ref
    rz_all[pl.ds(z, 1)] = total[None]
    g_parts = (RUN, z, along_z, lambda i: kg_ref.at[z], kg_ref, gs, gr)
    exchange(*g_parts)

    remote(rgall.at[far], rgall.at[far], ssem.at[13], rsem.at[13], (t, far)).wait_recv()
    pass_on = cp(15, rgall.at[far], rgall.at[far], (t, partner))
    pass_on.start()
    racc[...] = racc[...] + back(far)
    remote(rgall.at[diag], rgall.at[diag], ssem.at[15], rsem.at[15], (t, partner)).wait_recv()
    dot_ref[...] = (racc[...] + back(diag)).astype(BF16)
    finish(*g_parts)
    for c in [cot_up, cot_down, give_far, cross, give_near, norm_up, norm_down]:
        c.wait_send()
    for c in stat_copies + stat_copies2 + [share_far, share_near, pass_on]:
        c.wait_send()


def attend_back(
    qt_ref, win_ref, att_ref, lse_ref, dot_ref, gm_ref, gl_ref,
    dq_ref, dk_ref, dv_ref,
    rin, rout, own, dq, delta, send, recv, xsend, xrecv,
):
    t, hd = lax.axis_index("tm"), lax.axis_index("heads")
    n = lax.axis_size("tm")
    z = lax.rem(t, RUN)
    ring = [lax.rem(t + by, n) for by in (1, n - 1, RUN, n - RUN)]
    greet([(to, hd) for to in ring])

    dq[...] = jnp.zeros(dq.shape, F32)
    for h in range(HEADS_HERE):
        rows = head_rows(h)
        both = dot_ref[rows, :].astype(F32) * att_ref[rows, :].astype(F32)
        delta[h : h + 1, :] = jnp.sum(both, axis=0, keepdims=True)

    def terms(b):
        limit = window_limit(gm_ref, gl_ref, t, b)
        for h in range(HEADS_HERE):
            rows = head_rows(h)
            kt, vt = win_ref[b, 0, rows, :], win_ref[b, 1, rows, :]
            qt, gt = qt_ref[rows, :], dot_ref[rows, :]
            s = dot(kt, qt, TN)
            inside = lax.broadcasted_iota(jnp.int32, s.shape, 0) < limit
            p = jnp.exp2(jnp.where(inside, s * SCALE2, NEG) - lse_ref[h : h + 1, :])
            dp = dot(vt, gt, TN)
            ds = (p * (dp - delta[h : h + 1, :])).astype(BF16)
            dq[rows, :] = dq[rows, :] + dot(kt, ds, NN)
            own[0, rows, :] = dot(qt, ds, NT) * SCALE
            own[1, rows, :] = dot(gt, p.astype(BF16), NT)

    def passing(b, i):
        upward = b > z
        to = jnp.where(upward, ring[0], ring[1])
        slot = jnp.where(upward, b + 1, b - 1)
        return remote(rout.at[b, i], rin.at[slot, i], send.at[b, i], recv.at[slot, i], (to, hd))

    def incoming(b):
        return jnp.where(b > z, z >= 1, z < RUN - 1)

    def wait_in(b, i):
        remote(rout.at[0, i], rin.at[b, i], send.at[0, i], recv.at[b, i], (ring[0], hd)).wait_recv()

    lead = jnp.maximum(7 - 2 * z, 2 * z - 7)
    down_leads = 2 * z > RUN - 1

    def slot_of(j):
        jj = j - lead
        leads = (j < lead) | (lax.rem(jj + 8, 2) == 0)
        place = jnp.where(j < lead, j, jnp.where(lax.rem(jj + 8, 2) == 0, lead + jj // 2, jj // 2))
        towards_lower = leads == down_leads
        return jnp.where(towards_lower, z - place, z + 1 + place)

    def step(j, carry):
        b = slot_of(j)
        terms(b)
        for i in range(2):
            @pl.when(incoming(b))
            def _(i=i):
                wait_in(b, i)
                rout[b, i] = (own[i] + rin[b, i].astype(F32)).astype(BF16)

            @pl.when(jnp.logical_not(incoming(b)))
            def _(i=i):
                rout[b, i] = own[i].astype(BF16)

            passing(b, i).start()
        return carry

    lax.fori_loop(0, 7, step, 0)
    terms(0)

    def cross(i):
        return remote(rin.at[8, i], rin.at[9, i], xsend.at[i], xrecv.at[i], (ring[3], hd))

    for i in range(2):
        @pl.when(z >= 1)
        def _(i=i):
            wait_in(8, i)
            cross(i).start()

    dq_ref[...] = (dq[...] * SCALE).astype(BF16).T
    for i in range(2):
        @pl.when(z < RUN - 1)
        def _(i=i):
            wait_in(0, i)
            own[i] = own[i] + rin[0, i].astype(F32)

    for i, ref in enumerate((dk_ref, dv_ref)):
        @pl.when(z >= 1)
        def _(i=i):
            cross(i).wait_recv()
            own[i] = own[i] + rin[9, i].astype(F32)

        ref[...] = own[i].astype(BF16).T

    def drain(b, carry):
        for i in range(2):
            passing(b, i).wait_send()
        return carry

    lax.fori_loop(1, 8, drain, 0)
    for i in range(2):
        @pl.when(z >= 1)
        def _(i=i):
            cross(i).wait_send()


VM = pl.BlockSpec(memory_space=pltpu.VMEM)
SM = pl.BlockSpec(memory_space=pltpu.SMEM)
HB = pl.BlockSpec(memory_space=pl.ANY)
DMA = pltpu.SemaphoreType.DMA


def shape(dims, kind=BF16):
    return jax.ShapeDtypeStruct(dims, kind)


def params(which):
    return pltpu.CompilerParams(
        collective_id=which, has_side_effects=True, vmem_limit_bytes=VMEM_LIMIT
    )


def body(
    queries, key_input, value_input, residual, out_weight, norm_gain, conv_kernel, cotangent,
    group_mask, group_len,
):
    turned = (COLS, GROUP)
    att, lse, qt, win = pl.pallas_call(
        gather_attend,
        out_shape=[shape(turned), shape((8, GROUP), F32), shape(turned), shape((WIN, 2) + turned)],
        in_specs=[VM, VM, VM, SM, SM],
        out_specs=[VM, VM, VM, HB],
        scratch_shapes=[
            pltpu.VMEM((9, 2) + turned, BF16),
            pltpu.VMEM(turned, F32),
            pltpu.VMEM((8, GROUP), F32),
            pltpu.VMEM((8, GROUP), F32),
            DMA((9, 2)),
            DMA((2,)),
            DMA((9, 2)),
            DMA,
        ],
        compiler_params=params(0),
        name="gather_attend",
    )(queries, key_input, value_input, group_mask, group_len)

    block = (GROUP, COLS)
    block_out, residual_grad, att_grad, kg = pl.pallas_call(
        middle,
        out_shape=[shape(block), shape(block), shape(turned), shape((8, 16, 128), F32)],
        in_specs=[VM] * 6,
        out_specs=[VM] * 4,
        scratch_shapes=[
            pltpu.VMEM((2,) + block, F32),
            pltpu.VMEM((2,) + block, F32),
            pltpu.VMEM(block, F32),
            pltpu.VMEM(block, BF16),
            pltpu.VMEM(block, BF16),
            pltpu.VMEM(block, F32),
            pltpu.VMEM((4, 8, GROUP), F32),
            pltpu.VMEM((4, 8, GROUP), F32),
            pltpu.VMEM((128, GROUP), F32),
            pltpu.VMEM(block, F32),
            pltpu.VMEM((10, 32, COLS), BF16),
            pltpu.VMEM((2, 16, COLS), BF16),
            pltpu.VMEM((GROUP + 64, COLS), F32),
            pltpu.VMEM((GROUP + 32, COLS), F32),
            pltpu.VMEM((GROUP + 32, COLS), F32),
            pltpu.VMEM((GROUP + 32, COLS), F32),
            pltpu.VMEM(block, F32),
            pltpu.VMEM((40, 8, COLS), F32),
            pltpu.VMEM((128, 128), F32),
            pltpu.VMEM((8, 16, 128), F32),
            pltpu.VMEM((4, 16, 128), F32),
            pltpu.VMEM((4, 16, 128), F32),
            pltpu.VMEM((4,) + block, BF16),
            pltpu.VMEM(turned, F32),
            DMA((16,)),
            DMA((16,)),
            DMA((8,)),
            DMA((8,)),
            DMA((8,)),
            DMA((8,)),
            DMA((4,)),
            DMA((4,)),
            DMA((4,)),
            DMA((4,)),
        ],
        compiler_params=params(1),
        name="middle",
    )(att, out_weight, residual, norm_gain.reshape(1, COLS), conv_kernel, cotangent)

    query_grad, key_grad, value_grad = pl.pallas_call(
        attend_back,
        out_shape=[shape(block)] * 3,
        in_specs=[VM, VM, VM, VM, VM, SM, SM],
        out_specs=[VM] * 3,
        scratch_shapes=[
            pltpu.VMEM((10, 2) + turned, BF16),
            pltpu.VMEM((8, 2) + turned, BF16),
            pltpu.VMEM((2,) + turned, F32),
            pltpu.VMEM(turned, F32),
            pltpu.VMEM((8, GROUP), F32),
            DMA((8, 2)),
            DMA((9, 2)),
            DMA((2,)),
            DMA((2,)),
        ],
        compiler_params=params(2),
        name="attend_back",
    )(qt, win, att, lse, att_grad, group_mask, group_len)

    flat = kg.reshape(128, 128)[:120].reshape(3, 40, 128)
    wide = jnp.concatenate([flat[0], flat[1], flat[2]], axis=1)
    return (
        block_out,
        residual_grad,
        query_grad,
        key_grad,
        value_grad,
        wide[TAPS],
        wide[:TAPS],
    )


def solution(mesh):
    rows = P("tm", "heads")
    in_specs = (
        rows, rows, rows, rows, P("heads", None), P("heads"), P(None, "heads"), rows, P(), P(),
    )
    out_specs = (rows, rows, rows, rows, rows, P("heads"), P(None, "heads"))
    return jax.shard_map(body, mesh=mesh, in_specs=in_specs, out_specs=out_specs, check_vma=False)
```

```python
import jax
import jax.numpy as jnp
from jax import lax
from jax.experimental import pallas as pl
from jax.experimental.pallas import tpu as pltpu
from jax.sharding import PartitionSpec as P

D = 1536
DH = 96
GROUP = 256
COLS = 384
RUN = 8
TAPS = 32
SCALE = DH ** (-0.5)
SCALE2 = SCALE * 1.4426950408889634
NEG = -1e30
F32 = jnp.float32
BF16 = jnp.bfloat16
VMEM_LIMIT = 32 * 1024 * 1024

TN = (((0,), (0,)), ((), ()))
NT = (((1,), (1,)), ((), ()))
NN = (((1,), (0,)), ((), ()))


def dot(a, b, dims):
    return lax.dot_general(a, b, dims, preferred_element_type=F32)


def remote(src, dst, send_sem, recv_sem, where):
    return pltpu.make_async_remote_copy(
        src_ref=src,
        dst_ref=dst,
        send_sem=send_sem,
        recv_sem=recv_sem,
        device_id=where,
        device_id_type=pl.DeviceIdType.MESH,
    )


def greet(places):
    barrier = pltpu.get_barrier_semaphore()
    for where in places:
        pl.semaphore_signal(barrier, inc=1, device_id=where, device_id_type=pl.DeviceIdType.MESH)
    pl.semaphore_wait(barrier, len(places))


def quad_of(t, n):
    i = lax.rem(t, 4)
    base = t - i
    return i, base, lax.rem(base + 4, n), lax.rem(base + n - 4, n)


def quad_places(t, n, hd):
    i, base, following, earlier = quad_of(t, n)
    places = [(base + lax.rem(i + s, 4), hd) for s in range(1, 4)]
    places += [(following + s, hd) for s in range(4)] + [(earlier + s, hd) for s in range(4)]
    return places + [(lax.rem(t + RUN, n), hd), (lax.rem(t + n - RUN, n), hd)]


def block_limit(gm_ref, gl_ref, base, w, j):
    source = base + w - 8
    lag = 8 + j - w
    return jnp.where(source >= 0, gm_ref[base + j, lag] * gl_ref[jnp.maximum(source, 0)], 0)


def scores(kt, qt, limit):
    s = dot(kt, qt, TN)
    inside = lax.broadcasted_iota(jnp.int32, s.shape, 0) < limit
    return jnp.where(inside, s * SCALE2, NEG)


def head_peers(hd):
    core = lax.rem(hd, 2)
    partner = hd + 1 - 2 * core
    return partner, lax.rem(hd + 2, 4), lax.rem(partner + 2, 4)


def four_off(t):
    return jnp.where(lax.rem(t, RUN) < 4, t + 4, t - 4)


ORDER = (0, 2, 1, 3)


def quarter(c):
    return pl.ds(c * 64, 64)


def first_leg(t, hd, src, buf, ss, rs):
    far, t4 = lax.rem(hd + 2, 4), four_off(t)
    return [
        remote(src(c), buf.at[c], ss.at[c], rs.at[c], (t4, hd if c < 2 else far)) for c in ORDER
    ]


def second_leg(t, hd, dst, buf, ss, rs):
    far, t4 = lax.rem(hd + 2, 4), four_off(t)
    return [
        remote(buf.at[c], dst(c), ss.at[c], rs.at[c], (t4, far if c < 2 else hd)) for c in ORDER
    ]


def hand_on(first, second):
    for a, b in zip(first, second):
        a.wait_recv()
        b.start()


def over_heads(t, hd, buf, turn, a, b, ss, rs, meanwhile=None):
    lane = lax.broadcasted_iota(jnp.int32, (GROUP, 128), 1)
    both = jnp.where(lane == 0, a, jnp.where(lane == 1, b, 0.0))
    buf[pl.ds(hd, 1)] = both.T[0:8, :][None]
    copies = [
        remote(buf.at[hd], buf.at[hd], ss.at[i], rs.at[i], (t, lax.rem(hd + i + 1, 4)))
        for i in range(3)
    ]
    for c in copies:
        c.start()
    turn[...] = jnp.zeros(turn.shape, F32)
    if meanwhile is not None:
        meanwhile()
    for c in copies:
        c.wait_recv()
    turn[0:8, :] = buf[0] + buf[1] + buf[2] + buf[3]
    back = turn[...].T
    return copies, back[:, 0:1], back[:, 1:2]


def forward(
    q_hbm, k_hbm, v_hbm, w_hbm, res_hbm, cot_hbm, gain_ref, gm_ref, gl_ref,
    win_ref, qb_ref, mine_ref, lse_ref, mixed, standard, hn, cote, inv_ref,
    qkv, kvs, qs, acc, m_s, l_s, att, w_ref, res_ref, cot_ref, hc,
    dsend, drecv, pfar, fsend, frecv, relay, stats, turn,
    load, osend, orecv, qsend, qrecv, nsend, nrecv, xsend, xrecv, asend, arecv,
    ssem, rsem, leg1s, leg1r, leg2s, leg2r,
):
    t, hd = lax.axis_index("tm"), lax.axis_index("heads")
    n = lax.axis_size("tm")
    i, base, following, _ = quad_of(t, n)
    partner, far, diag = head_peers(hd)
    after, before = lax.rem(t + 1, n), lax.rem(t + n - 1, n)
    loads = [
        pltpu.make_async_copy(ref, to, load.at[a])
        for a, (ref, to) in enumerate(
            (
                (k_hbm, qkv.at[0]), (v_hbm, qkv.at[1]), (q_hbm, qkv.at[2]),
                (cot_hbm, cot_ref), (w_hbm, w_ref), (res_hbm, res_ref),
            )
        )
    ]
    for c in loads:
        c.start()
    greet(
        quad_places(t, n, hd)
        + [(t, partner), (t, far), (t, diag), (after, hd), (before, hd), (four_off(t), far)]
    )
    for a in range(2):
        loads[a].wait()
        kvs[:, a] = qkv[a].T.reshape(4, DH, GROUP)

    own_kv, own_q, next_kv = [], [], []
    for s in range(1, 4):
        to = lax.rem(i + s, 4)
        own_kv.append(
            remote(kvs.at[to], win_ref.at[8 + i], osend.at[s], orecv.at[i], (base + to, hd))
        )
        own_q.append(
            remote(qs.at[to], qb_ref.at[i], qsend.at[s], qrecv.at[i], (base + to, hd))
        )
    for s in range(4):
        to = lax.rem(i + s, 4)
        next_kv.append(
            remote(kvs.at[to], win_ref.at[4 + i], nsend.at[s], nrecv.at[i], (following + to, hd))
        )

    next_kv[0].start()
    for c in own_kv:
        c.start()
    loads[2].wait()
    qs[...] = qkv[2].T.reshape(4, DH, GROUP)
    for c in own_q:
        c.start()
    next_kv[1].start()
    win_ref[pl.ds(8 + i, 1)] = kvs[pl.ds(i, 1)]
    qb_ref[pl.ds(i, 1)] = qs[pl.ds(i, 1)]

    def onward(j):
        return remote(
            win_ref.at[8 + j], win_ref.at[j], xsend.at[j], xrecv.at[j], (lax.rem(t + RUN, n), hd)
        )

    @pl.when(i >= 1)
    def _():
        onward(i).start()

    loads[3].wait()
    cot_up = remote(cot_ref.at[pl.ds(GROUP - 16, 16)], hc.at[0], ssem.at[0], rsem.at[0], (after, hd))
    cot_down = remote(cot_ref.at[pl.ds(0, 16)], hc.at[1], ssem.at[1], rsem.at[1], (before, hd))
    cot_up.start()
    cot_down.start()

    m_s[...] = jnp.full(m_s.shape, NEG, F32)
    l_s[...] = jnp.zeros(l_s.shape, F32)
    acc[...] = jnp.zeros(acc.shape, F32)

    for s in range(1, 4):
        j = lax.rem(i + 4 - s, 4)
        remote(kvs.at[0], win_ref.at[8 + j], osend.at[s], orecv.at[j], (following, hd)).wait_recv()

        @pl.when(j >= 1)
        def _(j=j):
            onward(j).start()

    for s in range(1, 4):
        j = lax.rem(i + 4 - s, 4)
        remote(qs.at[0], qb_ref.at[j], qsend.at[s], qrecv.at[j], (following, hd)).wait_recv()

    def attend(group_for):
        for j in range(4):
            w = group_for(j)
            s = scores(win_ref[w, 0], qb_ref[j], block_limit(gm_ref, gl_ref, base, w, j))
            m_old = m_s[j]
            m_new = jnp.maximum(m_old, jnp.max(s, axis=0, keepdims=True))
            alpha = jnp.exp2(m_old - m_new)
            p = jnp.exp2(s - m_new)
            m_s[j] = m_new
            l_s[j] = l_s[j] * alpha + jnp.sum(p, axis=0, keepdims=True)
            acc[j] = acc[j] * alpha + dot(win_ref[w, 1], p.astype(BF16), NN)

    def own_step(m, carry):
        @pl.when(m >= 1)
        def _():
            remote(win_ref.at[m], win_ref.at[m], xsend.at[m], xrecv.at[m], (following, hd)).wait_recv()

        attend(lambda j: jnp.where(j >= m, 8 + m, m))
        return carry

    lax.fori_loop(0, 2, own_step, 0)
    next_kv[0].wait_send()
    next_kv[2].start()
    lax.fori_loop(2, 4, own_step, 0)
    next_kv[1].wait_send()
    next_kv[3].start()

    def before_step(s, carry):
        j = lax.rem(i + 4 - s, 4)
        remote(kvs.at[0], win_ref.at[4 + j], nsend.at[0], nrecv.at[j], (following, hd)).wait_recv()
        attend(lambda _: 4 + j)
        return carry

    lax.fori_loop(0, 4, before_step, 0)

    def give(s):
        j = lax.rem(i + s, 4)
        return remote(mine_ref.at[j], att.at[i], asend.at[s], arecv.at[i], (base + j, hd))

    for s in (1, 2, 3, 0):
        j = lax.rem(i + s, 4)
        mine_ref[j] = (acc[j] / l_s[j]).astype(BF16)
        if s:
            give(s).start()
    att[pl.ds(i, 1)] = mine_ref[pl.ds(i, 1)]
    lse_ref[...] = m_s[...] + jnp.log2(l_s[...])
    cot_up.wait_recv()
    cot_down.wait_recv()
    cote[16 : 16 + GROUP, :] = cot_ref[...].astype(F32)
    cote[0:16, :] = jnp.where(t > 0, hc[0].astype(F32), 0.0)
    cote[16 + GROUP :, :] = jnp.where(t < n - 1, hc[1].astype(F32), 0.0)
    loads[4].wait()
    loads[5].wait()
    for s in range(1, 4):
        j = lax.rem(i + 4 - s, 4)
        remote(mine_ref.at[0], att.at[j], asend.at[s], arecv.at[j], (following, hd)).wait_recv()

    def project(j):
        cols = pl.ds(pl.multiple_of(j * COLS, 128), COLS)
        return dot(att[...].reshape(COLS, GROUP), w_ref[:, cols], TN)

    dsend[0] = project(diag)
    give_far = remote(dsend.at[0], drecv.at[0], ssem.at[2], rsem.at[2], (t, partner))
    give_far.start()
    pfar[...] = project(far)
    give_far.wait_recv()
    fsend[...] = (pfar[...] + drecv[0]).astype(BF16)
    cross1 = first_leg(t, hd, lambda c: fsend.at[quarter(c)], relay, leg1s, leg1r)
    cross2 = second_leg(t, hd, lambda c: frecv.at[quarter(c)], relay, leg2s, leg2r)
    for c in cross1:
        c.start()
    dsend[1] = project(partner)
    give_near = remote(dsend.at[1], drecv.at[1], ssem.at[3], rsem.at[3], (t, partner))
    give_near.start()
    mixed[...] = project(hd) + res_ref[...].astype(F32)
    give_near.wait_recv()
    mixed[...] = mixed[...] + drecv[1]
    hand_on(cross1, cross2)
    for c, part in zip(ORDER, cross2):
        part.wait_recv()
        rows = slice(c * 64, c * 64 + 64)
        mixed[rows, :] = mixed[rows, :] + frecv[rows, :].astype(F32)

    mx = mixed[...]
    stat_copies, row_sum, row_square = over_heads(
        t, hd, stats, turn,
        jnp.sum(mx, axis=1, keepdims=True), jnp.sum(mx * mx, axis=1, keepdims=True),
        ssem.at[pl.ds(4, 3)], rsem.at[pl.ds(4, 3)],
    )
    centre = row_sum / D
    inverse = lax.rsqrt(row_square / D - centre * centre + 1e-05)
    inv_ref[...] = jnp.broadcast_to(inverse, inv_ref.shape)
    standard[...] = (mixed[...] - centre) * inverse
    hn[1:9, :, :] = (standard[...] * gain_ref[...]).astype(BF16).reshape(8, 32, COLS)
    norm_up = remote(hn.at[8], hn.at[0], ssem.at[7], rsem.at[7], (after, hd))
    norm_down = remote(hn.at[1], hn.at[9], ssem.at[8], rsem.at[8], (before, hd))
    norm_up.start()
    norm_down.start()
    for c in own_kv + own_q + next_kv[2:] + [cot_up, cot_down, give_far, give_near]:
        c.wait_send()
    for c in cross1 + cross2 + stat_copies:
        c.wait_send()
    for s in range(1, 4):
        onward(s).wait_send()
        give(s).wait_send()
    norm_up.wait()
    norm_down.wait()

    @pl.when(t == 0)
    def _():
        hn[0] = jnp.zeros((32, COLS), BF16)

    @pl.when(t == n - 1)
    def _():
        hn[9] = jnp.zeros((32, COLS), BF16)


def convolution(
    hn, cote, mixed, standard, ck_ref,
    out_ref, ng, kpart,
    pn, cg, silu, kacc,
):
    pn[...] = hn[...].astype(F32).reshape(GROUP + 64, COLS)
    kacc[...] = jnp.zeros(kacc.shape, F32)
    for cb in range(3):
        cols = slice(cb * 128, cb * 128 + 128)

        def convolve(i, carry, cols=cols):
            base = pl.multiple_of(i * 96, 32)
            rows = pn[pl.ds(base, 128), cols]
            total = jnp.zeros((96, 128), F32)
            for r in range(8):
                moved = rows[r : r + 120]
                for a in range(4):
                    m = 8 * a + r
                    total = total + ck_ref[m : m + 1, cols] * moved[8 * a : 8 * a + 96]
            gate = jax.nn.sigmoid(total)
            silu[pl.ds(base, 96), cols] = total * gate
            cg[pl.ds(base, 96), cols] = (
                cote[pl.ds(base, 96), cols] * gate * (1.0 + total * (1.0 - gate))
            )
            return carry

        lax.fori_loop(0, 3, convolve, 0)

    for cb in range(3):
        cols = slice(cb * 128, cb * 128 + 128)

        def backward(i, carry, cols=cols):
            base = pl.multiple_of(i * 64, 64)
            rows = cg[pl.ds(base, 96), cols]
            total = jnp.zeros((64, 128), F32)
            for r in range(8):
                moved = rows if r == 0 else rows[r : r + 88]
                for a in range(5 if r == 0 else 4):
                    u = 8 * a + r
                    if u == 0:
                        continue
                    m = 32 - u
                    total = total + ck_ref[m : m + 1, cols] * moved[8 * a : 8 * a + 64]
            ng[pl.ds(base, 64), cols] = total
            prod = total * standard[pl.ds(base, 64), cols]
            kacc[TAPS, :, cols] = kacc[TAPS, :, cols] + jnp.sum(prod.reshape(8, 8, 128), axis=0)
            grad = rows[16:80]
            normed = pn[pl.ds(base + 16, 96), cols]
            for r in range(8):
                moved = normed[r : r + 88]
                for a in range(4):
                    m = 8 * a + r
                    prod = grad * moved[8 * a : 8 * a + 64]
                    kacc[m, :, cols] = kacc[m, :, cols] + jnp.sum(prod.reshape(8, 8, 128), axis=0)
            return carry

        lax.fori_loop(0, 4, backward, 0)

    out_ref[...] = (mixed[...] + silu[16 : 16 + GROUP, :]).astype(BF16)

    kpart[...] = jnp.zeros(kpart.shape, F32)
    summed = jnp.sum(kacc[...], axis=1)
    for cb in range(3):
        kpart[cb * 40 : cb * 40 + 40, :] = summed[:, cb * 128 : cb * 128 + 128]

def backward(
    ng, kpart, cote, standard, inv_ref, gain_ref, w_hbm,
    qb_ref, win_ref, mine_ref, lse_ref, gm_ref, gl_ref,
    rg_ref, kg_ref, dq_ref, dk_ref, dv_ref,
    w_ref, stats, turn, relay, rgall, racc, rz, rx, ry, dgrad,
    gq, delta, dq, dqs, part, ownp, out, racross, rown, rnext, rq,
    gsend, grecv, nsend, nrecv, xsend, xrecv, osend, orecv, qsend, qrecv,
    ssem, rsem, leg1s, leg1r, leg2s, leg2r, psend, precv,
    zs, zr, gs, gr, xs, xr, ys, yr, load,
):
    t, hd = lax.axis_index("tm"), lax.axis_index("heads")
    n = lax.axis_size("tm")
    i, base, following, earlier = quad_of(t, n)
    partner, far, diag = head_peers(hd)
    z, x, y = lax.rem(t, RUN), lax.rem(t // RUN, 4), t // (4 * RUN)
    fetch = pltpu.make_async_copy(w_hbm, w_ref, load)
    fetch.start()

    def along_z(a):
        return ((t - z + a), hd)

    def along_x(a):
        return ((t + (a - x) * RUN), hd)

    def along_y(a):
        return ((t + (a - y) * 4 * RUN), hd)

    places = quad_places(t, n, hd) + [(t, partner), (t, far), (t, diag), (four_off(t), far)]
    places += [along_z(lax.rem(z + d, RUN)) for d in range(1, RUN)]
    places += [along_x(lax.rem(x + d, 4)) for d in range(1, 4)]
    places += [along_y(lax.rem(y + d, 4)) for d in range(1, 4)]
    greet(places)

    def exchange(count, here, place, source, buf, ss, rs):
        for a in range(count):
            @pl.when(here != a)
            def _(a=a):
                remote(source(a), buf.at[here], ss.at[a], rs.at[here], place(a)).start()

    def finish(count, here, place, source, buf, ss, rs):
        for a in range(count):
            @pl.when(here != a)
            def _(a=a):
                remote(source(a), buf.at[a], ss.at[a], rs.at[a], place(a)).wait()

    z_parts = (RUN, z, along_z, lambda a: kpart.at[pl.ds(16 * a, 16)], rz, zs, zr)
    x_parts = (4, x, along_x, lambda a: rx.at[x], rx, xs, xr)
    y_parts = (4, y, along_y, lambda a: ry.at[y], ry, ys, yr)
    g_parts = (RUN, z, along_z, lambda a: kg_ref.at[z], kg_ref, gs, gr)

    def start_sums():
        exchange(*z_parts)
        rz[pl.ds(z, 1)] = kpart[pl.ds(pl.multiple_of(z * 16, 16), 16), :][None]

    sg = ng[...] * gain_ref[...]
    stat_copies, grad_mean, grad_proj = over_heads(
        t, hd, stats, turn,
        jnp.sum(sg, axis=1, keepdims=True), jnp.sum(sg * standard[...], axis=1, keepdims=True),
        ssem.at[pl.ds(0, 3)], rsem.at[pl.ds(0, 3)], start_sums,
    )
    grad = cote[16 : 16 + GROUP, :] + inv_ref[:, 0:1] * (
        ng[...] * gain_ref[...] - grad_mean / D - standard[...] * (grad_proj / D)
    )
    rgb = grad.astype(BF16)
    rgall[pl.ds(hd, 1)] = rgb[None]
    share1 = first_leg(t, hd, lambda c: rgall.at[hd, quarter(c)], relay, leg1s, leg1r)
    share2 = second_leg(
        t, hd, lambda c: rgall.at[hd if c < 2 else far, quarter(c)], relay, leg2s, leg2r
    )
    share_near = remote(rgall.at[hd], rgall.at[hd], ssem.at[3], rsem.at[3], (t, partner))
    for c in share1:
        c.start()
    share_near.start()
    rg_ref[...] = rgb

    def back(j):
        cols = pl.ds(pl.multiple_of(j * COLS, 128), COLS)
        rows = rgall[pl.ds(j, 1)].reshape(GROUP, COLS)
        return dot(w_ref[:, cols], rows, NT)

    fetch.wait()
    racc[...] = back(hd)
    hand_on(share1, share2)
    finish(*z_parts)
    rx[pl.ds(x, 1)] = sum((rz[a] for a in range(1, RUN)), rz[0])[None]
    exchange(*x_parts)
    remote(rgall.at[partner], rgall.at[partner], ssem.at[3], rsem.at[3], (t, partner)).wait_recv()
    racc[...] = racc[...] + back(partner)

    def pass_on(c, which):
        rows = rgall.at[which, quarter(c)]
        return remote(rows, rows, psend.at[c], precv.at[c], (t, partner))

    for c, piece in zip(ORDER, share2):
        rows = rgall.at[far, quarter(c)]
        remote(rows, rows, leg2s.at[c], leg2r.at[c], (t, partner)).wait_recv()
        pass_on(c, far).start()
    racc[...] = racc[...] + back(far)
    for c in ORDER:
        pass_on(c, diag).wait_recv()
    dgrad[...] = (racc[...] + back(diag)).astype(BF16).reshape(4, DH, GROUP)

    spread = []
    for s in range(1, 4):
        to = lax.rem(i + s, 4)
        spread.append(remote(dgrad.at[to], gq.at[i], gsend.at[s], grecv.at[i], (base + to, hd)))
    for c in spread:
        c.start()
    gq[pl.ds(i, 1)] = dgrad[pl.ds(i, 1)]
    dq[...] = jnp.zeros(dq.shape, F32)
    finish(*x_parts)
    ry[pl.ds(y, 1)] = (rx[0] + rx[1] + rx[2] + rx[3])[None]
    exchange(*y_parts)
    for s in range(1, 4):
        j = lax.rem(i + 4 - s, 4)
        remote(dgrad.at[0], gq.at[j], gsend.at[s], grecv.at[j], (following, hd)).wait_recv()
    delta[...] = jnp.sum(gq[...].astype(F32) * mine_ref[...].astype(F32), axis=1, keepdims=True)

    def terms(group_for, place_for):
        part[...] = jnp.zeros(part.shape, F32)
        for j in range(4):
            w, place = group_for(j), place_for(j)
            kt, qt, gt = win_ref[w, 0], qb_ref[j], gq[j]
            s = scores(kt, qt, block_limit(gm_ref, gl_ref, base, w, j))
            p = jnp.exp2(s - lse_ref[j])
            ds = (p * (dot(win_ref[w, 1], gt, TN) - delta[j])).astype(BF16)
            dq[j] = dq[j] + dot(kt, ds, NN)
            part[place, 0] = part[place, 0] + dot(qt, ds, NT) * SCALE
            part[place, 1] = part[place, 1] + dot(gt, p.astype(BF16), NT)

    def to_before(j):
        return remote(out.at[4 + j], rnext.at[i], nsend.at[j], nrecv.at[i], (earlier + j, hd))

    def before_step(s, carry):
        j = lax.rem(i + s, 4)
        terms(lambda _: 4 + j, lambda _: 0)
        out[4 + j] = part[0].astype(BF16)
        to_before(j).start()
        return carry

    lax.fori_loop(0, 4, before_step, 0)
    finish(*y_parts)
    kg_ref[pl.ds(z, 1)] = (ry[0] + ry[1] + ry[2] + ry[3])[None]
    exchange(*g_parts)

    def to_across(w):
        return remote(
            out.at[w], racross.at[w], xsend.at[w], xrecv.at[w], (lax.rem(t + n - RUN, n), hd)
        )

    def own_step(s, carry):
        m = 3 - s
        terms(lambda j: jnp.where(j >= m, 8 + m, m), lambda j: jnp.where(j >= m, 0, 1))
        ownp[m] = part[0]

        @pl.when(m >= 1)
        def _():
            out[m] = part[1].astype(BF16)
            to_across(m).start()

        return carry

    lax.fori_loop(0, 4, own_step, 0)

    def give(s):
        j = lax.rem(i + s, 4)
        return remote(dqs.at[j], rq.at[i], qsend.at[s], qrecv.at[i], (base + j, hd))

    dqs[...] = (dq[...] * SCALE).astype(BF16)
    for s in range(1, 4):
        give(s).start()
    rq[pl.ds(i, 1)] = dqs[pl.ds(i, 1)]

    def to_own(j):
        return remote(out.at[8 + j], rown.at[i], osend.at[j], orecv.at[i], (base + j, hd))

    for j in (0, 3, 2, 1):
        if j:
            to_across(j).wait_recv()
            out[8 + j] = (ownp[j] + racross[j].astype(F32)).astype(BF16)
        else:
            out[8 + j] = ownp[j].astype(BF16)

        @pl.when(j != i)
        def _(j=j):
            to_own(j).start()

    rown[pl.ds(i, 1)] = out[pl.ds(8 + i, 1)]
    for s in range(1, 4):
        j = lax.rem(i + 4 - s, 4)
        remote(dqs.at[0], rq.at[j], qsend.at[s], qrecv.at[j], (following, hd)).wait_recv()
    dq_ref[...] = rq[...].reshape(COLS, GROUP).T
    finish(*g_parts)
    for c in share1 + share2 + spread + stat_copies + [share_near]:
        c.wait_send()
    for c in ORDER:
        pass_on(c, far).wait_send()
    for s in range(1, 4):
        give(s).wait_send()
        to_across(s).wait_send()
    for s in range(1, 4):
        j = lax.rem(i + 4 - s, 4)
        remote(out.at[8], rown.at[j], osend.at[0], orecv.at[j], (following, hd)).wait_recv()
    for j in range(4):
        remote(out.at[4], rnext.at[j], nsend.at[0], nrecv.at[j], (following, hd)).wait_recv()
    both = (rown[...].astype(F32) + rnext[...].astype(F32)).astype(BF16)
    dk_ref[...] = both[:, 0].reshape(COLS, GROUP).T
    dv_ref[...] = both[:, 1].reshape(COLS, GROUP).T
    for j in range(4):
        to_before(j).wait_send()

        @pl.when(j != i)
        def _(j=j):
            to_own(j).wait_send()


VM = pl.BlockSpec(memory_space=pltpu.VMEM)
SM = pl.BlockSpec(memory_space=pltpu.SMEM)
HB = pl.BlockSpec(memory_space=pl.ANY)
DMA = pltpu.SemaphoreType.DMA


def shape(dims, kind=BF16):
    return jax.ShapeDtypeStruct(dims, kind)


def params(which):
    return pltpu.CompilerParams(
        collective_id=which, has_side_effects=True, vmem_limit_bytes=VMEM_LIMIT
    )


def body(
    queries, key_input, value_input, residual, out_weight, norm_gain, conv_kernel, cotangent,
    group_mask, group_len,
):
    turned = (4, DH, GROUP)
    block = (GROUP, COLS)
    row = (4, 1, GROUP)
    window = (12, 2, DH, GROUP)
    pieces = (4, 2, DH, GROUP)
    legs = (4, 64, COLS)
    halo = (10, 32, COLS)
    longer = (GROUP + 32, COLS)
    gain = norm_gain.reshape(1, COLS)
    win, qb, mine, lse, mixed, standard, hn, cote, inverse = pl.pallas_call(
        forward,
        out_shape=[
            shape(window), shape(turned), shape(turned), shape(row, F32), shape(block, F32),
            shape(block, F32), shape(halo), shape(longer, F32), shape((GROUP, 128), F32),
        ],
        in_specs=[HB] * 6 + [VM, SM, SM],
        out_specs=[VM] * 9,
        scratch_shapes=[
            pltpu.VMEM((3,) + block, BF16),
            pltpu.VMEM(pieces, BF16),
            pltpu.VMEM(turned, BF16),
            pltpu.VMEM(turned, F32),
            pltpu.VMEM(row, F32),
            pltpu.VMEM(row, F32),
            pltpu.VMEM(turned, BF16),
            pltpu.VMEM((COLS, D), BF16),
            pltpu.VMEM(block, BF16),
            pltpu.VMEM(block, BF16),
            pltpu.VMEM((2, 16, COLS), BF16),
            pltpu.VMEM((2,) + block, F32),
            pltpu.VMEM((2,) + block, F32),
            pltpu.VMEM(block, F32),
            pltpu.VMEM(block, BF16),
            pltpu.VMEM(block, BF16),
            pltpu.VMEM(legs, BF16),
            pltpu.VMEM((4, 8, GROUP), F32),
            pltpu.VMEM((128, GROUP), F32),
            DMA((6,)),
        ]
        + [DMA((4,))] * 10
        + [DMA((9,))] * 2
        + [DMA((4,))] * 4,
        compiler_params=params(0),
        name="forward",
    )(
        queries, key_input, value_input, out_weight, residual, cotangent, gain,
        group_mask, group_len,
    )

    block_out, ng, kpart = pl.pallas_call(
        convolution,
        out_shape=[shape(block), shape(block, F32), shape((128, 128), F32)],
        in_specs=[VM] * 5,
        out_specs=[VM] * 3,
        scratch_shapes=[
            pltpu.VMEM((GROUP + 64, COLS), F32),
            pltpu.VMEM(longer, F32),
            pltpu.VMEM(longer, F32),
            pltpu.VMEM((40, 8, COLS), F32),
        ],
        compiler_params=pltpu.CompilerParams(vmem_limit_bytes=VMEM_LIMIT),
        name="convolution",
    )(hn, cote, mixed, standard, conv_kernel)

    residual_grad, kg, query_grad, key_grad, value_grad = pl.pallas_call(
        backward,
        out_shape=[shape(block), shape((8, 16, 128), F32)] + [shape(block)] * 3,
        in_specs=[VM] * 6 + [HB] + [VM] * 4 + [SM, SM],
        out_specs=[VM] * 5,
        scratch_shapes=[
            pltpu.VMEM((COLS, D), BF16),
            pltpu.VMEM((4, 8, GROUP), F32),
            pltpu.VMEM((128, GROUP), F32),
            pltpu.VMEM(legs, BF16),
            pltpu.VMEM((4,) + block, BF16),
            pltpu.VMEM((COLS, GROUP), F32),
            pltpu.VMEM((8, 16, 128), F32),
            pltpu.VMEM((4, 16, 128), F32),
            pltpu.VMEM((4, 16, 128), F32),
            pltpu.VMEM(turned, BF16),
            pltpu.VMEM(turned, BF16),
            pltpu.VMEM(row, F32),
            pltpu.VMEM(turned, F32),
            pltpu.VMEM(turned, BF16),
            pltpu.VMEM((2, 2, DH, GROUP), F32),
            pltpu.VMEM(pieces, F32),
            pltpu.VMEM(window, BF16),
            pltpu.VMEM(pieces, BF16),
            pltpu.VMEM(pieces, BF16),
            pltpu.VMEM(pieces, BF16),
            pltpu.VMEM(turned, BF16),
        ]
        + [DMA((4,))] * 18
        + [DMA((8,))] * 4
        + [DMA((4,))] * 4
        + [DMA],
        compiler_params=params(1),
        name="backward",
    )(
        ng, kpart, cote, standard, inverse, gain, out_weight, qb, win, mine, lse,
        group_mask, group_len,
    )

    flat = kg.reshape(128, 128)[:120].reshape(3, 40, 128)
    wide = jnp.concatenate([flat[0], flat[1], flat[2]], axis=1)
    return (
        block_out,
        residual_grad,
        query_grad,
        key_grad,
        value_grad,
        wide[TAPS],
        wide[:TAPS],
    )


def solution(mesh):
    rows = P("tm", "heads")
    in_specs = (
        rows, rows, rows, rows, P("heads", None), P("heads"), P(None, "heads"), rows, P(), P(),
    )
    out_specs = (rows, rows, rows, rows, rows, P("heads"), P(None, "heads"))
    return jax.shard_map(body, mesh=mesh, in_specs=in_specs, out_specs=out_specs, check_vma=False)
```

```python
import jax
import jax.numpy as jnp
from jax import lax
from jax.experimental import pallas as pl
from jax.experimental.pallas import tpu as pltpu
from jax.sharding import PartitionSpec as P

D = 1536
DH = 96
GROUP = 256
COLS = 384
RUN = 8
TAPS = 32
SCALE = DH ** (-0.5)
SCALE2 = SCALE * 1.4426950408889634
NEG = -1e30
F32 = jnp.float32
BF16 = jnp.bfloat16
VMEM_LIMIT = 58 * 1024 * 1024

NT = (((1,), (1,)), ((), ()))
NN = (((1,), (0,)), ((), ()))


def dot(a, b, dims):
    return lax.dot_general(a, b, dims, preferred_element_type=F32)


def remote(src, dst, send_sem, recv_sem, where):
    return pltpu.make_async_remote_copy(
        src_ref=src,
        dst_ref=dst,
        send_sem=send_sem,
        recv_sem=recv_sem,
        device_id=where,
        device_id_type=pl.DeviceIdType.MESH,
    )


def greet(places):
    barrier = pltpu.get_barrier_semaphore()
    for where in places:
        pl.semaphore_signal(barrier, inc=1, device_id=where, device_id_type=pl.DeviceIdType.MESH)
    return lambda: pl.semaphore_wait(barrier, len(places))


def quad_of(t, n):
    i = lax.rem(t, 4)
    base = t - i
    return i, base, lax.rem(base + 4, n), lax.rem(base + n - 4, n)


def quad_places(t, n, hd):
    i, base, following, earlier = quad_of(t, n)
    places = [(base + lax.rem(i + s, 4), hd) for s in range(1, 4)]
    places += [(following + s, hd) for s in range(4)] + [(earlier + s, hd) for s in range(4)]
    return places + [(lax.rem(t + RUN, n), hd), (lax.rem(t + n - RUN, n), hd)]


def block_limit(gm_ref, gl_ref, base, w, j):
    source = base + w - 8
    lag = 8 + j - w
    return jnp.where(source >= 0, gm_ref[lag, base + j] * gl_ref[jnp.maximum(source, 0)], 0)


def scores(k, qt, limit):
    s = dot(k, qt, NN)
    inside = lax.broadcasted_iota(jnp.int32, s.shape, 0) < limit
    return jnp.where(inside, s * SCALE2, NEG)


def head_peers(hd):
    partner = hd + 1 - 2 * lax.rem(hd, 2)
    return partner, lax.rem(hd + 2, 4), lax.rem(partner + 2, 4)


def quarter(c):
    return pl.ds(c * 64, 64)


def conformer(
    q_hbm, k_hbm, v_hbm, w_hbm, res_hbm, cot_hbm, gain_ref, ck_ref, gm_ref, gl_ref,
    blk_ref, rg_ref, kg_ref, rq, rown, rnext,
    qkv, kvs, qs, win, qb, knat, vnat, mine, acc, m_s, l_s, lse, att, attn, w2, res_ref, cot_ref, hc,
    fsend, frecv, mixed, standard, inv_ref, stats, stats2, nst, hm, turn,
    pn, cote, cg, silu, ng, kacc, kpart,
    rgall, racc, rz, rx, ry, dgrad, gq, delta, dq, dqs, part, ownp, out, racross,
    load, fosend, forecv, fqsend, fqrecv, fnsend, fnrecv, fxsend, fxrecv, asend, arecv,
    gsend, grecv, nsend, nrecv, xsend, xrecv, osend, orecv, qsend, qrecv,
    csend, crecv, ssend, srecv, psend, precv, tsend, trecv, usend, urecv,
    zs, zr, gs, gr, hsend, hrecv, xs, xr, ys, yr, ssem, rsem,
):
    t, hd = lax.axis_index("tm"), lax.axis_index("heads")
    n = lax.axis_size("tm")
    i, base, following, earlier = quad_of(t, n)
    partner, far, diag = head_peers(hd)
    after, before = lax.rem(t + 1, n), lax.rem(t + n - 1, n)
    z, x, y = lax.rem(t, RUN), lax.rem(t // RUN, 4), t // (4 * RUN)

    def along_z(a):
        return ((t - z + a), hd)

    def along_x(a):
        return ((t + (a - x) * RUN), hd)

    def along_y(a):
        return ((t + (a - y) * 4 * RUN), hd)

    places = quad_places(t, n, hd) + [(t, partner), (t, far), (t, diag)]
    places += [(to, h) for to in (after, before) for h in range(4)]
    places += [along_z(lax.rem(z + d, RUN)) for d in range(1, RUN)]
    places += [along_x(lax.rem(x + d, 4)) for d in range(1, 4)]
    places += [along_y(lax.rem(y + d, 4)) for d in range(1, 4)]
    entered = greet(places)
    gain = gain_ref[...].reshape(1, COLS)

    loads = [
        pltpu.make_async_copy(ref, to, load.at[a])
        for a, (ref, to) in enumerate(
            (
                (k_hbm, qkv.at[0]), (v_hbm, qkv.at[1]), (q_hbm, qkv.at[2]),
                (cot_hbm, cot_ref), (w_hbm, w2.at[0]), (res_hbm, res_ref),
            )
        )
    ]
    for c in loads:
        c.start()
    for a in range(2):
        loads[a].wait()
        kvs[:, a] = qkv[a].T.reshape(4, DH, GROUP)

    own_kv, own_q, next_kv = [], [], []
    for s in range(1, 4):
        to = lax.rem(i + s, 4)
        own_kv.append(
            remote(kvs.at[to], win.at[8 + i], fosend.at[s], forecv.at[i], (base + to, hd))
        )
        own_q.append(remote(qs.at[to], qb.at[i], fqsend.at[s], fqrecv.at[i], (base + to, hd)))
    for s in range(4):
        to = lax.rem(i + s, 4)
        next_kv.append(
            remote(kvs.at[to], win.at[4 + i], fnsend.at[s], fnrecv.at[i], (following + to, hd))
        )

    entered()
    next_kv[0].start()
    for c in own_kv:
        c.start()
    loads[2].wait()
    qs[...] = qkv[2].T.reshape(4, DH, GROUP)
    for c in own_q:
        c.start()
    next_kv[1].start()
    win[pl.ds(8 + i, 1)] = kvs[pl.ds(i, 1)]
    qb[pl.ds(i, 1)] = qs[pl.ds(i, 1)]

    def onward(j):
        return remote(
            win.at[8 + j], win.at[j], fxsend.at[j], fxrecv.at[j], (lax.rem(t + RUN, n), hd)
        )

    @pl.when(i >= 1)
    def _():
        onward(i).start()

    loads[3].wait()
    loads[4].wait()
    cot_up = remote(cot_ref.at[pl.ds(GROUP - 16, 16)], hc.at[0], ssem.at[0], rsem.at[0], (after, hd))
    cot_down = remote(cot_ref.at[pl.ds(0, 16)], hc.at[1], ssem.at[1], rsem.at[1], (before, hd))
    weight = remote(w2.at[0], w2.at[1], ssem.at[2], rsem.at[2], (t, partner))
    cot_up.start()
    cot_down.start()
    weight.start()

    m_s[...] = jnp.full(m_s.shape, NEG, F32)
    l_s[...] = jnp.zeros(l_s.shape, F32)
    acc[...] = jnp.zeros(acc.shape, F32)

    for s in range(1, 4):
        j = lax.rem(i + 4 - s, 4)
        remote(kvs.at[0], win.at[8 + j], fosend.at[s], forecv.at[j], (following, hd)).wait_recv()

        @pl.when(j >= 1)
        def _(j=j):
            onward(j).start()

    for s in range(1, 4):
        j = lax.rem(i + 4 - s, 4)
        remote(qs.at[0], qb.at[j], fqsend.at[s], fqrecv.at[j], (following, hd)).wait_recv()

    def turn_keys(w):
        knat[w] = win[w, 0].T

    def attend(group_for):
        for j in range(4):
            w = group_for(j)
            s = scores(knat[w], qb[j], block_limit(gm_ref, gl_ref, base, w, j))
            m_old = m_s[j]
            m_new = jnp.maximum(m_old, jnp.max(s, axis=0, keepdims=True))
            alpha = jnp.exp2(m_old - m_new)
            p = jnp.exp2(s - m_new)
            m_s[j] = m_new
            l_s[j] = l_s[j] * alpha + jnp.sum(p, axis=0, keepdims=True)
            acc[j] = acc[j] * alpha + dot(win[w, 1], p.astype(BF16), NN)

    def own_step_in(m, carry):
        @pl.when(m >= 1)
        def _():
            remote(win.at[m], win.at[m], fxsend.at[m], fxrecv.at[m], (following, hd)).wait_recv()
            turn_keys(m)

        turn_keys(8 + m)
        attend(lambda j: jnp.where(j >= m, 8 + m, m))
        return carry

    lax.fori_loop(0, 2, own_step_in, 0)
    next_kv[0].wait_send()
    next_kv[2].start()
    lax.fori_loop(2, 4, own_step_in, 0)
    next_kv[1].wait_send()
    next_kv[3].start()

    def before_step_in(s, carry):
        j = lax.rem(i + 4 - s, 4)
        remote(kvs.at[0], win.at[4 + j], fnsend.at[0], fnrecv.at[j], (following, hd)).wait_recv()
        turn_keys(4 + j)
        attend(lambda _: 4 + j)
        return carry

    lax.fori_loop(0, 4, before_step_in, 0)

    def give_att(s):
        j = lax.rem(i + s, 4)
        return remote(mine.at[j], att.at[i], asend.at[s], arecv.at[i], (base + j, hd))

    for s in (1, 2, 3, 0):
        j = lax.rem(i + s, 4)
        mine[j] = (acc[j] / l_s[j]).astype(BF16)
        if s:
            give_att(s).start()
    att[pl.ds(i, 1)] = mine[pl.ds(i, 1)]
    lse[...] = m_s[...] + jnp.log2(l_s[...])
    cot_up.wait_recv()
    cot_down.wait_recv()
    cote[16 : 16 + GROUP, :] = cot_ref[...].astype(F32)
    cote[0:16, :] = jnp.where(t > 0, hc[0].astype(F32), 0.0)
    cote[16 + GROUP :, :] = jnp.where(t < n - 1, hc[1].astype(F32), 0.0)
    loads[5].wait()
    weight.wait_recv()
    for s in range(1, 4):
        j = lax.rem(i + 4 - s, 4)
        remote(mine.at[0], att.at[j], asend.at[s], arecv.at[j], (following, hd)).wait_recv()

    attn[0] = att[...].reshape(COLS, GROUP).T
    swap = remote(attn.at[0], attn.at[1], ssem.at[3], rsem.at[3], (t, partner))
    swap.start()

    def weight_cols(core, j):
        return w2[core, :, pl.ds(pl.multiple_of(j * COLS, 128), COLS)]

    mixed[...] = dot(attn[0], weight_cols(0, far), NN)
    swap.wait_recv()
    cross = []
    for c in range(4):
        rows = slice(c * 64, c * 64 + 64)
        fsend[rows, :] = (mixed[rows, :] + dot(attn[1, rows, :], weight_cols(1, far), NN)).astype(BF16)
        cross.append(
            remote(fsend.at[quarter(c)], frecv.at[quarter(c)], csend.at[c], crecv.at[c], (t, far))
        )
        cross[c].start()
    mixed[...] = (
        dot(attn[0], weight_cols(0, hd), NN)
        + dot(attn[1], weight_cols(1, hd), NN)
        + res_ref[...].astype(F32)
    )

    def turn_values(w, carry):
        vnat[w] = win[w, 1].T
        return carry

    lax.fori_loop(1, 12, turn_values, 0)
    kacc[...] = jnp.zeros(kacc.shape, F32)
    turn[...] = jnp.zeros(turn.shape, F32)
    for c in range(4):
        cross[c].wait_recv()
        rows = slice(c * 64, c * 64 + 64)
        mixed[rows, :] = mixed[rows, :] + frecv[rows, :].astype(F32)

    halos = [
        remote(mixed.at[pl.ds(GROUP - 32, 32)], hm.at[0], ssem.at[4], rsem.at[4], (after, hd)),
        remote(mixed.at[pl.ds(0, 32)], hm.at[1], ssem.at[5], rsem.at[5], (before, hd)),
    ]
    for c in halos:
        c.start()

    def row_pair(a, b):
        lane = lax.broadcasted_iota(jnp.int32, (GROUP, 128), 1)
        return jnp.where(lane == 0, a, jnp.where(lane == 1, b, 0.0)).T[0:8, :][None]

    def to_heads(buf, ss, rs):
        return [
            remote(buf.at[hd], buf.at[hd], ss.at[a], rs.at[a], (t, lax.rem(hd + a + 1, 4)))
            for a in (1, 2, 0)
        ]

    def turned_back(total, width):
        turn[0:8, 0:width] = total
        return turn[:, 0:width].T

    mx = mixed[...]
    stats[pl.ds(hd, 1)] = row_pair(
        jnp.sum(mx, axis=1, keepdims=True), jnp.sum(mx * mx, axis=1, keepdims=True)
    )
    stat_copies = to_heads(stats, tsend, trecv)
    for c in stat_copies:
        c.start()
    for side, to in ((0, after), (1, before)):
        ends = stats.at[hd, :, pl.ds(128 - 128 * side, 128)]
        for h in range(4):
            c = remote(ends, nst.at[side, hd], hsend.at[side * 4 + h], hrecv.at[side * 4 + hd], (to, h))
            c.start()
            stat_copies.append(c)
    for c in stat_copies[:3]:
        c.wait_recv()

    def norm_of(back):
        centre = back[:, 0:1] / D
        return centre, lax.rsqrt(back[:, 1:2] / D - centre * centre + 1e-05)

    centre, inverse = norm_of(turned_back(stats[0] + stats[1] + stats[2] + stats[3], GROUP))
    inv_ref[...] = jnp.broadcast_to(inverse, inv_ref.shape)
    standard[...] = (mixed[...] - centre) * inverse
    pn[32 : 32 + GROUP, :] = (standard[...] * gain).astype(BF16).astype(F32)
    for side in range(2):
        halos[side].wait_recv()
        for h in range(4):
            remote(
                stats.at[0, :, pl.ds(0, 128)], nst.at[side, h],
                hsend.at[side * 4 + h], hrecv.at[side * 4 + h], (after, hd),
            ).wait_recv()
        there = nst[side, 0] + nst[side, 1] + nst[side, 2] + nst[side, 3]
        centre, inverse = norm_of(turned_back(there, 128)[slice(96, 128) if side == 0 else slice(0, 32)])
        normed = (((hm[side] - centre) * inverse) * gain).astype(BF16).astype(F32)
        if side == 0:
            pn[0:32, :] = jnp.where(t > 0, normed, 0.0)
        else:
            pn[32 + GROUP :, :] = jnp.where(t < n - 1, normed, 0.0)

    for cb in range(3):
        cols = slice(cb * 128, cb * 128 + 128)

        def convolve(i, carry, cols=cols):
            base = pl.multiple_of(i * 96, 32)
            rows = pn[pl.ds(base, 128), cols]
            total = jnp.zeros((96, 128), F32)
            for r in range(8):
                moved = rows[r : r + 120]
                for a in range(4):
                    m = 8 * a + r
                    total = total + ck_ref[m : m + 1, cols] * moved[8 * a : 8 * a + 96]
            gate = jax.nn.sigmoid(total)
            silu[pl.ds(base, 96), cols] = total * gate
            cg[pl.ds(base, 96), cols] = (
                cote[pl.ds(base, 96), cols] * gate * (1.0 + total * (1.0 - gate))
            )
            return carry

        lax.fori_loop(0, 3, convolve, 0)

    for cb in range(3):
        cols = slice(cb * 128, cb * 128 + 128)

        def correlate(i, carry, cols=cols):
            base = pl.multiple_of(i * 64, 64)
            rows = cg[pl.ds(base, 96), cols]
            total = jnp.zeros((64, 128), F32)
            for r in range(8):
                moved = rows if r == 0 else rows[r : r + 88]
                for a in range(5 if r == 0 else 4):
                    u = 8 * a + r
                    if u == 0:
                        continue
                    m = 32 - u
                    total = total + ck_ref[m : m + 1, cols] * moved[8 * a : 8 * a + 64]
            ng[pl.ds(base, 64), cols] = total
            prod = total * standard[pl.ds(base, 64), cols]
            kacc[TAPS, :, cols] = kacc[TAPS, :, cols] + jnp.sum(prod.reshape(8, 8, 128), axis=0)
            grad = rows[16:80]
            normed = pn[pl.ds(base + 16, 96), cols]
            for r in range(8):
                moved = normed[r : r + 88]
                for a in range(4):
                    m = 8 * a + r
                    prod = grad * moved[8 * a : 8 * a + 64]
                    kacc[m, :, cols] = kacc[m, :, cols] + jnp.sum(prod.reshape(8, 8, 128), axis=0)
            return carry

        lax.fori_loop(0, 4, correlate, 0)

    blk_ref[...] = (mixed[...] + silu[16 : 16 + GROUP, :]).astype(BF16)

    kpart[...] = jnp.zeros(kpart.shape, F32)
    summed = jnp.sum(kacc[...], axis=1)
    for cb in range(3):
        kpart[cb * 40 : cb * 40 + 40, :] = summed[:, cb * 128 : cb * 128 + 128]

    def exchange(count, here, place, source, buf, ss, rs):
        for a in range(count):
            @pl.when(here != a)
            def _(a=a):
                remote(source(a), buf.at[here], ss.at[a], rs.at[here], place(a)).start()

    def finish(count, here, place, source, buf, ss, rs):
        for a in range(count):
            @pl.when(here != a)
            def _(a=a):
                remote(source(a), buf.at[a], ss.at[a], rs.at[a], place(a)).wait()

    z_parts = (RUN, z, along_z, lambda a: kpart.at[pl.ds(16 * a, 16)], rz, zs, zr)
    x_parts = (4, x, along_x, lambda a: rx.at[x], rx, xs, xr)
    y_parts = (4, y, along_y, lambda a: ry.at[y], ry, ys, yr)
    g_parts = (RUN, z, along_z, lambda a: kg_ref.at[z], kg_ref, gs, gr)

    sg = ng[...] * gain
    stats2[pl.ds(hd, 1)] = row_pair(
        jnp.sum(sg, axis=1, keepdims=True), jnp.sum(sg * standard[...], axis=1, keepdims=True)
    )
    stat_copies2 = to_heads(stats2, usend, urecv)
    for c in stat_copies2:
        c.start()
    exchange(*z_parts)
    rz[pl.ds(z, 1)] = kpart[pl.ds(pl.multiple_of(z * 16, 16), 16), :][None]
    for c in stat_copies2:
        c.wait_recv()
    sums = turned_back(stats2[0] + stats2[1] + stats2[2] + stats2[3], GROUP)
    grad = cote[16 : 16 + GROUP, :] + inv_ref[:, 0:1] * (
        ng[...] * gain - sums[:, 0:1] / D - standard[...] * (sums[:, 1:2] / D)
    )
    rgb = grad.astype(BF16)
    rgall[pl.ds(hd, 1)] = rgb[None]

    def share(c, which, to, ss, rs):
        rows = rgall.at[which, quarter(c)]
        return remote(rows, rows, ss.at[c], rs.at[c], (t, to))

    share_far = [share(c, hd, far, ssend, srecv) for c in range(4)]
    share_near = remote(rgall.at[hd], rgall.at[hd], ssem.at[6], rsem.at[6], (t, partner))
    for c in share_far:
        c.start()
    share_near.start()
    rg_ref[...] = rgb

    def back(j):
        return dot(weight_cols(0, j), rgall[pl.ds(j, 1)].reshape(GROUP, COLS), NT)

    racc[...] = back(hd)
    remote(rgall.at[partner], rgall.at[partner], ssem.at[6], rsem.at[6], (t, partner)).wait_recv()
    racc[...] = racc[...] + back(partner)
    dq[...] = jnp.zeros(dq.shape, F32)
    finish(*z_parts)
    rx[pl.ds(x, 1)] = sum((rz[a] for a in range(1, RUN)), rz[0])[None]
    exchange(*x_parts)
    passed = []
    for c in range(4):
        share(c, far, far, ssend, srecv).wait_recv()
        passed.append(share(c, far, partner, psend, precv))
        passed[c].start()
    racc[...] = racc[...] + back(far)
    for c in range(4):
        share(c, diag, partner, psend, precv).wait_recv()
    dgrad[...] = (racc[...] + back(diag)).astype(BF16).reshape(4, DH, GROUP)

    spread = []
    for s in range(1, 4):
        to = lax.rem(i + s, 4)
        spread.append(remote(dgrad.at[to], gq.at[i], gsend.at[s], grecv.at[i], (base + to, hd)))
    for c in spread:
        c.start()
    gq[pl.ds(i, 1)] = dgrad[pl.ds(i, 1)]
    finish(*x_parts)
    ry[pl.ds(y, 1)] = (rx[0] + rx[1] + rx[2] + rx[3])[None]
    exchange(*y_parts)
    for s in range(1, 4):
        j = lax.rem(i + 4 - s, 4)
        remote(dgrad.at[0], gq.at[j], gsend.at[s], grecv.at[j], (following, hd)).wait_recv()
    delta[...] = jnp.sum(gq[...].astype(F32) * mine[...].astype(F32), axis=1, keepdims=True)

    def terms(group_for, place_for):
        part[...] = jnp.zeros(part.shape, F32)
        for j in range(4):
            w, place = group_for(j), place_for(j)
            kt, qt, gt = win[w, 0], qb[j], gq[j]
            s = scores(knat[w], qt, block_limit(gm_ref, gl_ref, base, w, j))
            p = jnp.exp2(s - lse[j])
            ds = (p * (dot(vnat[w], gt, NN) - delta[j])).astype(BF16)
            dq[j] = dq[j] + dot(kt, ds, NN)
            part[place, 0] = part[place, 0] + dot(qt, ds, NT) * SCALE
            part[place, 1] = part[place, 1] + dot(gt, p.astype(BF16), NT)

    def to_before(j):
        return remote(out.at[4 + j], rnext.at[i], nsend.at[j], nrecv.at[i], (earlier + j, hd))

    def before_step(s, carry):
        j = lax.rem(i + s, 4)
        terms(lambda _: 4 + j, lambda _: 0)
        out[4 + j] = part[0].astype(BF16)
        to_before(j).start()
        return carry

    lax.fori_loop(0, 4, before_step, 0)
    finish(*y_parts)
    kg_ref[pl.ds(z, 1)] = (ry[0] + ry[1] + ry[2] + ry[3])[None]
    exchange(*g_parts)

    def to_across(w):
        return remote(
            out.at[w], racross.at[w], xsend.at[w], xrecv.at[w], (lax.rem(t + n - RUN, n), hd)
        )

    def own_step(s, carry):
        m = 3 - s
        terms(lambda j: jnp.where(j >= m, 8 + m, m), lambda j: jnp.where(j >= m, 0, 1))
        ownp[m] = part[0]

        @pl.when(m >= 1)
        def _():
            out[m] = part[1].astype(BF16)
            to_across(m).start()

        return carry

    lax.fori_loop(0, 4, own_step, 0)

    def give(s):
        j = lax.rem(i + s, 4)
        return remote(dqs.at[j], rq.at[i], qsend.at[s], qrecv.at[i], (base + j, hd))

    dqs[...] = (dq[...] * SCALE).astype(BF16)
    for s in range(1, 4):
        give(s).start()
    rq[pl.ds(i, 1)] = dqs[pl.ds(i, 1)]

    def to_own(j):
        return remote(out.at[8 + j], rown.at[i], osend.at[j], orecv.at[i], (base + j, hd))

    for j in (0, 3, 2, 1):
        if j:
            to_across(j).wait_recv()
            out[8 + j] = (ownp[j] + racross[j].astype(F32)).astype(BF16)
        else:
            out[8 + j] = ownp[j].astype(BF16)

        @pl.when(j != i)
        def _(j=j):
            to_own(j).start()

    rown[pl.ds(i, 1)] = out[pl.ds(8 + i, 1)]
    finish(*g_parts)
    for c in own_kv + own_q + next_kv[2:] + [cot_up, cot_down, weight, swap] + cross + halos:
        c.wait_send()
    for c in stat_copies + stat_copies2 + share_far + [share_near] + passed + spread:
        c.wait_send()
    for s in range(1, 4):
        onward(s).wait_send()
        give_att(s).wait_send()
        give(s).wait_send()
        to_across(s).wait_send()
    for s in range(1, 4):
        j = lax.rem(i + 4 - s, 4)
        remote(dqs.at[0], rq.at[j], qsend.at[s], qrecv.at[j], (following, hd)).wait_recv()
        remote(out.at[8], rown.at[j], osend.at[0], orecv.at[j], (following, hd)).wait_recv()
    for j in range(4):
        remote(out.at[4], rnext.at[j], nsend.at[0], nrecv.at[j], (following, hd)).wait_recv()
    for j in range(4):
        to_before(j).wait_send()

        @pl.when(j != i)
        def _(j=j):
            to_own(j).wait_send()


def finals(
    blk, rg, kg, rq, rown, rnext,
    block_out, residual_grad, query_grad, key_grad, value_grad, gain_grad, kernel_grad,
):
    block_out[...] = blk[...]
    residual_grad[...] = rg[...]
    query_grad[...] = rq[...].reshape(COLS, GROUP).T
    for a, ref in enumerate((key_grad, value_grad)):
        both = rown[:, a].astype(F32) + rnext[:, a].astype(F32)
        ref[...] = both.astype(BF16).reshape(COLS, GROUP).T
    flat = kg[...].reshape(128, 128)
    for cb in range(3):
        cols = slice(cb * 128, cb * 128 + 128)
        kernel_grad[:, cols] = flat[cb * 40 : cb * 40 + TAPS]
        gain_grad[cols] = flat[cb * 40 + TAPS]


VM = pl.BlockSpec(memory_space=pltpu.VMEM)
SM = pl.BlockSpec(memory_space=pltpu.SMEM)
HB = pl.BlockSpec(memory_space=pltpu.HBM)
DMA = pltpu.SemaphoreType.DMA


def shape(dims, kind=BF16):
    return jax.ShapeDtypeStruct(dims, kind)


def body(
    queries, key_input, value_input, residual, out_weight, norm_gain, conv_kernel, cotangent,
    group_mask, group_len,
):
    turned = (4, DH, GROUP)
    block = (GROUP, COLS)
    row = (4, 1, GROUP)
    window = (12, 2, DH, GROUP)
    pieces = (4, 2, DH, GROUP)
    longer = (GROUP + 32, COLS)
    across = (4, 16, 128)
    results = pl.pallas_call(
        conformer,
        out_shape=[
            shape(block), shape(block), shape((8, 16, 128), F32),
            shape(turned), shape(pieces), shape(pieces),
        ],
        in_specs=[HB] * 6 + [VM, VM, SM, SM],
        out_specs=[VM] * 6,
        scratch_shapes=[
            pltpu.VMEM(dims, kind)
            for dims, kind in (
                ((3,) + block, BF16), (pieces, BF16), (turned, BF16), (window, BF16),
                (turned, BF16), ((12, GROUP, DH), BF16), ((12, GROUP, DH), BF16), (turned, BF16),
                (turned, F32), (row, F32), (row, F32), (row, F32), (turned, BF16),
                ((2,) + block, BF16), ((2, COLS, D), BF16), (block, BF16), (block, BF16),
                ((2, 16, COLS), BF16),
                (block, BF16), (block, BF16), (block, F32), (block, F32), ((GROUP, 128), F32),
                ((4, 8, GROUP), F32), ((4, 8, GROUP), F32), ((2, 4, 8, 128), F32),
                ((2, 32, COLS), F32), ((128, GROUP), F32),
                ((GROUP + 64, COLS), F32), (longer, F32), (longer, F32), (longer, F32),
                (block, F32), ((40, 8, COLS), F32), ((128, 128), F32),
                ((4,) + block, BF16), ((COLS, GROUP), F32), ((8, 16, 128), F32), (across, F32),
                (across, F32), (turned, BF16), (turned, BF16), (row, F32), (turned, F32),
                (turned, BF16), ((2, 2, DH, GROUP), F32), (pieces, F32), (window, BF16),
                (pieces, BF16),
            )
        ]
        + [DMA((6,))]
        + [DMA((4,))] * 30
        + [DMA((8,))] * 6
        + [DMA((4,))] * 4
        + [DMA((7,))] * 2,
        compiler_params=pltpu.CompilerParams(
            collective_id=0, has_side_effects=True, vmem_limit_bytes=VMEM_LIMIT
        ),
        name="conformer",
    )(
        queries, key_input, value_input, out_weight, residual, cotangent,
        norm_gain, conv_kernel, group_mask.T, group_len,
    )
    return pl.pallas_call(
        finals,
        out_shape=[shape(block)] * 5 + [shape((COLS,), F32), shape((TAPS, COLS), F32)],
        in_specs=[VM] * 6,
        out_specs=[VM] * 7,
        compiler_params=pltpu.CompilerParams(vmem_limit_bytes=VMEM_LIMIT),
        name="finals",
    )(*results)


def solution(mesh):
    rows = P("tm", "heads")
    in_specs = (
        rows, rows, rows, rows, P("heads", None), P("heads"), P(None, "heads"), rows, P(), P(),
    )
    out_specs = (rows, rows, rows, rows, rows, P("heads"), P(None, "heads"))
    return jax.shard_map(body, mesh=mesh, in_specs=in_specs, out_specs=out_specs, check_vma=False)
```

```python
import jax
import jax.numpy as jnp
from jax import lax
from jax.experimental import pallas as pl
from jax.experimental.pallas import tpu as pltpu
from jax.sharding import PartitionSpec as P

D = 1536
DH = 96
GROUP = 256
COLS = 384
RUN = 8
TAPS = 32
SCALE = DH ** (-0.5)
SCALE2 = SCALE * 1.4426950408889634
NEG = -1e30
F32 = jnp.float32
BF16 = jnp.bfloat16
VMEM_LIMIT = 58 * 1024 * 1024

NT = (((1,), (1,)), ((), ()))
NN = (((1,), (0,)), ((), ()))


def dot(a, b, dims):
    return lax.dot_general(a, b, dims, preferred_element_type=F32)


def remote(src, dst, send_sem, recv_sem, where):
    return pltpu.make_async_remote_copy(
        src_ref=src,
        dst_ref=dst,
        send_sem=send_sem,
        recv_sem=recv_sem,
        device_id=where,
        device_id_type=pl.DeviceIdType.MESH,
    )


def greet(places):
    barrier = pltpu.get_barrier_semaphore()
    for where in places:
        pl.semaphore_signal(barrier, inc=1, device_id=where, device_id_type=pl.DeviceIdType.MESH)
    return lambda: pl.semaphore_wait(barrier, len(places))


def quad_of(t, n):
    i = lax.rem(t, 4)
    base = t - i
    return i, base, lax.rem(base + 4, n), lax.rem(base + n - 4, n)


def quad_places(t, n, hd):
    i, base, following, earlier = quad_of(t, n)
    places = [(base + lax.rem(i + s, 4), hd) for s in range(1, 4)]
    places += [(following + s, hd) for s in range(4)] + [(earlier + s, hd) for s in range(4)]
    return places + [(lax.rem(t + RUN, n), hd), (lax.rem(t + n - RUN, n), hd)]


def block_limit(gm_ref, gl_ref, base, w, j):
    source = base + w - 8
    lag = 8 + j - w
    return jnp.where(source >= 0, gm_ref[lag, base + j] * gl_ref[jnp.maximum(source, 0)], 0)


def scores(k, qt, limit):
    s = dot(k, qt, NN)
    inside = lax.broadcasted_iota(jnp.int32, s.shape, 0) < limit
    return jnp.where(inside, s * SCALE2, NEG)


def head_peers(hd):
    partner = hd + 1 - 2 * lax.rem(hd, 2)
    return partner, lax.rem(hd + 2, 4), lax.rem(partner + 2, 4)


def quarter(c):
    return pl.ds(c * 64, 64)


def conformer(
    q_hbm, k_hbm, v_hbm, w_hbm, res_hbm, cot_hbm, gain_ref, ck_ref, gm_ref, gl_ref,
    blk_ref, rg_ref, dq_ref, kg_ref, rown, rnext,
    qkv, kvs, qs, win, qb, knat, qnat, gnat, lse_wide, delta_wide, mine, acc, m_s, l_s, lse, att, w_ref, wpart, wfar,
    res_ref, cot_ref, hc,
    mixed, standard, inv_ref, stats, stats2, nst, hm, turn,
    pn, cote, cg, silu, ng, kacc, kpart,
    rgb, dout, din, dhalf, near, cross, rz, rx, ry, gq, delta, dq, dqs, rq, part, ownp, out, racross,
    load, fosend, forecv, fqsend, fqrecv, fnsend, fnrecv, fxsend, fxrecv, asend, arecv,
    gsend, grecv, nsend, nrecv, xsend, xrecv, osend, orecv, qsend, qrecv,
    bsend, brecv, wxs, wxr, wys, wyr, tsend, trecv, dsums, dsumr, csend, crecv, usend, urecv,
    zs, zr, gs, gr, hsend, hrecv, dsend, drecv, xs, xr, ys, yr, ssem, rsem,
):
    t, hd = lax.axis_index("tm"), lax.axis_index("heads")
    n = lax.axis_size("tm")
    i, base, following, earlier = quad_of(t, n)
    partner, far, diag = head_peers(hd)
    after, before = lax.rem(t + 1, n), lax.rem(t + n - 1, n)
    z, x, y = lax.rem(t, RUN), lax.rem(t // RUN, 4), t // (4 * RUN)

    def along_z(a):
        return ((t - z + a), hd)

    def along_x(a):
        return ((t + (a - x) * RUN), hd)

    def along_y(a):
        return ((t + (a - y) * 4 * RUN), hd)

    places = quad_places(t, n, hd) + [(t, partner), (t, diag)]
    places += [(base + j, far) for j in range(4)]
    places += [(to, lax.rem(hd + d, 4)) for to in (after, before) for d in range(1, 4)]
    places += [along_x(lax.rem(x + d, 4)) for d in range(1, 4)]
    places += [along_y(lax.rem(y + d, 4)) for d in range(1, 4)]
    entered = greet(places)
    gain = gain_ref[...].reshape(1, COLS)

    loads = [
        pltpu.make_async_copy(ref, to, load.at[a])
        for a, (ref, to) in enumerate(
            (
                (k_hbm, qkv.at[0]), (v_hbm, qkv.at[1]), (q_hbm, qkv.at[2]),
                (cot_hbm, cot_ref), (w_hbm, w_ref), (res_hbm, res_ref),
            )
        )
    ]
    for c in loads:
        c.start()
    for a in range(2):
        loads[a].wait()
        kvs[:, a] = qkv[a].T.reshape(4, DH, GROUP)

    own_kv, own_q, next_kv = [], [], []
    for s in range(1, 4):
        to = lax.rem(i + s, 4)
        own_kv.append(
            remote(kvs.at[to], win.at[8 + i], fosend.at[s], forecv.at[i], (base + to, hd))
        )
        own_q.append(remote(qs.at[to], qb.at[i], fqsend.at[s], fqrecv.at[i], (base + to, hd)))
    for s in range(4):
        to = lax.rem(i + s, 4)
        next_kv.append(
            remote(kvs.at[to], win.at[4 + i], fnsend.at[s], fnrecv.at[i], (following + to, hd))
        )

    entered()
    next_kv[0].start()
    for c in own_kv:
        c.start()
    loads[2].wait()
    qs[...] = qkv[2].T.reshape(4, DH, GROUP)
    for c in own_q:
        c.start()
    next_kv[1].start()
    next_kv[2].start()
    win[pl.ds(8 + i, 1)] = kvs[pl.ds(i, 1)]
    qb[pl.ds(i, 1)] = qs[pl.ds(i, 1)]

    def onward(j):
        return remote(
            win.at[8 + j], win.at[j], fxsend.at[j], fxrecv.at[j], (lax.rem(t + RUN, n), hd)
        )

    @pl.when(i >= 1)
    def _():
        onward(i).start()

    loads[3].wait()
    loads[4].wait()
    cot_up = remote(cot_ref.at[pl.ds(GROUP - 16, 16)], hc.at[0], ssem.at[0], rsem.at[0], (after, hd))
    cot_down = remote(cot_ref.at[pl.ds(0, 16)], hc.at[1], ssem.at[1], rsem.at[1], (before, hd))
    cot_up.start()
    cot_down.start()

    def columns(h):
        return pl.ds(pl.multiple_of(h * COLS, 128), COLS)

    weight = remote(w_ref.at[:, columns(partner)], wpart, ssem.at[2], rsem.at[2], (t, partner))
    weight.start()
    plane = y * 4 + x
    sliver = pl.ds(pl.multiple_of(lax.rem(plane, 8) * 48, 16), 48)
    other = 2 * (1 - hd // 2)

    def to_far_core(k):
        return remote(
            w_ref.at[sliver, columns(other + k)], wfar.at[plane],
            ssem.at[3 + k], rsem.at[3], (t, other + k),
        )

    @pl.when(lax.rem(hd, 2) == plane // 8)
    def _():
        to_far_core(0).start()
        to_far_core(1).start()

    def over_x(a):
        return remote(wfar.at[plane], wfar.at[plane], wxs.at[a], wxr.at[x], along_x(a))

    def over_y(a):
        rows = wfar.at[pl.ds(4 * y, 4)]
        return remote(rows, rows, wys.at[a], wyr.at[y], along_y(a))

    def pass_weights(count, here, copy):
        for a in range(count):
            @pl.when(here != a)
            def _(a=a):
                copy(a).start()

    def weights_from_x():
        for a in range(4):
            @pl.when(x != a)
            def _(a=a):
                there = wfar.at[y * 4 + a]
                remote(there, there, wxs.at[a], wxr.at[a], along_x(a)).wait_recv()

    def weights_from_y():
        for a in range(4):
            @pl.when(y != a)
            def _(a=a):
                there = wfar.at[pl.ds(4 * a, 4)]
                remote(there, there, wys.at[a], wyr.at[a], along_y(a)).wait_recv()

    m_s[...] = jnp.full(m_s.shape, NEG, F32)
    l_s[...] = jnp.zeros(l_s.shape, F32)
    acc[...] = jnp.zeros(acc.shape, F32)

    for s in range(1, 4):
        j = lax.rem(i + 4 - s, 4)
        remote(kvs.at[0], win.at[8 + j], fosend.at[s], forecv.at[j], (following, hd)).wait_recv()

        @pl.when(j >= 1)
        def _(j=j):
            onward(j).start()

    for s in range(1, 4):
        j = lax.rem(i + 4 - s, 4)
        remote(qs.at[0], qb.at[j], fqsend.at[s], fqrecv.at[j], (following, hd)).wait_recv()

    next_kv[3].start()
    remote(wfar.at[plane], wfar.at[plane], ssem.at[3], rsem.at[3], (t, far)).wait_recv()
    pass_weights(4, x, over_x)

    def turn_keys(w):
        knat[w] = win[w, 0].T

    def attend_one(j, w):
        s = scores(knat[w], qb[j], block_limit(gm_ref, gl_ref, base, w, j))
        m_old = m_s[j]
        m_new = jnp.maximum(m_old, jnp.max(s, axis=0, keepdims=True))
        alpha = jnp.exp2(m_old - m_new)
        p = jnp.exp2(s - m_new)
        m_s[j] = m_new
        l_s[j] = l_s[j] * alpha + jnp.sum(p, axis=0, keepdims=True)
        acc[j] = acc[j] * alpha + dot(win[w, 1], p.astype(BF16), NN)

    def attend(group_for):
        for j in range(4):
            attend_one(j, group_for(j))

    def own_step_in(m, carry):
        @pl.when(m >= 1)
        def _():
            remote(win.at[m], win.at[m], fxsend.at[m], fxrecv.at[m], (following, hd)).wait_recv()
            turn_keys(m)

        turn_keys(8 + m)
        attend(lambda j: jnp.where(j >= m, 8 + m, m))
        return carry

    lax.fori_loop(0, 4, own_step_in, 0)
    weights_from_x()
    pass_weights(4, y, over_y)

    def arrive_before(s):
        j = lax.rem(i + 4 - s, 4)
        remote(kvs.at[0], win.at[4 + j], fnsend.at[0], fnrecv.at[j], (following, hd)).wait_recv()
        turn_keys(4 + j)
        return 4 + j

    def before_step_in(s, carry):
        w = arrive_before(s)
        attend(lambda _: w)
        return carry

    lax.fori_loop(0, 3, before_step_in, 0)
    last = arrive_before(3)

    def give_att(s):
        j = lax.rem(i + s, 4)
        return remote(mine.at[j], att.at[hd, i], asend.at[s], arecv.at[i], (base + j, hd))

    def give_att_far(s):
        j = lax.rem(i + s, 4)
        return remote(mine.at[j], att.at[hd, i], bsend.at[s], brecv.at[i], (base + j, far))

    for s in (1, 2, 3, 0):
        j = lax.rem(i + s, 4)
        attend_one(j, last)
        mine[j] = (acc[j] / l_s[j]).astype(BF16)
        give_att_far(s).start()
        if s:
            give_att(s).start()
    att[pl.ds(hd, 1), pl.ds(i, 1)] = mine[pl.ds(i, 1)][None]

    def to_partner(k, j):
        piece = att.at[far if k else hd, j]
        return remote(piece, piece, dsend.at[4 * k + j], drecv.at[4 * k + j], (t, partner))

    def from_partner(k, j):
        piece = att.at[diag if k else partner, j]
        remote(piece, piece, dsend.at[4 * k + j], drecv.at[4 * k + j], (t, partner)).wait_recv()

    to_partner(0, i).start()
    lse[...] = m_s[...] + jnp.log2(l_s[...])
    cot_up.wait_recv()
    cot_down.wait_recv()
    cote[16 : 16 + GROUP, :] = cot_ref[...].astype(F32)
    cote[0:16, :] = jnp.where(t > 0, hc[0].astype(F32), 0.0)
    cote[16 + GROUP :, :] = jnp.where(t < n - 1, hc[1].astype(F32), 0.0)
    loads[5].wait()
    weight.wait_recv()
    for s in range(1, 4):
        j = lax.rem(i + 4 - s, 4)
        remote(mine.at[0], att.at[hd, j], asend.at[s], arecv.at[j], (following, hd)).wait_recv()
        to_partner(0, j).start()
    weights_from_y()

    def weight_rows(which):
        if which == 0:
            return w_ref[:, columns(hd)]
        if which == 1:
            return wpart[...]
        k = lax.rem(hd, 2) if which == 2 else 1 - lax.rem(hd, 2)
        return wfar[pl.ds(8 * k, 8)].reshape(COLS, COLS)

    def project(which):
        shard = (hd, partner, far, diag)[which]
        there = att[pl.ds(shard, 1)].reshape(COLS, GROUP).T
        return dot(there, weight_rows(which), NN)

    mixed[...] = project(0) + res_ref[...].astype(F32)

    kacc[...] = jnp.zeros(kacc.shape, F32)
    turn[...] = jnp.zeros(turn.shape, F32)

    def turned_back(total, width):
        turn[0:8, 0:width] = total
        return turn[:, 0:width].T

    def widen(rows, wide):
        columns_of = turned_back(jnp.concatenate([rows, rows], axis=0).reshape(8, GROUP), GROUP)
        for j in range(4):
            wide[j] = jnp.broadcast_to(columns_of[:, j : j + 1], (GROUP, 128))

    widen(lse[...], lse_wide)
    for j in range(4):
        qnat[j] = qb[j].T
    dq[...] = jnp.zeros(dq.shape, F32)
    for j in range(4):
        from_partner(0, j)
    mixed[...] = mixed[...] + project(1)
    def add_piece(shard, k, j):
        rows = wfar[pl.ds(8 * k + 2 * j, 2)].reshape(DH, COLS)
        mixed[...] = mixed[...] + dot(att[shard, j].T, rows, NN)

    core = lax.rem(hd, 2)
    for s in (1, 2, 3, 0):
        j = lax.rem(i + 4 - s, 4)
        remote(mine.at[0], att.at[far, j], bsend.at[s], brecv.at[j], (following, hd)).wait_recv()
        to_partner(1, j).start()
        add_piece(far, core, j)
    for s in (1, 2, 3, 0):
        j = lax.rem(i + 4 - s, 4)
        from_partner(1, j)
        add_piece(diag, 1 - core, j)

    halos = [
        remote(mixed.at[pl.ds(GROUP - 32, 32)], hm.at[0], ssem.at[7], rsem.at[7], (after, hd)),
        remote(mixed.at[pl.ds(0, 32)], hm.at[1], ssem.at[8], rsem.at[8], (before, hd)),
    ]
    for c in halos:
        c.start()

    def row_pair(a, b):
        lane = lax.broadcasted_iota(jnp.int32, (a.shape[0], 128), 1)
        return jnp.where(lane == 0, a, jnp.where(lane == 1, b, 0.0)).T[0:8, :][None]

    def to_heads(buf, ss, rs):
        return [
            remote(buf.at[hd], buf.at[hd], ss.at[a], rs.at[a], (t, lax.rem(hd + a + 1, 4)))
            for a in (1, 2, 0)
        ]

    mx = mixed[...]
    stats[pl.ds(hd, 1)] = row_pair(
        jnp.sum(mx, axis=1, keepdims=True), jnp.sum(mx * mx, axis=1, keepdims=True)
    )
    stat_copies = to_heads(stats, tsend, trecv)
    for c in stat_copies:
        c.start()
    for side, to in ((0, after), (1, before)):
        ends = stats.at[hd, :, pl.ds(128 - 128 * side, 128)]
        for h in range(4):
            c = remote(ends, nst.at[side, hd], hsend.at[side * 4 + h], hrecv.at[side * 4 + hd], (to, h))
            c.start()
            stat_copies.append(c)
    for c in stat_copies[:3]:
        c.wait_recv()

    def norm_of(back):
        centre = back[:, 0:1] / D
        return centre, lax.rsqrt(back[:, 1:2] / D - centre * centre + 1e-05)

    centre, inverse = norm_of(turned_back(stats[0] + stats[1] + stats[2] + stats[3], GROUP))
    inv_ref[...] = jnp.broadcast_to(inverse, inv_ref.shape)
    standard[...] = (mixed[...] - centre) * inverse
    pn[32 : 32 + GROUP, :] = (standard[...] * gain).astype(BF16).astype(F32)
    for side in range(2):
        halos[side].wait_recv()
        for h in range(4):
            remote(
                stats.at[0, :, pl.ds(0, 128)], nst.at[side, h],
                hsend.at[side * 4 + h], hrecv.at[side * 4 + h], (after, hd),
            ).wait_recv()
        there = nst[side, 0] + nst[side, 1] + nst[side, 2] + nst[side, 3]
        centre, inverse = norm_of(turned_back(there, 128)[slice(96, 128) if side == 0 else slice(0, 32)])
        normed = (((hm[side] - centre) * inverse) * gain).astype(BF16).astype(F32)
        if side == 0:
            pn[0:32, :] = jnp.where(t > 0, normed, 0.0)
        else:
            pn[32 + GROUP :, :] = jnp.where(t < n - 1, normed, 0.0)

    def convolve_rows(first, last):
        for cb in range(3):
            cols = slice(cb * 128, cb * 128 + 128)

            def convolve(a, carry, cols=cols):
                begin = pl.multiple_of(a * 96, 32)
                rows = pn[pl.ds(begin, 128), cols]
                total = jnp.zeros((96, 128), F32)
                for r in range(8):
                    moved = rows[r : r + 120]
                    for b in range(4):
                        m = 8 * b + r
                        total = total + ck_ref[m : m + 1, cols] * moved[8 * b : 8 * b + 96]
                gate = jax.nn.sigmoid(total)
                silu[pl.ds(begin, 96), cols] = total * gate
                cg[pl.ds(begin, 96), cols] = (
                    cote[pl.ds(begin, 96), cols] * gate * (1.0 + total * (1.0 - gate))
                )
                return carry

            lax.fori_loop(first, last, convolve, 0)

    def correlate_rows(first, last):
        for cb in range(3):
            cols = slice(cb * 128, cb * 128 + 128)

            def correlate(a, carry, cols=cols):
                begin = pl.multiple_of(a * 64, 64)
                rows = cg[pl.ds(begin, 96), cols]
                total = jnp.zeros((64, 128), F32)
                for r in range(8):
                    moved = rows if r == 0 else rows[r : r + 88]
                    for b in range(5 if r == 0 else 4):
                        u = 8 * b + r
                        if u == 0:
                            continue
                        m = 32 - u
                        total = total + ck_ref[m : m + 1, cols] * moved[8 * b : 8 * b + 64]
                ng[pl.ds(begin, 64), cols] = total
                return carry

            lax.fori_loop(first, last, correlate, 0)

    def kernel_sums():
        for cb in range(3):
            cols = slice(cb * 128, cb * 128 + 128)

            def taps(i, carry, cols=cols):
                base = pl.multiple_of(i * 64, 64)
                prod = ng[pl.ds(base, 64), cols] * standard[pl.ds(base, 64), cols]
                kacc[TAPS, :, cols] = kacc[TAPS, :, cols] + jnp.sum(prod.reshape(8, 8, 128), axis=0)
                grad = cg[pl.ds(base + 16, 64), cols]
                normed = pn[pl.ds(base + 16, 96), cols]
                for r in range(8):
                    moved = normed[r : r + 88]
                    for a in range(4):
                        m = 8 * a + r
                        prod = grad * moved[8 * a : 8 * a + 64]
                        kacc[m, :, cols] = kacc[m, :, cols] + jnp.sum(
                            prod.reshape(8, 8, 128), axis=0
                        )
                return carry

            lax.fori_loop(0, 4, taps, 0)
        kpart[...] = jnp.zeros(kpart.shape, F32)
        summed = jnp.sum(kacc[...], axis=1)
        for cb in range(3):
            kpart[cb * 40 : cb * 40 + 40, :] = summed[:, cb * 128 : cb * 128 + 128]

    def exchange(count, here, place, source, buf, ss, rs):
        for a in range(count):
            @pl.when(here != a)
            def _(a=a):
                remote(source(a), buf.at[here], ss.at[a], rs.at[here], place(a)).start()

    def finish(count, here, place, source, buf, ss, rs):
        for a in range(count):
            @pl.when(here != a)
            def _(a=a):
                remote(source(a), buf.at[a], ss.at[a], rs.at[a], place(a)).wait()

    z_parts = (RUN, z, along_z, lambda a: kpart.at[pl.ds(16 * a, 16)], rz, zs, zr)
    x_parts = (4, x, along_x, lambda a: rx.at[x], rx, xs, xr)
    y_parts = (4, y, along_y, lambda a: ry.at[y], ry, ys, yr)
    g_parts = (RUN, z, along_z, lambda a: kg_ref.at[z], kg_ref, gs, gr)

    def lanes(h):
        return pl.ds(128 * h, 128)

    def half_rows(h):
        return slice(128 * h, 128 * h + 128)

    def half_sums(h):
        rows = half_rows(h)
        sg = ng[rows, :] * gain
        stats2[pl.ds(hd, 1), :, rows] = row_pair(
            jnp.sum(sg, axis=1, keepdims=True),
            jnp.sum(sg * standard[rows, :], axis=1, keepdims=True),
        )
        mine_here = stats2.at[hd, :, lanes(h)]
        copies = [
            remote(
                mine_here, mine_here, usend.at[4 * h + a], urecv.at[4 * h + a],
                (t, lax.rem(hd + a + 1, 4)),
            )
            for a in (1, 2, 0)
        ]
        for c in copies:
            c.start()
        return copies

    convolve_rows(0, 2)
    correlate_rows(0, 2)
    stat_copies2 = [half_sums(0)]
    convolve_rows(2, 3)
    correlate_rows(2, 4)
    stat_copies2.append(half_sums(1))

    def partial(which, h):
        return dot(weight_rows(which), rgb[half_rows(h), :], NT)

    def give_sum(h, kind):
        return remote(
            dout.at[h, kind], din.at[h, kind], dsums.at[2 * h + kind], dsumr.at[2 * h + kind],
            (t, partner),
        )

    def to_far_heads(h, s):
        j = lax.rem(i + s, 4)
        return remote(
            cross.at[h, j], gq.at[1, i, :, lanes(h)], csend.at[4 * h + s], crecv.at[4 * h + i],
            (base + j, far),
        )

    for h in range(2):
        rows = half_rows(h)
        for c in stat_copies2[h]:
            c.wait_recv()
        there = stats2[0, :, rows] + stats2[1, :, rows] + stats2[2, :, rows] + stats2[3, :, rows]
        sums = turned_back(there, 128)
        grad = cote[16 + 128 * h : 144 + 128 * h, :] + inv_ref[rows, 0:1] * (
            ng[rows, :] * gain - sums[:, 0:1] / D - standard[rows, :] * (sums[:, 1:2] / D)
        )
        rgb[rows, :] = grad.astype(BF16)
        dout[h, 0] = partial(3, h)
        give_sum(h, 0).start()
        dhalf[...] = partial(2, h)
        give_sum(h, 0).wait_recv()
        cross[h] = (dhalf[...] + din[h, 0]).astype(BF16).reshape(4, DH, 128)
        for s in (1, 2, 3, 0):
            to_far_heads(h, s).start()
        dout[h, 1] = partial(1, h)
        give_sum(h, 1).start()

    for h in range(2):
        dhalf[...] = partial(0, h)
        give_sum(h, 1).wait_recv()
        near[:, :, half_rows(h)] = (dhalf[...] + din[h, 1]).astype(BF16).reshape(4, DH, 128)

    def to_near_heads(s):
        j = lax.rem(i + s, 4)
        return remote(near.at[j], gq.at[0, i], gsend.at[s], grecv.at[i], (base + j, hd))

    for s in (1, 2, 3):
        to_near_heads(s).start()
    gq[0, pl.ds(i, 1)] = near[pl.ds(i, 1)]
    rg_ref[...] = rgb[...]
    blk_ref[...] = (mixed[...] + silu[16 : 16 + GROUP, :]).astype(BF16)
    kernel_sums()
    exchange(*z_parts)
    rz[pl.ds(z, 1)] = kpart[pl.ds(pl.multiple_of(z * 16, 16), 16), :][None]
    finish(*z_parts)
    rx[pl.ds(x, 1)] = sum((rz[a] for a in range(1, RUN)), rz[0])[None]
    exchange(*x_parts)
    for s in (1, 2, 3):
        j = lax.rem(i + 4 - s, 4)
        remote(near.at[0], gq.at[0, j], gsend.at[s], grecv.at[j], (following, hd)).wait_recv()
    for s in (1, 2, 3, 0):
        j = lax.rem(i + 4 - s, 4)
        for h in range(2):
            remote(
                cross.at[0, 0], gq.at[1, j, :, lanes(h)], csend.at[4 * h + s], crecv.at[4 * h + j],
                (following, hd),
            ).wait_recv()
    for j in range(4):
        both = gq[0, j].astype(F32) + gq[1, j].astype(F32)
        gnat[j] = both.T.astype(BF16)
        rounded = both.astype(BF16)
        gq[0, j] = rounded
        delta[j] = jnp.sum(rounded.astype(F32) * mine[j].astype(F32), axis=0, keepdims=True)
    widen(delta[...], delta_wide)

    def both_halves(half):
        return jnp.concatenate([half, half], axis=1)

    def terms(group_for, place_for):
        part[...] = jnp.zeros(part.shape, F32)
        for j in range(4):
            w, place = group_for(j), place_for(j)
            limit = block_limit(gm_ref, gl_ref, base, w, j)
            s = dot(qnat[j], win[w, 0], NN)
            inside = lax.broadcasted_iota(jnp.int32, s.shape, 1) < limit
            p = jnp.exp2(jnp.where(inside, s * SCALE2, NEG) - both_halves(lse_wide[j]))
            ds = (p * (dot(gnat[j], win[w, 1], NN) - both_halves(delta_wide[j]))).astype(BF16)
            dq[j] = dq[j] + dot(ds, knat[w], NN)
            part[place, 0] = part[place, 0] + dot(qb[j], ds, NN)
            part[place, 1] = part[place, 1] + dot(gq[0, j], p.astype(BF16), NN)
        part[:, 0] = part[:, 0] * SCALE

    def to_before(j):
        return remote(out.at[4 + j], rnext.at[i], nsend.at[j], nrecv.at[i], (earlier + j, hd))

    def before_step(s, carry):
        j = lax.rem(i + s, 4)
        terms(lambda _: 4 + j, lambda _: 0)
        out[4 + j] = part[0].astype(BF16)
        to_before(j).start()
        return carry

    lax.fori_loop(0, 2, before_step, 0)
    finish(*x_parts)
    ry[pl.ds(y, 1)] = (rx[0] + rx[1] + rx[2] + rx[3])[None]
    exchange(*y_parts)
    lax.fori_loop(2, 4, before_step, 0)
    finish(*y_parts)
    kg_ref[pl.ds(z, 1)] = (ry[0] + ry[1] + ry[2] + ry[3])[None]
    exchange(*g_parts)

    def to_across(w):
        return remote(
            out.at[w], racross.at[w], xsend.at[w], xrecv.at[w], (lax.rem(t + n - RUN, n), hd)
        )

    def own_step(s, carry):
        m = 3 - s
        terms(lambda j: jnp.where(j >= m, 8 + m, m), lambda j: jnp.where(j >= m, 0, 1))
        ownp[m] = part[0]

        @pl.when(m >= 1)
        def _():
            out[m] = part[1].astype(BF16)
            to_across(m).start()

        return carry

    lax.fori_loop(0, 4, own_step, 0)

    def give(s):
        j = lax.rem(i + s, 4)
        return remote(dqs.at[j], rq.at[i], qsend.at[s], qrecv.at[i], (base + j, hd))

    for j in range(4):
        dqs[j] = (dq[j] * SCALE).T.astype(BF16)
    for s in range(1, 4):
        give(s).start()
    rq[pl.ds(i, 1)] = dqs[pl.ds(i, 1)]

    def to_own(j):
        return remote(out.at[8 + j], rown.at[i], osend.at[j], orecv.at[i], (base + j, hd))

    for j in (0, 3, 2, 1):
        if j:
            to_across(j).wait_recv()
            out[8 + j] = (ownp[j] + racross[j].astype(F32)).astype(BF16)
        else:
            out[8 + j] = ownp[j].astype(BF16)

        @pl.when(j != i)
        def _(j=j):
            to_own(j).start()

    rown[pl.ds(i, 1)] = out[pl.ds(8 + i, 1)]
    for s in range(1, 4):
        j = lax.rem(i + 4 - s, 4)
        remote(dqs.at[0], rq.at[j], qsend.at[s], qrecv.at[j], (following, hd)).wait_recv()
    dq_ref[...] = rq[...].reshape(COLS, GROUP).T
    finish(*g_parts)
    for c in own_kv + own_q + next_kv + [cot_up, cot_down, weight] + halos:
        c.wait_send()
    for c in stat_copies + stat_copies2[0] + stat_copies2[1]:
        c.wait_send()

    @pl.when(lax.rem(hd, 2) == plane // 8)
    def _():
        to_far_core(0).wait_send()
        to_far_core(1).wait_send()

    for a in range(4):
        @pl.when(x != a)
        def _(a=a):
            over_x(a).wait_send()

        @pl.when(y != a)
        def _(a=a):
            over_y(a).wait_send()

        to_partner(0, a).wait_send()
        to_partner(1, a).wait_send()
        give_att_far(a).wait_send()
        to_far_heads(0, a).wait_send()
        to_far_heads(1, a).wait_send()
        give_sum(a // 2, a % 2).wait_send()
    for s in range(1, 4):
        onward(s).wait_send()
        give_att(s).wait_send()
        to_near_heads(s).wait_send()
        give(s).wait_send()
        to_across(s).wait_send()
    for s in range(1, 4):
        j = lax.rem(i + 4 - s, 4)
        remote(out.at[8], rown.at[j], osend.at[0], orecv.at[j], (following, hd)).wait_recv()
    for j in range(4):
        remote(out.at[4], rnext.at[j], nsend.at[0], nrecv.at[j], (following, hd)).wait_recv()
    for j in range(4):
        to_before(j).wait_send()

        @pl.when(j != i)
        def _(j=j):
            to_own(j).wait_send()


def finals(
    blk, rg, dq, kg, rown, rnext,
    block_out, residual_grad, query_grad, key_grad, value_grad, gain_grad, kernel_grad,
):
    block_out[...] = blk[...]
    residual_grad[...] = rg[...]
    query_grad[...] = dq[...]
    for a, ref in enumerate((key_grad, value_grad)):
        both = rown[:, a].astype(F32) + rnext[:, a].astype(F32)
        ref[...] = both.astype(BF16).reshape(COLS, GROUP).T
    flat = kg[...].reshape(128, 128)
    for cb in range(3):
        cols = slice(cb * 128, cb * 128 + 128)
        kernel_grad[:, cols] = flat[cb * 40 : cb * 40 + TAPS]
        gain_grad[cols] = flat[cb * 40 + TAPS]


VM = pl.BlockSpec(memory_space=pltpu.VMEM)
SM = pl.BlockSpec(memory_space=pltpu.SMEM)
HB = pl.BlockSpec(memory_space=pltpu.HBM)
DMA = pltpu.SemaphoreType.DMA


def shape(dims, kind=BF16):
    return jax.ShapeDtypeStruct(dims, kind)


def body(
    queries, key_input, value_input, residual, out_weight, norm_gain, conv_kernel, cotangent,
    group_mask, group_len,
):
    turned = (4, DH, GROUP)
    block = (GROUP, COLS)
    row = (4, 1, GROUP)
    window = (12, 2, DH, GROUP)
    pieces = (4, 2, DH, GROUP)
    longer = (GROUP + 32, COLS)
    across = (4, 16, 128)
    results = pl.pallas_call(
        conformer,
        out_shape=[
            shape(block), shape(block), shape(block), shape((8, 16, 128), F32),
            shape(pieces), shape(pieces),
        ],
        in_specs=[HB] * 6 + [VM, VM, SM, SM],
        out_specs=[VM] * 6,
        scratch_shapes=[
            pltpu.VMEM(dims, kind)
            for dims, kind in (
                ((3,) + block, BF16), (pieces, BF16), (turned, BF16), (window, BF16),
                (turned, BF16), ((12, GROUP, DH), BF16), ((4, GROUP, DH), BF16), ((4, GROUP, DH), BF16),
                ((4, GROUP, 128), F32), ((4, GROUP, 128), F32), (turned, BF16),
                (turned, F32), (row, F32), (row, F32), (row, F32), ((4,) + turned, BF16),
                ((COLS, D), BF16), ((COLS, COLS), BF16), ((16, 48, COLS), BF16),
                (block, BF16), (block, BF16), ((2, 16, COLS), BF16),
                (block, F32), (block, F32), ((GROUP, 128), F32),
                ((4, 8, GROUP), F32), ((4, 8, GROUP), F32), ((2, 4, 8, 128), F32),
                ((2, 32, COLS), F32), ((128, GROUP), F32),
                ((GROUP + 64, COLS), F32), (longer, F32), (longer, F32), (longer, F32),
                (block, F32), ((40, 8, COLS), F32), ((128, 128), F32),
                (block, BF16), ((2, 2, COLS, 128), F32), ((2, 2, COLS, 128), F32),
                ((COLS, 128), F32), (turned, BF16), ((2, 4, DH, 128), BF16),
                ((8, 16, 128), F32), (across, F32), (across, F32), ((2,) + turned, BF16),
                (row, F32), ((4, GROUP, DH), F32), (turned, BF16), (turned, BF16),
                ((2, 2, DH, GROUP), F32), (pieces, F32), (window, BF16), (pieces, BF16),
            )
        ]
        + [DMA((6,))]
        + [DMA((4,))] * 30
        + [DMA((8,))] * 12
        + [DMA((4,))] * 4
        + [DMA((9,))] * 2,
        compiler_params=pltpu.CompilerParams(
            collective_id=0, has_side_effects=True, vmem_limit_bytes=VMEM_LIMIT
        ),
        name="conformer",
    )(
        queries, key_input, value_input, out_weight, residual, cotangent,
        norm_gain, conv_kernel, group_mask.T, group_len,
    )
    return pl.pallas_call(
        finals,
        out_shape=[shape(block)] * 5 + [shape((COLS,), F32), shape((TAPS, COLS), F32)],
        in_specs=[VM] * 6,
        out_specs=[VM] * 7,
        compiler_params=pltpu.CompilerParams(vmem_limit_bytes=VMEM_LIMIT),
        name="finals",
    )(*results)


def solution(mesh):
    rows = P("tm", "heads")
    in_specs = (
        rows, rows, rows, rows, P("heads", None), P("heads"), P(None, "heads"), rows, P(), P(),
    )
    out_specs = (rows, rows, rows, rows, rows, P("heads"), P(None, "heads"))
    return jax.shard_map(body, mesh=mesh, in_specs=in_specs, out_specs=out_specs, check_vma=False)
```

```python
import jax
import jax.numpy as jnp
from jax import lax
from jax.experimental import pallas as pl
from jax.experimental.pallas import tpu as pltpu
from jax.sharding import PartitionSpec as P

D = 1536
DH = 96
GROUP = 256
COLS = 384
RUN = 8
TAPS = 32
SCALE = DH ** (-0.5)
SCALE2 = SCALE * 1.4426950408889634
NEG = -1e30
F32 = jnp.float32
BF16 = jnp.bfloat16
VMEM_LIMIT = 58 * 1024 * 1024

NT = (((1,), (1,)), ((), ()))
NN = (((1,), (0,)), ((), ()))


def dot(a, b, dims):
    return lax.dot_general(a, b, dims, preferred_element_type=F32)


def remote(src, dst, send_sem, recv_sem, where):
    return pltpu.make_async_remote_copy(
        src_ref=src,
        dst_ref=dst,
        send_sem=send_sem,
        recv_sem=recv_sem,
        device_id=where,
        device_id_type=pl.DeviceIdType.MESH,
    )


def greet(places, more):
    barrier = pltpu.get_barrier_semaphore()
    for where in places:
        pl.semaphore_signal(barrier, inc=1, device_id=where, device_id_type=pl.DeviceIdType.MESH)
    return lambda: pl.semaphore_wait(barrier, len(places) - 1 + more)


def quad_of(t, n):
    i = lax.rem(t, 4)
    base = t - i
    return i, base, lax.rem(base + 4, n), lax.rem(base + n - 4, n)


def quad_places(t, n, hd):
    i, base, following, earlier = quad_of(t, n)
    places = [(base + lax.rem(i + s, 4), hd) for s in range(1, 4)]
    places += [(following + s, hd) for s in range(4)] + [(earlier + s, hd) for s in range(4)]
    return places + [(lax.rem(t + RUN, n), hd), (lax.rem(t + n - RUN, n), hd)]


def block_limit(gm_ref, gl_ref, base, w, j):
    source = base + w - 8
    lag = 8 + j - w
    return jnp.where(source >= 0, gm_ref[lag, base + j] * gl_ref[jnp.maximum(source, 0)], 0)


def scores(k, qt, limit):
    s = dot(k, qt, NN)
    inside = lax.broadcasted_iota(jnp.int32, s.shape, 0) < limit
    return jnp.where(inside, s * SCALE2, NEG)


def head_peers(hd):
    partner = hd + 1 - 2 * lax.rem(hd, 2)
    return partner, lax.rem(hd + 2, 4), lax.rem(partner + 2, 4)


def quarter(c):
    return pl.ds(c * 64, 64)


def conformer(
    q_hbm, k_hbm, v_hbm, w_hbm, res_hbm, cot_hbm, gain_ref, ck_ref, gm_ref, gl_ref,
    blk_ref, rg_ref, dq_ref, kg_ref, rown, rnext,
    qkv, kvs, qs, win, qb, knat, qnat, gnat, lse_wide, delta_wide, mine, acc, m_s, l_s, lse, att, w_ref, wpart, wfar,
    res_ref, cot_ref, hc,
    mixed, standard, inv_ref, stats, stats2, nst, hm, turn,
    pn, cote, cg, silu, ng, kacc, kpart,
    rgb, dout, din, dhalf, near, cross, rz, rx, ry, gq, pfirst, delta, dq, dqs, rq, part, ownp, out, racross,
    load, fosend, forecv, fqsend, fqrecv, fnsend, fnrecv, fxsend, fxrecv, asend, arecv,
    gsend, grecv, nsend, nrecv, xsend, xrecv, osend, orecv, qsend, qrecv,
    bsend, brecv, wxs, wxr, wys, wyr, tsend, trecv, dsums, dsumr, csend, crecv, usend, urecv,
    zs, zr, gs, gr, hsend, hrecv, dsend, drecv, fss, xs, xr, ys, yr, ssem, rsem,
):
    t, hd = lax.axis_index("tm"), lax.axis_index("heads")
    n = lax.axis_size("tm")
    i, base, following, earlier = quad_of(t, n)
    partner, far, diag = head_peers(hd)
    after, before = lax.rem(t + 1, n), lax.rem(t + n - 1, n)
    z, x, y = lax.rem(t, RUN), lax.rem(t // RUN, 4), t // (4 * RUN)

    def along_z(a):
        return ((t - z + a), hd)

    def along_x(a):
        return ((t + (a - x) * RUN), hd)

    def along_y(a):
        return ((t + (a - y) * 4 * RUN), hd)

    places = quad_places(t, n, hd) + [(t, partner), (t, diag)]
    places += [(base + j, far) for j in range(4)]
    places += [(to, lax.rem(hd + d, 4)) for to in (after, before) for d in range(1, 4)]
    places += [along_x(lax.rem(x + d, 4)) for d in range(1, 4)]
    places += [along_y(lax.rem(y + d, 4)) for d in range(1, 4)]
    loads = [
        pltpu.make_async_copy(ref, to, load.at[a])
        for a, (ref, to) in enumerate(
            (
                (k_hbm, qkv.at[0]), (v_hbm, qkv.at[1]), (q_hbm, qkv.at[2]),
                (cot_hbm, cot_ref), (w_hbm, w_ref), (res_hbm, res_ref),
            )
        )
    ]
    for c in loads:
        c.start()
    plane = y * 4 + x
    other = 2 * (1 - hd // 2)
    core = lax.rem(hd, 2)
    sends_weights = ((z == 0) | (z == RUN - 1)) & (core == plane // 8)
    places += [(jnp.where(z < 4, t - z + RUN - 1, t - z), other + plane // 8)]
    entered = greet(places, jnp.where(sends_weights, 8, 0))
    gain = gain_ref[...].reshape(1, COLS)

    for a in range(2):
        loads[a].wait()
        kvs[:, a] = qkv[a].T.reshape(4, DH, GROUP)

    own_kv, own_q, next_kv = [], [], []
    for s in range(1, 4):
        to = lax.rem(i + s, 4)
        own_kv.append(
            remote(kvs.at[to], win.at[8 + i], fosend.at[s], forecv.at[i], (base + to, hd))
        )
        own_q.append(remote(qs.at[to], qb.at[i], fqsend.at[s], fqrecv.at[i], (base + to, hd)))
    for s in range(4):
        to = lax.rem(i + s, 4)
        next_kv.append(
            remote(kvs.at[to], win.at[4 + i], fnsend.at[s], fnrecv.at[i], (following + to, hd))
        )

    entered()
    next_kv[0].start()
    for c in own_kv:
        c.start()
    loads[2].wait()
    qs[...] = qkv[2].T.reshape(4, DH, GROUP)
    for c in own_q:
        c.start()
    next_kv[1].start()
    next_kv[2].start()
    win[pl.ds(8 + i, 1)] = kvs[pl.ds(i, 1)]
    qb[pl.ds(i, 1)] = qs[pl.ds(i, 1)]

    def onward(j):
        return remote(
            win.at[8 + j], win.at[j], fxsend.at[j], fxrecv.at[j], (lax.rem(t + RUN, n), hd)
        )

    @pl.when(i >= 1)
    def _():
        onward(i).start()

    loads[3].wait()
    loads[4].wait()
    cot_up = remote(cot_ref.at[pl.ds(GROUP - 16, 16)], hc.at[0], ssem.at[0], rsem.at[0], (after, hd))
    cot_down = remote(cot_ref.at[pl.ds(0, 16)], hc.at[1], ssem.at[1], rsem.at[1], (before, hd))
    cot_up.start()
    cot_down.start()

    def columns(h):
        return pl.ds(pl.multiple_of(h * COLS, 128), COLS)

    weight = remote(w_ref.at[:, columns(partner)], wpart, ssem.at[2], rsem.at[2], (t, partner))
    weight.start()
    sliver = pl.ds(pl.multiple_of(lax.rem(plane, 8) * 48, 16), 48)

    def to_far_core(a, k):
        return remote(
            w_ref.at[sliver, columns(other + k)], wfar.at[plane],
            fss.at[2 * a + k], rsem.at[3], (jnp.where(z == 0, t + 4 + a, t - 7 + a), other + k),
        )

    @pl.when(sends_weights)
    def _():
        for a in range(4):
            to_far_core(a, 0).start()
            to_far_core(a, 1).start()

    def over_x(a):
        return remote(wfar.at[plane], wfar.at[plane], wxs.at[a], wxr.at[x], along_x(a))

    def over_y(a):
        rows = wfar.at[pl.ds(4 * y, 4)]
        return remote(rows, rows, wys.at[a], wyr.at[y], along_y(a))

    def pass_weights(count, here, copy):
        for a in range(count):
            @pl.when(here != a)
            def _(a=a):
                copy(a).start()

    def weights_from_x():
        for a in range(4):
            @pl.when(x != a)
            def _(a=a):
                there = wfar.at[y * 4 + a]
                remote(there, there, wxs.at[a], wxr.at[a], along_x(a)).wait_recv()

    def weights_from_y():
        for a in range(4):
            @pl.when(y != a)
            def _(a=a):
                there = wfar.at[pl.ds(4 * a, 4)]
                remote(there, there, wys.at[a], wyr.at[a], along_y(a)).wait_recv()

    m_s[...] = jnp.full(m_s.shape, NEG, F32)
    l_s[...] = jnp.zeros(l_s.shape, F32)
    acc[...] = jnp.zeros(acc.shape, F32)

    for s in range(1, 4):
        j = lax.rem(i + 4 - s, 4)
        remote(kvs.at[0], win.at[8 + j], fosend.at[s], forecv.at[j], (following, hd)).wait_recv()

        @pl.when(j >= 1)
        def _(j=j):
            onward(j).start()

    for s in range(1, 4):
        j = lax.rem(i + 4 - s, 4)
        remote(qs.at[0], qb.at[j], fqsend.at[s], fqrecv.at[j], (following, hd)).wait_recv()

    next_kv[3].start()
    remote(wfar.at[plane], wfar.at[plane], ssem.at[3], rsem.at[3], (t, far)).wait_recv()
    pass_weights(4, x, over_x)

    def turn_keys(w):
        knat[w] = win[w, 0].T

    def attend_one(j, w):
        s = scores(knat[w], qb[j], block_limit(gm_ref, gl_ref, base, w, j))
        m_old = m_s[j]
        m_new = jnp.maximum(m_old, jnp.max(s, axis=0, keepdims=True))
        alpha = jnp.exp2(m_old - m_new)
        p = jnp.exp2(s - m_new)
        m_s[j] = m_new
        l_s[j] = l_s[j] * alpha + jnp.sum(p, axis=0, keepdims=True)
        acc[j] = acc[j] * alpha + dot(win[w, 1], p.astype(BF16), NN)

    def attend(group_for):
        for j in range(4):
            attend_one(j, group_for(j))

    def own_step_in(m, carry):
        @pl.when(m >= 1)
        def _():
            remote(win.at[m], win.at[m], fxsend.at[m], fxrecv.at[m], (following, hd)).wait_recv()
            turn_keys(m)

        turn_keys(8 + m)
        attend(lambda j: jnp.where(j >= m, 8 + m, m))
        return carry

    lax.fori_loop(0, 4, own_step_in, 0)
    weights_from_x()
    pass_weights(4, y, over_y)

    def arrive_before(s):
        j = lax.rem(i + 4 - s, 4)
        remote(kvs.at[0], win.at[4 + j], fnsend.at[0], fnrecv.at[j], (following, hd)).wait_recv()
        turn_keys(4 + j)
        return 4 + j

    def before_step_in(s, carry):
        w = arrive_before(s)
        attend(lambda _: w)
        return carry

    lax.fori_loop(0, 3, before_step_in, 0)
    last = arrive_before(3)

    def give_att(s):
        j = lax.rem(i + s, 4)
        return remote(mine.at[j], att.at[hd, i], asend.at[s], arecv.at[i], (base + j, hd))

    def give_att_far(s):
        j = lax.rem(i + s, 4)
        return remote(mine.at[j], att.at[hd, i], bsend.at[s], brecv.at[i], (base + j, far))

    for s in (1, 2, 3, 0):
        j = lax.rem(i + s, 4)
        attend_one(j, last)
        mine[j] = (acc[j] / l_s[j]).astype(BF16)
        give_att_far(s).start()
        if s:
            give_att(s).start()
    att[pl.ds(hd, 1), pl.ds(i, 1)] = mine[pl.ds(i, 1)][None]

    def to_partner(k, j):
        piece = att.at[far if k else hd, j]
        return remote(piece, piece, dsend.at[4 * k + j], drecv.at[4 * k + j], (t, partner))

    def from_partner(k, j):
        piece = att.at[diag if k else partner, j]
        remote(piece, piece, dsend.at[4 * k + j], drecv.at[4 * k + j], (t, partner)).wait_recv()

    to_partner(0, i).start()
    lse[...] = m_s[...] + jnp.log2(l_s[...])
    cot_up.wait_recv()
    cot_down.wait_recv()
    cote[16 : 16 + GROUP, :] = cot_ref[...].astype(F32)
    cote[0:16, :] = jnp.where(t > 0, hc[0].astype(F32), 0.0)
    cote[16 + GROUP :, :] = jnp.where(t < n - 1, hc[1].astype(F32), 0.0)
    loads[5].wait()
    weight.wait_recv()
    for s in range(1, 4):
        j = lax.rem(i + 4 - s, 4)
        remote(mine.at[0], att.at[hd, j], asend.at[s], arecv.at[j], (following, hd)).wait_recv()
        to_partner(0, j).start()
    weights_from_y()

    def weight_rows(which):
        if which == 0:
            return w_ref[:, columns(hd)]
        if which == 1:
            return wpart[...]
        k = lax.rem(hd, 2) if which == 2 else 1 - lax.rem(hd, 2)
        return wfar[pl.ds(8 * k, 8)].reshape(COLS, COLS)

    def project(which):
        shard = (hd, partner, far, diag)[which]
        there = att[pl.ds(shard, 1)].reshape(COLS, GROUP).T
        return dot(there, weight_rows(which), NN)

    mixed[...] = project(0) + res_ref[...].astype(F32)

    kacc[...] = jnp.zeros(kacc.shape, F32)
    turn[...] = jnp.zeros(turn.shape, F32)

    def turned_back(total, width):
        turn[0:8, 0:width] = total
        return turn[:, 0:width].T

    def widen(rows, wide):
        columns_of = turned_back(jnp.concatenate([rows, rows], axis=0).reshape(8, GROUP), GROUP)
        for j in range(4):
            wide[j] = jnp.broadcast_to(columns_of[:, j : j + 1], (GROUP, 128))

    widen(lse[...], lse_wide)
    for j in range(4):
        qnat[j] = qb[j].T
    dq[...] = jnp.zeros(dq.shape, F32)
    for j in range(4):
        from_partner(0, j)
    mixed[...] = mixed[...] + project(1)
    def add_piece(shard, k, j):
        rows = wfar[pl.ds(8 * k + 2 * j, 2)].reshape(DH, COLS)
        mixed[...] = mixed[...] + dot(att[shard, j].T, rows, NN)

    for s in (1, 2, 3, 0):
        j = lax.rem(i + 4 - s, 4)
        remote(mine.at[0], att.at[far, j], bsend.at[s], brecv.at[j], (following, hd)).wait_recv()
        to_partner(1, j).start()
        add_piece(far, core, j)
    for s in (1, 2, 3, 0):
        j = lax.rem(i + 4 - s, 4)
        from_partner(1, j)
        add_piece(diag, 1 - core, j)

    halos = [
        remote(mixed.at[pl.ds(GROUP - 32, 32)], hm.at[0], ssem.at[7], rsem.at[7], (after, hd)),
        remote(mixed.at[pl.ds(0, 32)], hm.at[1], ssem.at[8], rsem.at[8], (before, hd)),
    ]
    for c in halos:
        c.start()

    def row_pair(a, b):
        lane = lax.broadcasted_iota(jnp.int32, (a.shape[0], 128), 1)
        return jnp.where(lane == 0, a, jnp.where(lane == 1, b, 0.0)).T[0:8, :][None]

    def to_heads(buf, ss, rs):
        return [
            remote(buf.at[hd], buf.at[hd], ss.at[a], rs.at[a], (t, lax.rem(hd + a + 1, 4)))
            for a in (1, 2, 0)
        ]

    mx = mixed[...]
    stats[pl.ds(hd, 1)] = row_pair(
        jnp.sum(mx, axis=1, keepdims=True), jnp.sum(mx * mx, axis=1, keepdims=True)
    )
    stat_copies = to_heads(stats, tsend, trecv)
    for c in stat_copies:
        c.start()
    for side, to in ((0, after), (1, before)):
        ends = stats.at[hd, :, pl.ds(128 - 128 * side, 128)]
        for h in range(4):
            c = remote(ends, nst.at[side, hd], hsend.at[side * 4 + h], hrecv.at[side * 4 + hd], (to, h))
            c.start()
            stat_copies.append(c)
    for c in stat_copies[:3]:
        c.wait_recv()

    def norm_of(back):
        centre = back[:, 0:1] / D
        return centre, lax.rsqrt(back[:, 1:2] / D - centre * centre + 1e-05)

    centre, inverse = norm_of(turned_back(stats[0] + stats[1] + stats[2] + stats[3], GROUP))
    inv_ref[...] = jnp.broadcast_to(inverse, inv_ref.shape)
    standard[...] = (mixed[...] - centre) * inverse
    pn[32 : 32 + GROUP, :] = (standard[...] * gain).astype(BF16).astype(F32)
    for side in range(2):
        halos[side].wait_recv()
        for h in range(4):
            remote(
                stats.at[0, :, pl.ds(0, 128)], nst.at[side, h],
                hsend.at[side * 4 + h], hrecv.at[side * 4 + h], (after, hd),
            ).wait_recv()
        there = nst[side, 0] + nst[side, 1] + nst[side, 2] + nst[side, 3]
        centre, inverse = norm_of(turned_back(there, 128)[slice(96, 128) if side == 0 else slice(0, 32)])
        normed = (((hm[side] - centre) * inverse) * gain).astype(BF16).astype(F32)
        if side == 0:
            pn[0:32, :] = jnp.where(t > 0, normed, 0.0)
        else:
            pn[32 + GROUP :, :] = jnp.where(t < n - 1, normed, 0.0)

    def convolve_rows(first, last):
        for cb in range(3):
            cols = slice(cb * 128, cb * 128 + 128)

            def convolve(a, carry, cols=cols):
                begin = pl.multiple_of(a * 96, 32)
                rows = pn[pl.ds(begin, 128), cols]
                total = jnp.zeros((96, 128), F32)
                for r in range(8):
                    moved = rows[r : r + 120]
                    for b in range(4):
                        m = 8 * b + r
                        total = total + ck_ref[m : m + 1, cols] * moved[8 * b : 8 * b + 96]
                gate = jax.nn.sigmoid(total)
                silu[pl.ds(begin, 96), cols] = total * gate
                cg[pl.ds(begin, 96), cols] = (
                    cote[pl.ds(begin, 96), cols] * gate * (1.0 + total * (1.0 - gate))
                )
                return carry

            lax.fori_loop(first, last, convolve, 0)

    def correlate_rows(first, last):
        for cb in range(3):
            cols = slice(cb * 128, cb * 128 + 128)

            def correlate(a, carry, cols=cols):
                begin = pl.multiple_of(a * 64, 64)
                rows = cg[pl.ds(begin, 96), cols]
                total = jnp.zeros((64, 128), F32)
                for r in range(8):
                    moved = rows if r == 0 else rows[r : r + 88]
                    for b in range(5 if r == 0 else 4):
                        u = 8 * b + r
                        if u == 0:
                            continue
                        m = 32 - u
                        total = total + ck_ref[m : m + 1, cols] * moved[8 * b : 8 * b + 64]
                ng[pl.ds(begin, 64), cols] = total
                return carry

            lax.fori_loop(first, last, correlate, 0)

    def kernel_sums():
        for cb in range(3):
            cols = slice(cb * 128, cb * 128 + 128)

            def taps(i, carry, cols=cols):
                base = pl.multiple_of(i * 64, 64)
                prod = ng[pl.ds(base, 64), cols] * standard[pl.ds(base, 64), cols]
                kacc[TAPS, :, cols] = kacc[TAPS, :, cols] + jnp.sum(prod.reshape(8, 8, 128), axis=0)
                grad = cg[pl.ds(base + 16, 64), cols]
                normed = pn[pl.ds(base + 16, 96), cols]
                for r in range(8):
                    moved = normed[r : r + 88]
                    for a in range(4):
                        m = 8 * a + r
                        prod = grad * moved[8 * a : 8 * a + 64]
                        kacc[m, :, cols] = kacc[m, :, cols] + jnp.sum(
                            prod.reshape(8, 8, 128), axis=0
                        )
                return carry

            lax.fori_loop(0, 4, taps, 0)
        kpart[...] = jnp.zeros(kpart.shape, F32)
        summed = jnp.sum(kacc[...], axis=1)
        for cb in range(3):
            kpart[cb * 40 : cb * 40 + 40, :] = summed[:, cb * 128 : cb * 128 + 128]

    def exchange(count, here, place, source, buf, ss, rs):
        for a in range(count):
            @pl.when(here != a)
            def _(a=a):
                remote(source(a), buf.at[here], ss.at[a], rs.at[here], place(a)).start()

    def finish(count, here, place, source, buf, ss, rs):
        for a in range(count):
            @pl.when(here != a)
            def _(a=a):
                remote(source(a), buf.at[a], ss.at[a], rs.at[a], place(a)).wait()

    z_parts = (RUN, z, along_z, lambda a: kpart.at[pl.ds(16 * a, 16)], rz, zs, zr)
    x_parts = (4, x, along_x, lambda a: rx.at[x], rx, xs, xr)
    y_parts = (4, y, along_y, lambda a: ry.at[y], ry, ys, yr)
    g_parts = (RUN, z, along_z, lambda a: kg_ref.at[z], kg_ref, gs, gr)

    def lanes(h):
        return pl.ds(128 * h, 128)

    def half_rows(h):
        return slice(128 * h, 128 * h + 128)

    def half_sums(h):
        rows = half_rows(h)
        sg = ng[rows, :] * gain
        stats2[pl.ds(hd, 1), :, rows] = row_pair(
            jnp.sum(sg, axis=1, keepdims=True),
            jnp.sum(sg * standard[rows, :], axis=1, keepdims=True),
        )
        mine_here = stats2.at[hd, :, lanes(h)]
        copies = [
            remote(
                mine_here, mine_here, usend.at[4 * h + a], urecv.at[4 * h + a],
                (t, lax.rem(hd + a + 1, 4)),
            )
            for a in (1, 2, 0)
        ]
        for c in copies:
            c.start()
        return copies

    convolve_rows(0, 2)
    correlate_rows(0, 2)
    stat_copies2 = [half_sums(0)]
    convolve_rows(2, 3)
    correlate_rows(2, 4)
    stat_copies2.append(half_sums(1))

    def partial(which, h):
        return dot(weight_rows(which), rgb[half_rows(h), :], NT)

    def give_sum(h, kind):
        return remote(
            dout.at[h, kind], din.at[h, kind], dsums.at[2 * h + kind], dsumr.at[2 * h + kind],
            (t, partner),
        )

    def to_far_heads(h, s):
        j = lax.rem(i + s, 4)
        return remote(
            cross.at[h, j], gq.at[1, i, :, lanes(h)], csend.at[4 * h + s], crecv.at[4 * h + i],
            (base + j, far),
        )

    for h in range(2):
        rows = half_rows(h)
        for c in stat_copies2[h]:
            c.wait_recv()
        there = stats2[0, :, rows] + stats2[1, :, rows] + stats2[2, :, rows] + stats2[3, :, rows]
        sums = turned_back(there, 128)
        grad = cote[16 + 128 * h : 144 + 128 * h, :] + inv_ref[rows, 0:1] * (
            ng[rows, :] * gain - sums[:, 0:1] / D - standard[rows, :] * (sums[:, 1:2] / D)
        )
        rgb[rows, :] = grad.astype(BF16)
        dout[h, 0] = partial(3, h)
        give_sum(h, 0).start()
        dhalf[...] = partial(2, h)
        give_sum(h, 0).wait_recv()
        cross[h] = (dhalf[...] + din[h, 0]).astype(BF16).reshape(4, DH, 128)
        for s in (1, 2, 3, 0):
            to_far_heads(h, s).start()
        dout[h, 1] = partial(1, h)
        give_sum(h, 1).start()

    for h in range(2):
        dhalf[...] = partial(0, h)
        give_sum(h, 1).wait_recv()
        near[:, :, half_rows(h)] = (dhalf[...] + din[h, 1]).astype(BF16).reshape(4, DH, 128)

    def to_near_heads(s):
        j = lax.rem(i + s, 4)
        return remote(near.at[j], gq.at[0, i], gsend.at[s], grecv.at[i], (base + j, hd))

    for s in (1, 2, 3):
        to_near_heads(s).start()
    gq[0, pl.ds(i, 1)] = near[pl.ds(i, 1)]
    rg_ref[...] = rgb[...]
    blk_ref[...] = (mixed[...] + silu[16 : 16 + GROUP, :]).astype(BF16)
    kernel_sums()
    exchange(*z_parts)
    rz[pl.ds(z, 1)] = kpart[pl.ds(pl.multiple_of(z * 16, 16), 16), :][None]
    def both_halves(half):
        return jnp.concatenate([half, half], axis=1)

    def weights(j, w):
        s = dot(qnat[j], win[w, 0], NN)
        inside = lax.broadcasted_iota(jnp.int32, s.shape, 1) < block_limit(
            gm_ref, gl_ref, base, w, j
        )
        return jnp.exp2(jnp.where(inside, s * SCALE2, NEG) - both_halves(lse_wide[j]))

    for j in range(4):
        pfirst[j] = weights(j, 4 + i)
    finish(*z_parts)
    rx[pl.ds(x, 1)] = sum((rz[a] for a in range(1, RUN)), rz[0])[None]
    exchange(*x_parts)
    for s in (1, 2, 3):
        j = lax.rem(i + 4 - s, 4)
        remote(near.at[0], gq.at[0, j], gsend.at[s], grecv.at[j], (following, hd)).wait_recv()
    for s in (1, 2, 3, 0):
        j = lax.rem(i + 4 - s, 4)
        for h in range(2):
            remote(
                cross.at[0, 0], gq.at[1, j, :, lanes(h)], csend.at[4 * h + s], crecv.at[4 * h + j],
                (following, hd),
            ).wait_recv()
    for j in range(4):
        both = gq[0, j].astype(F32) + gq[1, j].astype(F32)
        gnat[j] = both.T.astype(BF16)
        rounded = both.astype(BF16)
        gq[0, j] = rounded
        delta[j] = jnp.sum(rounded.astype(F32) * mine[j].astype(F32), axis=0, keepdims=True)
    widen(delta[...], delta_wide)

    def terms(group_for, place_for, ready=False):
        part[...] = jnp.zeros(part.shape, F32)
        for j in range(4):
            w, place = group_for(j), place_for(j)
            p = pfirst[j] if ready else weights(j, w)
            ds = (p * (dot(gnat[j], win[w, 1], NN) - both_halves(delta_wide[j]))).astype(BF16)
            dq[j] = dq[j] + dot(ds, knat[w], NN)
            part[place, 0] = part[place, 0] + dot(qb[j], ds, NN)
            part[place, 1] = part[place, 1] + dot(gq[0, j], p.astype(BF16), NN)
        part[:, 0] = part[:, 0] * SCALE

    def to_before(j):
        return remote(out.at[4 + j], rnext.at[i], nsend.at[j], nrecv.at[i], (earlier + j, hd))

    def before_step(s, carry, ready=False):
        j = lax.rem(i + s, 4)
        terms(lambda _: 4 + j, lambda _: 0, ready)
        out[4 + j] = part[0].astype(BF16)
        to_before(j).start()
        return carry

    before_step(0, 0, True)
    lax.fori_loop(1, 2, before_step, 0)
    finish(*x_parts)
    ry[pl.ds(y, 1)] = (rx[0] + rx[1] + rx[2] + rx[3])[None]
    exchange(*y_parts)
    lax.fori_loop(2, 4, before_step, 0)
    finish(*y_parts)
    kg_ref[pl.ds(z, 1)] = (ry[0] + ry[1] + ry[2] + ry[3])[None]
    exchange(*g_parts)

    def to_across(w):
        return remote(
            out.at[w], racross.at[w], xsend.at[w], xrecv.at[w], (lax.rem(t + n - RUN, n), hd)
        )

    def own_step(s, carry):
        m = 3 - s
        terms(lambda j: jnp.where(j >= m, 8 + m, m), lambda j: jnp.where(j >= m, 0, 1))
        ownp[m] = part[0]

        @pl.when(m >= 1)
        def _():
            out[m] = part[1].astype(BF16)
            to_across(m).start()

        return carry

    lax.fori_loop(0, 4, own_step, 0)

    def give(s):
        j = lax.rem(i + s, 4)
        return remote(dqs.at[j], rq.at[i], qsend.at[s], qrecv.at[i], (base + j, hd))

    for j in range(4):
        dqs[j] = (dq[j] * SCALE).T.astype(BF16)
    for s in range(1, 4):
        give(s).start()
    rq[pl.ds(i, 1)] = dqs[pl.ds(i, 1)]

    def to_own(j):
        return remote(out.at[8 + j], rown.at[i], osend.at[j], orecv.at[i], (base + j, hd))

    for j in (0, 3, 2, 1):
        if j:
            to_across(j).wait_recv()
            out[8 + j] = (ownp[j] + racross[j].astype(F32)).astype(BF16)
        else:
            out[8 + j] = ownp[j].astype(BF16)

        @pl.when(j != i)
        def _(j=j):
            to_own(j).start()

    rown[pl.ds(i, 1)] = out[pl.ds(8 + i, 1)]
    for s in range(1, 4):
        j = lax.rem(i + 4 - s, 4)
        remote(dqs.at[0], rq.at[j], qsend.at[s], qrecv.at[j], (following, hd)).wait_recv()
    dq_ref[...] = rq[...].reshape(COLS, GROUP).T
    finish(*g_parts)
    for c in own_kv + own_q + next_kv + [cot_up, cot_down, weight] + halos:
        c.wait_send()
    for c in stat_copies + stat_copies2[0] + stat_copies2[1]:
        c.wait_send()

    @pl.when(sends_weights)
    def _():
        for a in range(4):
            to_far_core(a, 0).wait_send()
            to_far_core(a, 1).wait_send()

    for a in range(4):
        @pl.when(x != a)
        def _(a=a):
            over_x(a).wait_send()

        @pl.when(y != a)
        def _(a=a):
            over_y(a).wait_send()

        to_partner(0, a).wait_send()
        to_partner(1, a).wait_send()
        give_att_far(a).wait_send()
        to_far_heads(0, a).wait_send()
        to_far_heads(1, a).wait_send()
        give_sum(a // 2, a % 2).wait_send()
    for s in range(1, 4):
        onward(s).wait_send()
        give_att(s).wait_send()
        to_near_heads(s).wait_send()
        give(s).wait_send()
        to_across(s).wait_send()
    for s in range(1, 4):
        j = lax.rem(i + 4 - s, 4)
        remote(out.at[8], rown.at[j], osend.at[0], orecv.at[j], (following, hd)).wait_recv()
    for j in range(4):
        remote(out.at[4], rnext.at[j], nsend.at[0], nrecv.at[j], (following, hd)).wait_recv()
    for j in range(4):
        to_before(j).wait_send()

        @pl.when(j != i)
        def _(j=j):
            to_own(j).wait_send()


def finals(
    blk, rg, dq, kg, rown, rnext,
    block_out, residual_grad, query_grad, key_grad, value_grad, gain_grad, kernel_grad,
):
    block_out[...] = blk[...]
    residual_grad[...] = rg[...]
    query_grad[...] = dq[...]
    for a, ref in enumerate((key_grad, value_grad)):
        both = rown[:, a].astype(F32) + rnext[:, a].astype(F32)
        ref[...] = both.astype(BF16).reshape(COLS, GROUP).T
    flat = kg[...].reshape(128, 128)
    for cb in range(3):
        cols = slice(cb * 128, cb * 128 + 128)
        kernel_grad[:, cols] = flat[cb * 40 : cb * 40 + TAPS]
        gain_grad[cols] = flat[cb * 40 + TAPS]


VM = pl.BlockSpec(memory_space=pltpu.VMEM)
SM = pl.BlockSpec(memory_space=pltpu.SMEM)
HB = pl.BlockSpec(memory_space=pltpu.HBM)
DMA = pltpu.SemaphoreType.DMA


def shape(dims, kind=BF16):
    return jax.ShapeDtypeStruct(dims, kind)


def body(
    queries, key_input, value_input, residual, out_weight, norm_gain, conv_kernel, cotangent,
    group_mask, group_len,
):
    turned = (4, DH, GROUP)
    block = (GROUP, COLS)
    row = (4, 1, GROUP)
    window = (12, 2, DH, GROUP)
    pieces = (4, 2, DH, GROUP)
    longer = (GROUP + 32, COLS)
    across = (4, 16, 128)
    results = pl.pallas_call(
        conformer,
        out_shape=[
            shape(block), shape(block), shape(block), shape((8, 16, 128), F32),
            shape(pieces), shape(pieces),
        ],
        in_specs=[HB] * 6 + [VM, VM, SM, SM],
        out_specs=[VM] * 6,
        scratch_shapes=[
            pltpu.VMEM(dims, kind)
            for dims, kind in (
                ((3,) + block, BF16), (pieces, BF16), (turned, BF16), (window, BF16),
                (turned, BF16), ((12, GROUP, DH), BF16), ((4, GROUP, DH), BF16), ((4, GROUP, DH), BF16),
                ((4, GROUP, 128), F32), ((4, GROUP, 128), F32), (turned, BF16),
                (turned, F32), (row, F32), (row, F32), (row, F32), ((4,) + turned, BF16),
                ((COLS, D), BF16), ((COLS, COLS), BF16), ((16, 48, COLS), BF16),
                (block, BF16), (block, BF16), ((2, 16, COLS), BF16),
                (block, F32), (block, F32), ((GROUP, 128), F32),
                ((4, 8, GROUP), F32), ((4, 8, GROUP), F32), ((2, 4, 8, 128), F32),
                ((2, 32, COLS), F32), ((128, GROUP), F32),
                ((GROUP + 64, COLS), F32), (longer, F32), (longer, F32), (longer, F32),
                (block, F32), ((40, 8, COLS), F32), ((128, 128), F32),
                (block, BF16), ((2, 2, COLS, 128), F32), ((2, 2, COLS, 128), F32),
                ((COLS, 128), F32), (turned, BF16), ((2, 4, DH, 128), BF16),
                ((8, 16, 128), F32), (across, F32), (across, F32), ((2,) + turned, BF16),
                ((4, GROUP, GROUP), F32), (row, F32), ((4, GROUP, DH), F32), (turned, BF16), (turned, BF16),
                ((2, 2, DH, GROUP), F32), (pieces, F32), (window, BF16), (pieces, BF16),
            )
        ]
        + [DMA((6,))]
        + [DMA((4,))] * 30
        + [DMA((8,))] * 13
        + [DMA((4,))] * 4
        + [DMA((9,))] * 2,
        compiler_params=pltpu.CompilerParams(
            collective_id=0, has_side_effects=True, vmem_limit_bytes=VMEM_LIMIT
        ),
        name="conformer",
    )(
        queries, key_input, value_input, out_weight, residual, cotangent,
        norm_gain, conv_kernel, group_mask.T, group_len,
    )
    return pl.pallas_call(
        finals,
        out_shape=[shape(block)] * 5 + [shape((COLS,), F32), shape((TAPS, COLS), F32)],
        in_specs=[VM] * 6,
        out_specs=[VM] * 7,
        compiler_params=pltpu.CompilerParams(vmem_limit_bytes=VMEM_LIMIT),
        name="finals",
    )(*results)


def solution(mesh):
    rows = P("tm", "heads")
    in_specs = (
        rows, rows, rows, rows, P("heads", None), P("heads"), P(None, "heads"), rows, P(), P(),
    )
    out_specs = (rows, rows, rows, rows, rows, P("heads"), P(None, "heads"))
    return jax.shard_map(body, mesh=mesh, in_specs=in_specs, out_specs=out_specs, check_vma=False)
```

```python
import jax
import jax.numpy as jnp
from jax import lax
from jax.experimental import pallas as pl
from jax.experimental.pallas import tpu as pltpu
from jax.sharding import PartitionSpec as P

D = 1536
DH = 96
GROUP = 256
COLS = 384
RUN = 8
TAPS = 32
SCALE = DH ** (-0.5)
SCALE2 = SCALE * 1.4426950408889634
NEG = -1e30
F32 = jnp.float32
BF16 = jnp.bfloat16
VMEM_LIMIT = 58 * 1024 * 1024

NT = (((1,), (1,)), ((), ()))
NN = (((1,), (0,)), ((), ()))


def dot(a, b, dims):
    return lax.dot_general(a, b, dims, preferred_element_type=F32)


def remote(src, dst, send_sem, recv_sem, where):
    return pltpu.make_async_remote_copy(
        src_ref=src,
        dst_ref=dst,
        send_sem=send_sem,
        recv_sem=recv_sem,
        device_id=where,
        device_id_type=pl.DeviceIdType.MESH,
    )


def greet(places, more):
    barrier = pltpu.get_barrier_semaphore()
    for where in places:
        pl.semaphore_signal(barrier, inc=1, device_id=where, device_id_type=pl.DeviceIdType.MESH)
    return lambda: pl.semaphore_wait(barrier, len(places) - 1 + more)


def quad_of(t, n):
    i = lax.rem(t, 4)
    base = t - i
    return i, base, lax.rem(base + 4, n), lax.rem(base + n - 4, n)


def quad_places(t, n, hd):
    i, base, following, earlier = quad_of(t, n)
    places = [(base + lax.rem(i + s, 4), hd) for s in range(1, 4)]
    places += [(following + s, hd) for s in range(4)] + [(earlier + s, hd) for s in range(4)]
    return places + [(lax.rem(t + RUN, n), hd), (lax.rem(t + n - RUN, n), hd)]


def block_limit(gm_ref, gl_ref, base, w, j):
    source = base + w - 8
    lag = 8 + j - w
    return jnp.where(source >= 0, gm_ref[lag, base + j] * gl_ref[jnp.maximum(source, 0)], 0)


def scores(k, qt, limit):
    s = dot(k, qt, NN)
    inside = lax.broadcasted_iota(jnp.int32, s.shape, 0) < limit
    return jnp.where(inside, s * SCALE2, NEG)


def head_peers(hd):
    partner = hd + 1 - 2 * lax.rem(hd, 2)
    return partner, lax.rem(hd + 2, 4), lax.rem(partner + 2, 4)


def quarter(c):
    return pl.ds(c * 64, 64)


def conformer(
    q_hbm, k_hbm, v_hbm, w_hbm, res_hbm, cot_hbm, gain_ref, ck_ref, gm_ref, gl_ref,
    blk_ref, rg_ref, dq_ref, kg_ref, rown, rnext,
    qkv, kvs, qs, win, qb, knat, qnat, gnat, lse_wide, delta_wide, mine, acc, m_s, l_s, lse, att, w_ref, wpart, wfar,
    res_ref, cot_ref, hc,
    mixed, standard, inv_ref, stats, stats2, nst, hm, turn,
    pn, cote, cg, silu, ng, kacc, kpart,
    rgb, dout, din, dhalf, near, cross, rz, rx, ry, gq, pfirst, delta, dq, dqs, rq, part, ownp, out, racross,
    load, fosend, forecv, fqsend, fqrecv, fnsend, fnrecv, fxsend, fxrecv, asend, arecv,
    nsend, nrecv, xsend, xrecv, osend, orecv, qsend, qrecv,
    bsend, brecv, wxs, wxr, wys, wyr, tsend, trecv, dsums, dsumr, csend, crecv, usend, urecv,
    zs, zr, gs, gr, hsend, hrecv, dsend, drecv, fss, gsend, grecv, xs, xr, ys, yr, ssem, rsem,
):
    t, hd = lax.axis_index("tm"), lax.axis_index("heads")
    n = lax.axis_size("tm")
    i, base, following, earlier = quad_of(t, n)
    partner, far, diag = head_peers(hd)
    after, before = lax.rem(t + 1, n), lax.rem(t + n - 1, n)
    z, x, y = lax.rem(t, RUN), lax.rem(t // RUN, 4), t // (4 * RUN)

    def along_z(a):
        return ((t - z + a), hd)

    def along_x(a):
        return ((t + (a - x) * RUN), hd)

    def along_y(a):
        return ((t + (a - y) * 4 * RUN), hd)

    places = quad_places(t, n, hd) + [(t, partner), (t, diag)]
    places += [(base + j, far) for j in range(4)]
    places += [(to, lax.rem(hd + d, 4)) for to in (after, before) for d in range(1, 4)]
    places += [along_x(lax.rem(x + d, 4)) for d in range(1, 4)]
    places += [along_y(lax.rem(y + d, 4)) for d in range(1, 4)]
    loads = [
        pltpu.make_async_copy(ref, to, load.at[a])
        for a, (ref, to) in enumerate(
            (
                (k_hbm, qkv.at[0]), (v_hbm, qkv.at[1]), (q_hbm, qkv.at[2]),
                (cot_hbm, cot_ref), (w_hbm, w_ref), (res_hbm, res_ref),
            )
        )
    ]
    for c in loads:
        c.start()
    plane = y * 4 + x
    other = 2 * (1 - hd // 2)
    core = lax.rem(hd, 2)
    sends_weights = ((z == 0) | (z == RUN - 1)) & (core == plane // 8)
    places += [(jnp.where(z < 4, t - z + RUN - 1, t - z), other + plane // 8)]
    entered = greet(places, jnp.where(sends_weights, 8, 0))
    gain = gain_ref[...].reshape(1, COLS)

    for a in range(2):
        loads[a].wait()
        kvs[:, a] = qkv[a].T.reshape(4, DH, GROUP)

    own_kv, own_q, next_kv = [], [], []
    for s in range(1, 4):
        to = lax.rem(i + s, 4)
        own_kv.append(
            remote(kvs.at[to], win.at[8 + i], fosend.at[s], forecv.at[i], (base + to, hd))
        )
        own_q.append(remote(qs.at[to], qb.at[i], fqsend.at[s], fqrecv.at[i], (base + to, hd)))
    for s in range(4):
        to = lax.rem(i + s, 4)
        next_kv.append(
            remote(kvs.at[to], win.at[4 + i], fnsend.at[s], fnrecv.at[i], (following + to, hd))
        )

    entered()
    next_kv[0].start()
    for c in own_kv:
        c.start()
    loads[2].wait()
    qs[...] = qkv[2].T.reshape(4, DH, GROUP)
    for c in own_q:
        c.start()
    next_kv[1].start()
    next_kv[2].start()
    win[pl.ds(8 + i, 1)] = kvs[pl.ds(i, 1)]
    qb[pl.ds(i, 1)] = qs[pl.ds(i, 1)]

    def onward(j):
        return remote(
            win.at[8 + j], win.at[j], fxsend.at[j], fxrecv.at[j], (lax.rem(t + RUN, n), hd)
        )

    @pl.when(i >= 1)
    def _():
        onward(i).start()

    loads[3].wait()
    loads[4].wait()
    cot_up = remote(cot_ref.at[pl.ds(GROUP - 16, 16)], hc.at[0], ssem.at[0], rsem.at[0], (after, hd))
    cot_down = remote(cot_ref.at[pl.ds(0, 16)], hc.at[1], ssem.at[1], rsem.at[1], (before, hd))
    cot_up.start()
    cot_down.start()

    def columns(h):
        return pl.ds(pl.multiple_of(h * COLS, 128), COLS)

    weight = remote(w_ref.at[:, columns(partner)], wpart, ssem.at[2], rsem.at[2], (t, partner))
    weight.start()
    sliver = pl.ds(pl.multiple_of(lax.rem(plane, 8) * 48, 16), 48)

    def to_far_core(a, k):
        return remote(
            w_ref.at[sliver, columns(other + k)], wfar.at[plane],
            fss.at[2 * a + k], rsem.at[3], (jnp.where(z == 0, t + 4 + a, t - 7 + a), other + k),
        )

    @pl.when(sends_weights)
    def _():
        for a in range(4):
            to_far_core(a, 0).start()
            to_far_core(a, 1).start()

    def over_x(a):
        return remote(wfar.at[plane], wfar.at[plane], wxs.at[a], wxr.at[x], along_x(a))

    def over_y(a):
        rows = wfar.at[pl.ds(4 * y, 4)]
        return remote(rows, rows, wys.at[a], wyr.at[y], along_y(a))

    def pass_weights(count, here, copy):
        for a in range(count):
            @pl.when(here != a)
            def _(a=a):
                copy(a).start()

    def weights_from_x():
        for a in range(4):
            @pl.when(x != a)
            def _(a=a):
                there = wfar.at[y * 4 + a]
                remote(there, there, wxs.at[a], wxr.at[a], along_x(a)).wait_recv()

    def weights_from_y():
        for a in range(4):
            @pl.when(y != a)
            def _(a=a):
                there = wfar.at[pl.ds(4 * a, 4)]
                remote(there, there, wys.at[a], wyr.at[a], along_y(a)).wait_recv()

    m_s[...] = jnp.full(m_s.shape, NEG, F32)
    l_s[...] = jnp.zeros(l_s.shape, F32)
    acc[...] = jnp.zeros(acc.shape, F32)

    for s in range(1, 4):
        j = lax.rem(i + 4 - s, 4)
        remote(kvs.at[0], win.at[8 + j], fosend.at[s], forecv.at[j], (following, hd)).wait_recv()

        @pl.when(j >= 1)
        def _(j=j):
            onward(j).start()

    for s in range(1, 4):
        j = lax.rem(i + 4 - s, 4)
        remote(qs.at[0], qb.at[j], fqsend.at[s], fqrecv.at[j], (following, hd)).wait_recv()

    remote(wfar.at[plane], wfar.at[plane], ssem.at[3], rsem.at[3], (t, far)).wait_recv()
    pass_weights(4, x, over_x)

    def turn_keys(w):
        knat[w] = win[w, 0].T

    def attend_one(j, w):
        s = scores(knat[w], qb[j], block_limit(gm_ref, gl_ref, base, w, j))
        m_old = m_s[j]
        m_new = jnp.maximum(m_old, jnp.max(s, axis=0, keepdims=True))
        alpha = jnp.exp2(m_old - m_new)
        p = jnp.exp2(s - m_new)
        m_s[j] = m_new
        l_s[j] = l_s[j] * alpha + jnp.sum(p, axis=0, keepdims=True)
        acc[j] = acc[j] * alpha + dot(win[w, 1], p.astype(BF16), NN)

    def attend(group_for):
        for j in range(4):
            attend_one(j, group_for(j))

    def own_step_in(m, carry):
        @pl.when(m >= 1)
        def _():
            remote(win.at[m], win.at[m], fxsend.at[m], fxrecv.at[m], (following, hd)).wait_recv()
            turn_keys(m)

        turn_keys(8 + m)
        attend(lambda j: jnp.where(j >= m, 8 + m, m))
        return carry

    lax.fori_loop(0, 4, own_step_in, 0)
    weights_from_x()
    pass_weights(4, y, over_y)
    next_kv[0].wait_send()
    next_kv[3].start()

    def arrive_before(s):
        j = lax.rem(i + 4 - s, 4)
        remote(kvs.at[0], win.at[4 + j], fnsend.at[0], fnrecv.at[j], (following, hd)).wait_recv()
        turn_keys(4 + j)
        return 4 + j

    def before_step_in(s, carry):
        w = arrive_before(s)
        attend(lambda _: w)
        return carry

    lax.fori_loop(0, 3, before_step_in, 0)
    last = arrive_before(3)

    def give_att(s):
        j = lax.rem(i + s, 4)
        return remote(mine.at[j], att.at[hd, i], asend.at[s], arecv.at[i], (base + j, hd))

    def give_att_far(s):
        j = lax.rem(i + s, 4)
        return remote(mine.at[j], att.at[hd, i], bsend.at[s], brecv.at[i], (base + j, far))

    for s in (1, 2, 3, 0):
        j = lax.rem(i + s, 4)
        attend_one(j, last)
        mine[j] = (acc[j] / l_s[j]).astype(BF16)
        give_att_far(s).start()
        if s:
            give_att(s).start()
    att[pl.ds(hd, 1), pl.ds(i, 1)] = mine[pl.ds(i, 1)][None]

    def to_partner(k, j):
        piece = att.at[far if k else hd, j]
        return remote(piece, piece, dsend.at[4 * k + j], drecv.at[4 * k + j], (t, partner))

    def from_partner(k, j):
        piece = att.at[diag if k else partner, j]
        remote(piece, piece, dsend.at[4 * k + j], drecv.at[4 * k + j], (t, partner)).wait_recv()

    to_partner(0, i).start()
    lse[...] = m_s[...] + jnp.log2(l_s[...])
    cot_up.wait_recv()
    cot_down.wait_recv()
    cote[16 : 16 + GROUP, :] = cot_ref[...].astype(F32)
    cote[0:16, :] = jnp.where(t > 0, hc[0].astype(F32), 0.0)
    cote[16 + GROUP :, :] = jnp.where(t < n - 1, hc[1].astype(F32), 0.0)
    loads[5].wait()
    weight.wait_recv()
    for s in range(1, 4):
        j = lax.rem(i + 4 - s, 4)
        remote(mine.at[0], att.at[hd, j], asend.at[s], arecv.at[j], (following, hd)).wait_recv()
        to_partner(0, j).start()
    weights_from_y()

    def weight_rows(which):
        if which == 0:
            return w_ref[:, columns(hd)]
        if which == 1:
            return wpart[...]
        k = lax.rem(hd, 2) if which == 2 else 1 - lax.rem(hd, 2)
        return wfar[pl.ds(8 * k, 8)].reshape(COLS, COLS)

    def project(which):
        shard = (hd, partner, far, diag)[which]
        there = att[pl.ds(shard, 1)].reshape(COLS, GROUP).T
        return dot(there, weight_rows(which), NN)

    mixed[...] = project(0) + res_ref[...].astype(F32)

    kacc[...] = jnp.zeros(kacc.shape, F32)
    turn[...] = jnp.zeros(turn.shape, F32)

    def turned_back(total, width):
        turn[0:8, 0:width] = total
        return turn[:, 0:width].T

    def widen(rows, wide):
        columns_of = turned_back(jnp.concatenate([rows, rows], axis=0).reshape(8, GROUP), GROUP)
        for j in range(4):
            wide[j] = jnp.broadcast_to(columns_of[:, j : j + 1], (GROUP, 128))

    widen(lse[...], lse_wide)
    for j in range(4):
        qnat[j] = qb[j].T
    dq[...] = jnp.zeros(dq.shape, F32)
    for j in range(4):
        from_partner(0, j)
    mixed[...] = mixed[...] + project(1)
    def add_piece(shard, k, j):
        rows = wfar[pl.ds(8 * k + 2 * j, 2)].reshape(DH, COLS)
        mixed[...] = mixed[...] + dot(att[shard, j].T, rows, NN)

    for s in (1, 2, 3, 0):
        j = lax.rem(i + 4 - s, 4)
        remote(mine.at[0], att.at[far, j], bsend.at[s], brecv.at[j], (following, hd)).wait_recv()
        to_partner(1, j).start()
        add_piece(far, core, j)
    for s in (1, 2, 3, 0):
        j = lax.rem(i + 4 - s, 4)
        from_partner(1, j)
        add_piece(diag, 1 - core, j)

    halos = [
        remote(mixed.at[pl.ds(GROUP - 32, 32)], hm.at[0], ssem.at[7], rsem.at[7], (after, hd)),
        remote(mixed.at[pl.ds(0, 32)], hm.at[1], ssem.at[8], rsem.at[8], (before, hd)),
    ]
    for c in halos:
        c.start()

    def row_pair(a, b):
        lane = lax.broadcasted_iota(jnp.int32, (a.shape[0], 128), 1)
        return jnp.where(lane == 0, a, jnp.where(lane == 1, b, 0.0)).T[0:8, :][None]

    def to_heads(buf, ss, rs):
        return [
            remote(buf.at[hd], buf.at[hd], ss.at[a], rs.at[a], (t, lax.rem(hd + a + 1, 4)))
            for a in (1, 2, 0)
        ]

    mx = mixed[...]
    stats[pl.ds(hd, 1)] = row_pair(
        jnp.sum(mx, axis=1, keepdims=True), jnp.sum(mx * mx, axis=1, keepdims=True)
    )
    stat_copies = to_heads(stats, tsend, trecv)
    for c in stat_copies:
        c.start()
    for side, to in ((0, after), (1, before)):
        ends = stats.at[hd, :, pl.ds(128 - 128 * side, 128)]
        for h in range(4):
            c = remote(ends, nst.at[side, hd], hsend.at[side * 4 + h], hrecv.at[side * 4 + hd], (to, h))
            c.start()
            stat_copies.append(c)
    for c in stat_copies[:3]:
        c.wait_recv()

    def norm_of(back):
        centre = back[:, 0:1] / D
        return centre, lax.rsqrt(back[:, 1:2] / D - centre * centre + 1e-05)

    centre, inverse = norm_of(turned_back(stats[0] + stats[1] + stats[2] + stats[3], GROUP))
    inv_ref[...] = jnp.broadcast_to(inverse, inv_ref.shape)
    standard[...] = (mixed[...] - centre) * inverse
    pn[32 : 32 + GROUP, :] = (standard[...] * gain).astype(BF16).astype(F32)
    for side in range(2):
        halos[side].wait_recv()
        for h in range(4):
            remote(
                stats.at[0, :, pl.ds(0, 128)], nst.at[side, h],
                hsend.at[side * 4 + h], hrecv.at[side * 4 + h], (after, hd),
            ).wait_recv()
        there = nst[side, 0] + nst[side, 1] + nst[side, 2] + nst[side, 3]
        centre, inverse = norm_of(turned_back(there, 128)[slice(96, 128) if side == 0 else slice(0, 32)])
        normed = (((hm[side] - centre) * inverse) * gain).astype(BF16).astype(F32)
        if side == 0:
            pn[0:32, :] = jnp.where(t > 0, normed, 0.0)
        else:
            pn[32 + GROUP :, :] = jnp.where(t < n - 1, normed, 0.0)

    def convolve_rows(first, last):
        for cb in range(3):
            cols = slice(cb * 128, cb * 128 + 128)

            def convolve(a, carry, cols=cols):
                begin = pl.multiple_of(a * 96, 32)
                rows = pn[pl.ds(begin, 128), cols]
                total = jnp.zeros((96, 128), F32)
                for r in range(8):
                    moved = rows[r : r + 120]
                    for b in range(4):
                        m = 8 * b + r
                        total = total + ck_ref[m : m + 1, cols] * moved[8 * b : 8 * b + 96]
                gate = jax.nn.sigmoid(total)
                silu[pl.ds(begin, 96), cols] = total * gate
                cg[pl.ds(begin, 96), cols] = (
                    cote[pl.ds(begin, 96), cols] * gate * (1.0 + total * (1.0 - gate))
                )
                return carry

            lax.fori_loop(first, last, convolve, 0)

    def correlate_rows(first, last):
        for cb in range(3):
            cols = slice(cb * 128, cb * 128 + 128)

            def correlate(a, carry, cols=cols):
                begin = pl.multiple_of(a * 64, 64)
                rows = cg[pl.ds(begin, 96), cols]
                total = jnp.zeros((64, 128), F32)
                for r in range(8):
                    moved = rows if r == 0 else rows[r : r + 88]
                    for b in range(5 if r == 0 else 4):
                        u = 8 * b + r
                        if u == 0:
                            continue
                        m = 32 - u
                        total = total + ck_ref[m : m + 1, cols] * moved[8 * b : 8 * b + 64]
                ng[pl.ds(begin, 64), cols] = total
                return carry

            lax.fori_loop(first, last, correlate, 0)

    def kernel_sums():
        for cb in range(3):
            cols = slice(cb * 128, cb * 128 + 128)

            def taps(i, carry, cols=cols):
                base = pl.multiple_of(i * 64, 64)
                prod = ng[pl.ds(base, 64), cols] * standard[pl.ds(base, 64), cols]
                kacc[TAPS, :, cols] = kacc[TAPS, :, cols] + jnp.sum(prod.reshape(8, 8, 128), axis=0)
                grad = cg[pl.ds(base + 16, 64), cols]
                normed = pn[pl.ds(base + 16, 96), cols]
                for r in range(8):
                    moved = normed[r : r + 88]
                    for a in range(4):
                        m = 8 * a + r
                        prod = grad * moved[8 * a : 8 * a + 64]
                        kacc[m, :, cols] = kacc[m, :, cols] + jnp.sum(
                            prod.reshape(8, 8, 128), axis=0
                        )
                return carry

            lax.fori_loop(0, 4, taps, 0)
        kpart[...] = jnp.zeros(kpart.shape, F32)
        summed = jnp.sum(kacc[...], axis=1)
        for cb in range(3):
            kpart[cb * 40 : cb * 40 + 40, :] = summed[:, cb * 128 : cb * 128 + 128]

    def exchange(count, here, place, source, buf, ss, rs):
        for a in range(count):
            @pl.when(here != a)
            def _(a=a):
                remote(source(a), buf.at[here], ss.at[a], rs.at[here], place(a)).start()

    def finish(count, here, place, source, buf, ss, rs):
        for a in range(count):
            @pl.when(here != a)
            def _(a=a):
                remote(source(a), buf.at[a], ss.at[a], rs.at[a], place(a)).wait()

    z_parts = (RUN, z, along_z, lambda a: kpart.at[pl.ds(16 * a, 16)], rz, zs, zr)
    x_parts = (4, x, along_x, lambda a: rx.at[x], rx, xs, xr)
    y_parts = (4, y, along_y, lambda a: ry.at[y], ry, ys, yr)
    g_parts = (RUN, z, along_z, lambda a: kg_ref.at[z], kg_ref, gs, gr)

    def lanes(h):
        return pl.ds(128 * h, 128)

    def half_rows(h):
        return slice(128 * h, 128 * h + 128)

    def half_sums(h):
        rows = half_rows(h)
        sg = ng[rows, :] * gain
        stats2[pl.ds(hd, 1), :, rows] = row_pair(
            jnp.sum(sg, axis=1, keepdims=True),
            jnp.sum(sg * standard[rows, :], axis=1, keepdims=True),
        )
        mine_here = stats2.at[hd, :, lanes(h)]
        copies = [
            remote(
                mine_here, mine_here, usend.at[4 * h + a], urecv.at[4 * h + a],
                (t, lax.rem(hd + a + 1, 4)),
            )
            for a in (1, 2, 0)
        ]
        for c in copies:
            c.start()
        return copies

    convolve_rows(0, 2)
    correlate_rows(0, 2)
    stat_copies2 = [half_sums(0)]
    convolve_rows(2, 3)
    correlate_rows(2, 4)
    stat_copies2.append(half_sums(1))

    def partial(which, h):
        return dot(weight_rows(which), rgb[half_rows(h), :], NT)

    def give_sum(h, kind):
        return remote(
            dout.at[h, kind], din.at[h, kind], dsums.at[2 * h + kind], dsumr.at[2 * h + kind],
            (t, partner),
        )

    def to_far_heads(h, s):
        j = lax.rem(i + s, 4)
        return remote(
            cross.at[h, j], gq.at[1, i, :, lanes(h)], csend.at[4 * h + s], crecv.at[4 * h + i],
            (base + j, far),
        )

    def to_near_heads(h, s):
        j = lax.rem(i + s, 4)
        return remote(
            near.at[j, :, lanes(h)], gq.at[0, i, :, lanes(h)], gsend.at[4 * h + s],
            grecv.at[4 * h + i], (base + j, hd),
        )

    for h in range(2):
        rows = half_rows(h)
        for c in stat_copies2[h]:
            c.wait_recv()
        there = stats2[0, :, rows] + stats2[1, :, rows] + stats2[2, :, rows] + stats2[3, :, rows]
        sums = turned_back(there, 128)
        grad = cote[16 + 128 * h : 144 + 128 * h, :] + inv_ref[rows, 0:1] * (
            ng[rows, :] * gain - sums[:, 0:1] / D - standard[rows, :] * (sums[:, 1:2] / D)
        )
        rgb[rows, :] = grad.astype(BF16)
        dout[h, 0] = partial(3, h)
        give_sum(h, 0).start()
        dhalf[...] = partial(2, h)
        give_sum(h, 0).wait_recv()
        cross[h] = (dhalf[...] + din[h, 0]).astype(BF16).reshape(4, DH, 128)
        for s in (1, 2, 3, 0):
            to_far_heads(h, s).start()
        dout[h, 1] = partial(1, h)
        give_sum(h, 1).start()
        dhalf[...] = partial(0, h)
        give_sum(h, 1).wait_recv()
        near[:, :, rows] = (dhalf[...] + din[h, 1]).astype(BF16).reshape(4, DH, 128)
        for s in (1, 2, 3):
            to_near_heads(h, s).start()
        gq[0, pl.ds(i, 1), :, rows] = near[pl.ds(i, 1), :, rows]

    rg_ref[...] = rgb[...]
    blk_ref[...] = (mixed[...] + silu[16 : 16 + GROUP, :]).astype(BF16)
    kernel_sums()
    exchange(*z_parts)
    rz[pl.ds(z, 1)] = kpart[pl.ds(pl.multiple_of(z * 16, 16), 16), :][None]
    def both_halves(half):
        return jnp.concatenate([half, half], axis=1)

    def weights(j, w):
        s = dot(qnat[j], win[w, 0], NN)
        inside = lax.broadcasted_iota(jnp.int32, s.shape, 1) < block_limit(
            gm_ref, gl_ref, base, w, j
        )
        return jnp.exp2(jnp.where(inside, s * SCALE2, NEG) - both_halves(lse_wide[j]))

    for j in range(4):
        pfirst[j] = weights(j, 4 + i)
    finish(*z_parts)
    rx[pl.ds(x, 1)] = sum((rz[a] for a in range(1, RUN)), rz[0])[None]
    exchange(*x_parts)
    def arrive_half(h):
        for s in (1, 2, 3):
            j = lax.rem(i + 4 - s, 4)
            remote(
                cross.at[0, 0], gq.at[0, j, :, lanes(h)], gsend.at[4 * h + s], grecv.at[4 * h + j],
                (following, hd),
            ).wait_recv()
        for s in (1, 2, 3, 0):
            j = lax.rem(i + 4 - s, 4)
            remote(
                cross.at[0, 0], gq.at[1, j, :, lanes(h)], csend.at[4 * h + s], crecv.at[4 * h + j],
                (following, hd),
            ).wait_recv()
        rows = half_rows(h)
        for j in range(4):
            both = gq[0, j, :, rows].astype(F32) + gq[1, j, :, rows].astype(F32)
            rounded = both.astype(BF16)
            gnat[j, rows, :] = both.T.astype(BF16)
            gq[0, j, :, rows] = rounded
            delta[j, :, rows] = jnp.sum(
                rounded.astype(F32) * mine[j, :, rows].astype(F32), axis=0, keepdims=True
            )
        turn[0:4, 0:128] = delta[:, :, rows].reshape(4, 128)
        back = turn[:, 0:128].T
        for j in range(4):
            delta_wide[j, rows, :] = jnp.broadcast_to(back[:, j : j + 1], (128, 128))

    part[...] = jnp.zeros(part.shape, F32)
    first_values, first_turned = win[4 + i, 1], knat[4 + i]
    for h in range(2):
        arrive_half(h)
        rows = half_rows(h)
        for j in range(4):
            p = pfirst[j, rows, :]
            dp = dot(gnat[j, rows, :], first_values, NN)
            ds = (p * (dp - both_halves(delta_wide[j, rows, :]))).astype(BF16)
            dq[j, rows, :] = dq[j, rows, :] + dot(ds, first_turned, NN)
            part[0, 0] = part[0, 0] + dot(qb[j, :, rows], ds, NN)
            part[0, 1] = part[0, 1] + dot(gq[0, j, :, rows], p.astype(BF16), NN)
    part[:, 0] = part[:, 0] * SCALE

    def terms(group_for, place_for):
        part[...] = jnp.zeros(part.shape, F32)
        for j in range(4):
            w, place = group_for(j), place_for(j)
            p = weights(j, w)
            ds = (p * (dot(gnat[j], win[w, 1], NN) - both_halves(delta_wide[j]))).astype(BF16)
            dq[j] = dq[j] + dot(ds, knat[w], NN)
            part[place, 0] = part[place, 0] + dot(qb[j], ds, NN)
            part[place, 1] = part[place, 1] + dot(gq[0, j], p.astype(BF16), NN)
        part[:, 0] = part[:, 0] * SCALE

    def to_before(j):
        return remote(out.at[4 + j], rnext.at[i], nsend.at[j], nrecv.at[i], (earlier + j, hd))

    def send_before(j):
        out[4 + j] = part[0].astype(BF16)
        to_before(j).start()

    def before_step(s, carry):
        j = lax.rem(i + s, 4)
        terms(lambda _: 4 + j, lambda _: 0)
        send_before(j)
        return carry

    send_before(i)
    lax.fori_loop(1, 2, before_step, 0)
    finish(*x_parts)
    ry[pl.ds(y, 1)] = (rx[0] + rx[1] + rx[2] + rx[3])[None]
    exchange(*y_parts)
    lax.fori_loop(2, 4, before_step, 0)
    finish(*y_parts)
    kg_ref[pl.ds(z, 1)] = (ry[0] + ry[1] + ry[2] + ry[3])[None]
    exchange(*g_parts)

    def to_across(w):
        return remote(
            out.at[w], racross.at[w], xsend.at[w], xrecv.at[w], (lax.rem(t + n - RUN, n), hd)
        )

    def own_step(s, carry):
        m = 3 - s
        terms(lambda j: jnp.where(j >= m, 8 + m, m), lambda j: jnp.where(j >= m, 0, 1))
        ownp[m] = part[0]

        @pl.when(m >= 1)
        def _():
            out[m] = part[1].astype(BF16)
            to_across(m).start()

        return carry

    lax.fori_loop(0, 4, own_step, 0)

    def give(s):
        j = lax.rem(i + s, 4)
        return remote(dqs.at[j], rq.at[i], qsend.at[s], qrecv.at[i], (base + j, hd))

    for j in range(4):
        dqs[j] = (dq[j] * SCALE).T.astype(BF16)
    for s in range(1, 4):
        give(s).start()
    rq[pl.ds(i, 1)] = dqs[pl.ds(i, 1)]

    def to_own(j):
        return remote(out.at[8 + j], rown.at[i], osend.at[j], orecv.at[i], (base + j, hd))

    for j in (0, 3, 2, 1):
        if j:
            to_across(j).wait_recv()
            out[8 + j] = (ownp[j] + racross[j].astype(F32)).astype(BF16)
        else:
            out[8 + j] = ownp[j].astype(BF16)

        @pl.when(j != i)
        def _(j=j):
            to_own(j).start()

    rown[pl.ds(i, 1)] = out[pl.ds(8 + i, 1)]
    for s in range(1, 4):
        j = lax.rem(i + 4 - s, 4)
        remote(dqs.at[0], rq.at[j], qsend.at[s], qrecv.at[j], (following, hd)).wait_recv()
    dq_ref[...] = rq[...].reshape(COLS, GROUP).T
    finish(*g_parts)
    for c in own_kv + own_q + next_kv[1:] + [cot_up, cot_down, weight] + halos:
        c.wait_send()
    for c in stat_copies + stat_copies2[0] + stat_copies2[1]:
        c.wait_send()

    @pl.when(sends_weights)
    def _():
        for a in range(4):
            to_far_core(a, 0).wait_send()
            to_far_core(a, 1).wait_send()

    for a in range(4):
        @pl.when(x != a)
        def _(a=a):
            over_x(a).wait_send()

        @pl.when(y != a)
        def _(a=a):
            over_y(a).wait_send()

        to_partner(0, a).wait_send()
        to_partner(1, a).wait_send()
        give_att_far(a).wait_send()
        to_far_heads(0, a).wait_send()
        to_far_heads(1, a).wait_send()
        give_sum(a // 2, a % 2).wait_send()
    for s in range(1, 4):
        onward(s).wait_send()
        give_att(s).wait_send()
        to_near_heads(0, s).wait_send()
        to_near_heads(1, s).wait_send()
        give(s).wait_send()
        to_across(s).wait_send()
    for s in range(1, 4):
        j = lax.rem(i + 4 - s, 4)
        remote(out.at[8], rown.at[j], osend.at[0], orecv.at[j], (following, hd)).wait_recv()
    for j in range(4):
        remote(out.at[4], rnext.at[j], nsend.at[0], nrecv.at[j], (following, hd)).wait_recv()
    for j in range(4):
        to_before(j).wait_send()

        @pl.when(j != i)
        def _(j=j):
            to_own(j).wait_send()


def finals(
    blk, rg, dq, kg, rown, rnext,
    block_out, residual_grad, query_grad, key_grad, value_grad, gain_grad, kernel_grad,
):
    block_out[...] = blk[...]
    residual_grad[...] = rg[...]
    query_grad[...] = dq[...]
    for a, ref in enumerate((key_grad, value_grad)):
        both = rown[:, a].astype(F32) + rnext[:, a].astype(F32)
        ref[...] = both.astype(BF16).reshape(COLS, GROUP).T
    flat = kg[...].reshape(128, 128)
    for cb in range(3):
        cols = slice(cb * 128, cb * 128 + 128)
        kernel_grad[:, cols] = flat[cb * 40 : cb * 40 + TAPS]
        gain_grad[cols] = flat[cb * 40 + TAPS]


VM = pl.BlockSpec(memory_space=pltpu.VMEM)
SM = pl.BlockSpec(memory_space=pltpu.SMEM)
HB = pl.BlockSpec(memory_space=pltpu.HBM)
DMA = pltpu.SemaphoreType.DMA


def shape(dims, kind=BF16):
    return jax.ShapeDtypeStruct(dims, kind)


def body(
    queries, key_input, value_input, residual, out_weight, norm_gain, conv_kernel, cotangent,
    group_mask, group_len,
):
    turned = (4, DH, GROUP)
    block = (GROUP, COLS)
    row = (4, 1, GROUP)
    window = (12, 2, DH, GROUP)
    pieces = (4, 2, DH, GROUP)
    longer = (GROUP + 32, COLS)
    across = (4, 16, 128)
    results = pl.pallas_call(
        conformer,
        out_shape=[
            shape(block), shape(block), shape(block), shape((8, 16, 128), F32),
            shape(pieces), shape(pieces),
        ],
        in_specs=[HB] * 6 + [VM, VM, SM, SM],
        out_specs=[VM] * 6,
        scratch_shapes=[
            pltpu.VMEM(dims, kind)
            for dims, kind in (
                ((3,) + block, BF16), (pieces, BF16), (turned, BF16), (window, BF16),
                (turned, BF16), ((12, GROUP, DH), BF16), ((4, GROUP, DH), BF16), ((4, GROUP, DH), BF16),
                ((4, GROUP, 128), F32), ((4, GROUP, 128), F32), (turned, BF16),
                (turned, F32), (row, F32), (row, F32), (row, F32), ((4,) + turned, BF16),
                ((COLS, D), BF16), ((COLS, COLS), BF16), ((16, 48, COLS), BF16),
                (block, BF16), (block, BF16), ((2, 16, COLS), BF16),
                (block, F32), (block, F32), ((GROUP, 128), F32),
                ((4, 8, GROUP), F32), ((4, 8, GROUP), F32), ((2, 4, 8, 128), F32),
                ((2, 32, COLS), F32), ((128, GROUP), F32),
                ((GROUP + 64, COLS), F32), (longer, F32), (longer, F32), (longer, F32),
                (block, F32), ((40, 8, COLS), F32), ((128, 128), F32),
                (block, BF16), ((2, 2, COLS, 128), F32), ((2, 2, COLS, 128), F32),
                ((COLS, 128), F32), (turned, BF16), ((2, 4, DH, 128), BF16),
                ((8, 16, 128), F32), (across, F32), (across, F32), ((2,) + turned, BF16),
                ((4, GROUP, GROUP), F32), (row, F32), ((4, GROUP, DH), F32), (turned, BF16), (turned, BF16),
                ((2, 2, DH, GROUP), F32), (pieces, F32), (window, BF16), (pieces, BF16),
            )
        ]
        + [DMA((6,))]
        + [DMA((4,))] * 28
        + [DMA((8,))] * 15
        + [DMA((4,))] * 4
        + [DMA((9,))] * 2,
        compiler_params=pltpu.CompilerParams(
            collective_id=0, has_side_effects=True, vmem_limit_bytes=VMEM_LIMIT
        ),
        name="conformer",
    )(
        queries, key_input, value_input, out_weight, residual, cotangent,
        norm_gain, conv_kernel, group_mask.T, group_len,
    )
    return pl.pallas_call(
        finals,
        out_shape=[shape(block)] * 5 + [shape((COLS,), F32), shape((TAPS, COLS), F32)],
        in_specs=[VM] * 6,
        out_specs=[VM] * 7,
        compiler_params=pltpu.CompilerParams(vmem_limit_bytes=VMEM_LIMIT),
        name="finals",
    )(*results)


def solution(mesh):
    rows = P("tm", "heads")
    in_specs = (
        rows, rows, rows, rows, P("heads", None), P("heads"), P(None, "heads"), rows, P(), P(),
    )
    out_specs = (rows, rows, rows, rows, rows, P("heads"), P(None, "heads"))
    return jax.shard_map(body, mesh=mesh, in_specs=in_specs, out_specs=out_specs, check_vma=False)
```

```python
import jax
import jax.numpy as jnp
from jax import lax
from jax.experimental import pallas as pl
from jax.experimental.pallas import tpu as pltpu
from jax.sharding import PartitionSpec as P

D = 1536
DH = 96
GROUP = 256
COLS = 384
RUN = 8
TAPS = 32
SCALE = DH ** (-0.5)
SCALE2 = SCALE * 1.4426950408889634
NEG = -1e30
F32 = jnp.float32
BF16 = jnp.bfloat16
VMEM_LIMIT = 58 * 1024 * 1024

NT = (((1,), (1,)), ((), ()))
NN = (((1,), (0,)), ((), ()))


def dot(a, b, dims):
    return lax.dot_general(a, b, dims, preferred_element_type=F32)


def remote(src, dst, send_sem, recv_sem, where):
    return pltpu.make_async_remote_copy(
        src_ref=src,
        dst_ref=dst,
        send_sem=send_sem,
        recv_sem=recv_sem,
        device_id=where,
        device_id_type=pl.DeviceIdType.MESH,
    )


def greet(places, more):
    barrier = pltpu.get_barrier_semaphore()
    for where in places:
        pl.semaphore_signal(barrier, inc=1, device_id=where, device_id_type=pl.DeviceIdType.MESH)
    return lambda: pl.semaphore_wait(barrier, len(places) - 1 + more)


def quad_of(t, n):
    i = lax.rem(t, 4)
    base = t - i
    return i, base, lax.rem(base + 4, n), lax.rem(base + n - 4, n)


def quad_places(t, n, hd):
    i, base, following, earlier = quad_of(t, n)
    places = [(base + lax.rem(i + s, 4), hd) for s in range(1, 4)]
    places += [(following + s, hd) for s in range(4)] + [(earlier + s, hd) for s in range(4)]
    return places + [(lax.rem(t + RUN, n), hd), (lax.rem(t + n - RUN, n), hd)]


def block_limit(gm_ref, gl_ref, base, w, j):
    source = base + w - 8
    lag = 8 + j - w
    return jnp.where(source >= 0, gm_ref[lag, base + j] * gl_ref[jnp.maximum(source, 0)], 0)


def scores(k, qt, limit):
    s = dot(k, qt, NN)
    inside = lax.broadcasted_iota(jnp.int32, s.shape, 0) < limit
    return jnp.where(inside, s * SCALE2, NEG)


def head_peers(hd):
    partner = hd + 1 - 2 * lax.rem(hd, 2)
    return partner, lax.rem(hd + 2, 4), lax.rem(partner + 2, 4)


def quarter(c):
    return pl.ds(c * 64, 64)


def conformer(
    q_hbm, k_hbm, v_hbm, w_hbm, res_hbm, cot_hbm, gain_ref, ck_ref, gm_ref, gl_ref,
    blk_ref, rg_ref, dq_ref, kg_ref, rown, rnext,
    qkv, kvs, qs, win, qb, knat, qnat, gnat, lse_wide, delta_wide, mine, acc, m_s, l_s, lse, att, w_ref, wpart, wfar,
    res_ref, cot_ref, hc,
    mixed, standard, inv_ref, stats, stats2, nst, hm, turn,
    pn, cote, cg, silu, ng, kacc, kpart,
    rgb, dout, din, dhalf, near, cross, rz, rx, ry, gq, pfirst, delta, dq, dqs, rq, part, ownp, out, racross,
    load, fosend, forecv, fqsend, fqrecv, fnsend, fnrecv, fxsend, fxrecv, asend, arecv,
    nsend, nrecv, xsend, xrecv, osend, orecv, qsend, qrecv,
    bsend, brecv, wxs, wxr, wys, wyr, tsend, trecv, dsums, dsumr, csend, crecv, usend, urecv,
    zs, zr, gs, gr, hsend, hrecv, dsend, drecv, fss, gsend, grecv, xs, xr, ys, yr, ssem, rsem,
):
    t, hd = lax.axis_index("tm"), lax.axis_index("heads")
    n = lax.axis_size("tm")
    i, base, following, earlier = quad_of(t, n)
    partner, far, diag = head_peers(hd)
    after, before = lax.rem(t + 1, n), lax.rem(t + n - 1, n)
    z, x, y = lax.rem(t, RUN), lax.rem(t // RUN, 4), t // (4 * RUN)

    def along_z(a):
        return ((t - z + a), hd)

    def along_x(a):
        return ((t + (a - x) * RUN), hd)

    def along_y(a):
        return ((t + (a - y) * 4 * RUN), hd)

    places = quad_places(t, n, hd) + [(t, partner), (t, diag)]
    places += [(base + j, far) for j in range(4)]
    places += [(to, lax.rem(hd + d, 4)) for to in (after, before) for d in range(1, 4)]
    places += [along_x(lax.rem(x + d, 4)) for d in range(1, 4)]
    places += [along_y(lax.rem(y + d, 4)) for d in range(1, 4)]
    loads = [
        pltpu.make_async_copy(ref, to, load.at[a])
        for a, (ref, to) in enumerate(
            (
                (k_hbm, qkv.at[0]), (v_hbm, qkv.at[1]), (q_hbm, qkv.at[2]),
                (cot_hbm, cot_ref), (w_hbm, w_ref), (res_hbm, res_ref),
            )
        )
    ]
    for c in loads:
        c.start()
    plane = y * 4 + x
    other = 2 * (1 - hd // 2)
    core = lax.rem(hd, 2)
    sends_weights = ((z == 0) | (z == RUN - 1)) & (core == plane // 8)
    places += [(jnp.where(z < 4, t - z + RUN - 1, t - z), other + plane // 8)]
    entered = greet(places, jnp.where(sends_weights, 8, 0))
    gain = gain_ref[...].reshape(1, COLS)

    for a in range(2):
        loads[a].wait()
        kvs[:, a] = qkv[a].T.reshape(4, DH, GROUP)

    own_kv, own_q, next_kv = [], [], []
    for s in range(1, 4):
        to = lax.rem(i + s, 4)
        own_kv.append(
            remote(kvs.at[to], win.at[8 + i], fosend.at[s], forecv.at[i], (base + to, hd))
        )
        own_q.append(remote(qs.at[to], qb.at[i], fqsend.at[s], fqrecv.at[i], (base + to, hd)))
    for s in range(4):
        to = lax.rem(i + s, 4)
        next_kv.append(
            remote(kvs.at[to], win.at[4 + i], fnsend.at[s], fnrecv.at[i], (following + to, hd))
        )

    entered()
    next_kv[0].start()
    for c in own_kv:
        c.start()
    loads[2].wait()
    qs[...] = qkv[2].T.reshape(4, DH, GROUP)
    for c in own_q:
        c.start()
    next_kv[1].start()
    next_kv[2].start()
    win[pl.ds(8 + i, 1)] = kvs[pl.ds(i, 1)]
    qb[pl.ds(i, 1)] = qs[pl.ds(i, 1)]

    def onward(j):
        return remote(
            win.at[8 + j], win.at[j], fxsend.at[j], fxrecv.at[j], (lax.rem(t + RUN, n), hd)
        )

    @pl.when(i >= 1)
    def _():
        onward(i).start()

    loads[3].wait()
    loads[4].wait()
    cot_up = remote(cot_ref.at[pl.ds(GROUP - 16, 16)], hc.at[0], ssem.at[0], rsem.at[0], (after, hd))
    cot_down = remote(cot_ref.at[pl.ds(0, 16)], hc.at[1], ssem.at[1], rsem.at[1], (before, hd))
    cot_up.start()
    cot_down.start()

    def columns(h):
        return pl.ds(pl.multiple_of(h * COLS, 128), COLS)

    weight = remote(w_ref.at[:, columns(partner)], wpart, ssem.at[2], rsem.at[2], (t, partner))
    weight.start()
    sliver = pl.ds(pl.multiple_of(lax.rem(plane, 8) * 48, 16), 48)

    def to_far_core(a, k):
        return remote(
            w_ref.at[sliver, columns(other + k)], wfar.at[plane],
            fss.at[2 * a + k], rsem.at[3], (jnp.where(z == 0, t + 4 + a, t - 7 + a), other + k),
        )

    @pl.when(sends_weights)
    def _():
        for a in range(4):
            to_far_core(a, 0).start()
            to_far_core(a, 1).start()

    def over_x(a):
        return remote(wfar.at[plane], wfar.at[plane], wxs.at[a], wxr.at[x], along_x(a))

    def over_y(a):
        rows = wfar.at[pl.ds(4 * y, 4)]
        return remote(rows, rows, wys.at[a], wyr.at[y], along_y(a))

    def pass_weights(count, here, copy):
        for a in range(count):
            @pl.when(here != a)
            def _(a=a):
                copy(a).start()

    def weights_from_x():
        for a in range(4):
            @pl.when(x != a)
            def _(a=a):
                there = wfar.at[y * 4 + a]
                remote(there, there, wxs.at[a], wxr.at[a], along_x(a)).wait_recv()

    def weights_from_y():
        for a in range(4):
            @pl.when(y != a)
            def _(a=a):
                there = wfar.at[pl.ds(4 * a, 4)]
                remote(there, there, wys.at[a], wyr.at[a], along_y(a)).wait_recv()

    m_s[...] = jnp.full(m_s.shape, NEG, F32)
    l_s[...] = jnp.zeros(l_s.shape, F32)
    acc[...] = jnp.zeros(acc.shape, F32)

    for s in range(1, 4):
        j = lax.rem(i + 4 - s, 4)
        remote(kvs.at[0], win.at[8 + j], fosend.at[s], forecv.at[j], (following, hd)).wait_recv()

        @pl.when(j >= 1)
        def _(j=j):
            onward(j).start()

    for s in range(1, 4):
        j = lax.rem(i + 4 - s, 4)
        remote(qs.at[0], qb.at[j], fqsend.at[s], fqrecv.at[j], (following, hd)).wait_recv()

    next_kv[3].start()
    remote(wfar.at[plane], wfar.at[plane], ssem.at[3], rsem.at[3], (t, far)).wait_recv()
    pass_weights(4, x, over_x)

    def turn_keys(w):
        knat[w] = win[w, 0].T

    def attend_one(j, w):
        s = scores(knat[w], qb[j], block_limit(gm_ref, gl_ref, base, w, j))
        m_old = m_s[j]
        m_new = jnp.maximum(m_old, jnp.max(s, axis=0, keepdims=True))
        alpha = jnp.exp2(m_old - m_new)
        p = jnp.exp2(s - m_new)
        m_s[j] = m_new
        l_s[j] = l_s[j] * alpha + jnp.sum(p, axis=0, keepdims=True)
        acc[j] = acc[j] * alpha + dot(win[w, 1], p.astype(BF16), NN)

    def attend(group_for):
        for j in range(4):
            attend_one(j, group_for(j))

    def own_step_in(m, carry):
        @pl.when(m >= 1)
        def _():
            remote(win.at[m], win.at[m], fxsend.at[m], fxrecv.at[m], (following, hd)).wait_recv()
            turn_keys(m)

        turn_keys(8 + m)
        attend(lambda j: jnp.where(j >= m, 8 + m, m))
        return carry

    lax.fori_loop(0, 4, own_step_in, 0)
    weights_from_x()
    pass_weights(4, y, over_y)

    def arrive_before(s):
        j = lax.rem(i + 4 - s, 4)
        remote(kvs.at[0], win.at[4 + j], fnsend.at[0], fnrecv.at[j], (following, hd)).wait_recv()
        turn_keys(4 + j)
        return 4 + j

    def before_step_in(s, carry):
        w = arrive_before(s)
        attend(lambda _: w)
        return carry

    lax.fori_loop(0, 3, before_step_in, 0)
    last = arrive_before(3)

    def give_att(s):
        j = lax.rem(i + s, 4)
        return remote(mine.at[j], att.at[hd, i], asend.at[s], arecv.at[i], (base + j, hd))

    def give_att_far(s):
        j = lax.rem(i + s, 4)
        return remote(mine.at[j], att.at[hd, i], bsend.at[s], brecv.at[i], (base + j, far))

    for s in (1, 2, 3, 0):
        j = lax.rem(i + s, 4)
        attend_one(j, last)
        mine[j] = (acc[j] / l_s[j]).astype(BF16)
        give_att_far(s).start()
        if s:
            give_att(s).start()
    att[pl.ds(hd, 1), pl.ds(i, 1)] = mine[pl.ds(i, 1)][None]

    def to_partner(k, j):
        piece = att.at[far if k else hd, j]
        return remote(piece, piece, dsend.at[4 * k + j], drecv.at[4 * k + j], (t, partner))

    def from_partner(k, j):
        piece = att.at[diag if k else partner, j]
        remote(piece, piece, dsend.at[4 * k + j], drecv.at[4 * k + j], (t, partner)).wait_recv()

    to_partner(0, i).start()
    lse[...] = m_s[...] + jnp.log2(l_s[...])
    cot_up.wait_recv()
    cot_down.wait_recv()
    cote[16 : 16 + GROUP, :] = cot_ref[...].astype(F32)
    cote[0:16, :] = jnp.where(t > 0, hc[0].astype(F32), 0.0)
    cote[16 + GROUP :, :] = jnp.where(t < n - 1, hc[1].astype(F32), 0.0)
    loads[5].wait()
    weight.wait_recv()
    for s in range(1, 4):
        j = lax.rem(i + 4 - s, 4)
        remote(mine.at[0], att.at[hd, j], asend.at[s], arecv.at[j], (following, hd)).wait_recv()
        to_partner(0, j).start()
    weights_from_y()

    def weight_rows(which):
        if which == 0:
            return w_ref[:, columns(hd)]
        if which == 1:
            return wpart[...]
        k = lax.rem(hd, 2) if which == 2 else 1 - lax.rem(hd, 2)
        return wfar[pl.ds(8 * k, 8)].reshape(COLS, COLS)

    def project(which):
        shard = (hd, partner, far, diag)[which]
        there = att[pl.ds(shard, 1)].reshape(COLS, GROUP).T
        return dot(there, weight_rows(which), NN)

    mixed[...] = project(0) + res_ref[...].astype(F32)

    kacc[...] = jnp.zeros(kacc.shape, F32)
    turn[...] = jnp.zeros(turn.shape, F32)

    def turned_back(total, width):
        turn[0:8, 0:width] = total
        return turn[:, 0:width].T

    def widen(rows, wide):
        columns_of = turned_back(jnp.concatenate([rows, rows], axis=0).reshape(8, GROUP), GROUP)
        for j in range(4):
            wide[j] = jnp.broadcast_to(columns_of[:, j : j + 1], (GROUP, 128))

    widen(lse[...], lse_wide)
    for j in range(4):
        qnat[j] = qb[j].T
    dq[...] = jnp.zeros(dq.shape, F32)
    for j in range(4):
        from_partner(0, j)
    mixed[...] = mixed[...] + project(1)
    def add_piece(shard, k, j):
        rows = wfar[pl.ds(8 * k + 2 * j, 2)].reshape(DH, COLS)
        mixed[...] = mixed[...] + dot(att[shard, j].T, rows, NN)

    for s in (1, 2, 3, 0):
        j = lax.rem(i + 4 - s, 4)
        remote(mine.at[0], att.at[far, j], bsend.at[s], brecv.at[j], (following, hd)).wait_recv()
        to_partner(1, j).start()
        add_piece(far, core, j)
    for s in (1, 2, 3, 0):
        j = lax.rem(i + 4 - s, 4)
        from_partner(1, j)
        add_piece(diag, 1 - core, j)

    halos = [
        remote(mixed.at[pl.ds(GROUP - 32, 32)], hm.at[0], ssem.at[7], rsem.at[7], (after, hd)),
        remote(mixed.at[pl.ds(0, 32)], hm.at[1], ssem.at[8], rsem.at[8], (before, hd)),
    ]
    for c in halos:
        c.start()

    def row_pair(a, b):
        lane = lax.broadcasted_iota(jnp.int32, (a.shape[0], 128), 1)
        return jnp.where(lane == 0, a, jnp.where(lane == 1, b, 0.0)).T[0:8, :][None]

    def to_heads(buf, ss, rs):
        return [
            remote(buf.at[hd], buf.at[hd], ss.at[a], rs.at[a], (t, lax.rem(hd + a + 1, 4)))
            for a in (1, 2, 0)
        ]

    mx = mixed[...]
    stats[pl.ds(hd, 1)] = row_pair(
        jnp.sum(mx, axis=1, keepdims=True), jnp.sum(mx * mx, axis=1, keepdims=True)
    )
    stat_copies = to_heads(stats, tsend, trecv)
    for c in stat_copies:
        c.start()
    for side, to in ((0, after), (1, before)):
        ends = stats.at[hd, :, pl.ds(128 - 128 * side, 128)]
        for h in range(4):
            c = remote(ends, nst.at[side, hd], hsend.at[side * 4 + h], hrecv.at[side * 4 + hd], (to, h))
            c.start()
            stat_copies.append(c)
    for c in stat_copies[:3]:
        c.wait_recv()

    def norm_of(back):
        centre = back[:, 0:1] / D
        return centre, lax.rsqrt(back[:, 1:2] / D - centre * centre + 1e-05)

    centre, inverse = norm_of(turned_back(stats[0] + stats[1] + stats[2] + stats[3], GROUP))
    inv_ref[...] = jnp.broadcast_to(inverse, inv_ref.shape)
    standard[...] = (mixed[...] - centre) * inverse
    pn[32 : 32 + GROUP, :] = (standard[...] * gain).astype(BF16).astype(F32)
    for side in range(2):
        halos[side].wait_recv()
        for h in range(4):
            remote(
                stats.at[0, :, pl.ds(0, 128)], nst.at[side, h],
                hsend.at[side * 4 + h], hrecv.at[side * 4 + h], (after, hd),
            ).wait_recv()
        there = nst[side, 0] + nst[side, 1] + nst[side, 2] + nst[side, 3]
        centre, inverse = norm_of(turned_back(there, 128)[slice(96, 128) if side == 0 else slice(0, 32)])
        normed = (((hm[side] - centre) * inverse) * gain).astype(BF16).astype(F32)
        if side == 0:
            pn[0:32, :] = jnp.where(t > 0, normed, 0.0)
        else:
            pn[32 + GROUP :, :] = jnp.where(t < n - 1, normed, 0.0)

    def convolve_rows(first, last):
        for cb in range(3):
            cols = slice(cb * 128, cb * 128 + 128)

            def convolve(a, carry, cols=cols):
                begin = pl.multiple_of(a * 96, 32)
                rows = pn[pl.ds(begin, 128), cols]
                total = jnp.zeros((96, 128), F32)
                for r in range(8):
                    moved = rows[r : r + 120]
                    for b in range(4):
                        m = 8 * b + r
                        total = total + ck_ref[m : m + 1, cols] * moved[8 * b : 8 * b + 96]
                gate = jax.nn.sigmoid(total)
                silu[pl.ds(begin, 96), cols] = total * gate
                cg[pl.ds(begin, 96), cols] = (
                    cote[pl.ds(begin, 96), cols] * gate * (1.0 + total * (1.0 - gate))
                )
                return carry

            lax.fori_loop(first, last, convolve, 0)

    def correlate_rows(first, last):
        for cb in range(3):
            cols = slice(cb * 128, cb * 128 + 128)

            def correlate(a, carry, cols=cols):
                begin = pl.multiple_of(a * 64, 64)
                rows = cg[pl.ds(begin, 96), cols]
                total = jnp.zeros((64, 128), F32)
                for r in range(8):
                    moved = rows if r == 0 else rows[r : r + 88]
                    for b in range(5 if r == 0 else 4):
                        u = 8 * b + r
                        if u == 0:
                            continue
                        m = 32 - u
                        total = total + ck_ref[m : m + 1, cols] * moved[8 * b : 8 * b + 64]
                ng[pl.ds(begin, 64), cols] = total
                return carry

            lax.fori_loop(first, last, correlate, 0)

    def kernel_sums():
        for cb in range(3):
            cols = slice(cb * 128, cb * 128 + 128)

            def taps(i, carry, cols=cols):
                base = pl.multiple_of(i * 64, 64)
                prod = ng[pl.ds(base, 64), cols] * standard[pl.ds(base, 64), cols]
                kacc[TAPS, :, cols] = kacc[TAPS, :, cols] + jnp.sum(prod.reshape(8, 8, 128), axis=0)
                grad = cg[pl.ds(base + 16, 64), cols]
                normed = pn[pl.ds(base + 16, 96), cols]
                for r in range(8):
                    moved = normed[r : r + 88]
                    for a in range(4):
                        m = 8 * a + r
                        prod = grad * moved[8 * a : 8 * a + 64]
                        kacc[m, :, cols] = kacc[m, :, cols] + jnp.sum(
                            prod.reshape(8, 8, 128), axis=0
                        )
                return carry

            lax.fori_loop(0, 4, taps, 0)
        kpart[...] = jnp.zeros(kpart.shape, F32)
        summed = jnp.sum(kacc[...], axis=1)
        for cb in range(3):
            kpart[cb * 40 : cb * 40 + 40, :] = summed[:, cb * 128 : cb * 128 + 128]

    def exchange(count, here, place, source, buf, ss, rs):
        for a in range(count):
            @pl.when(here != a)
            def _(a=a):
                remote(source(a), buf.at[here], ss.at[a], rs.at[here], place(a)).start()

    def finish(count, here, place, source, buf, ss, rs):
        for a in range(count):
            @pl.when(here != a)
            def _(a=a):
                remote(source(a), buf.at[a], ss.at[a], rs.at[a], place(a)).wait()

    z_parts = (RUN, z, along_z, lambda a: kpart.at[pl.ds(16 * a, 16)], rz, zs, zr)
    x_parts = (4, x, along_x, lambda a: rx.at[x], rx, xs, xr)
    y_parts = (4, y, along_y, lambda a: ry.at[y], ry, ys, yr)
    g_parts = (RUN, z, along_z, lambda a: kg_ref.at[z], kg_ref, gs, gr)

    def lanes(h):
        return pl.ds(128 * h, 128)

    def half_rows(h):
        return slice(128 * h, 128 * h + 128)

    def half_sums(h):
        rows = half_rows(h)
        sg = ng[rows, :] * gain
        stats2[pl.ds(hd, 1), :, rows] = row_pair(
            jnp.sum(sg, axis=1, keepdims=True),
            jnp.sum(sg * standard[rows, :], axis=1, keepdims=True),
        )
        mine_here = stats2.at[hd, :, lanes(h)]
        copies = [
            remote(
                mine_here, mine_here, usend.at[4 * h + a], urecv.at[4 * h + a],
                (t, lax.rem(hd + a + 1, 4)),
            )
            for a in (1, 2, 0)
        ]
        for c in copies:
            c.start()
        return copies

    convolve_rows(0, 2)
    correlate_rows(0, 2)
    stat_copies2 = [half_sums(0)]
    convolve_rows(2, 3)
    correlate_rows(2, 4)
    stat_copies2.append(half_sums(1))

    def partial(which, h):
        return dot(weight_rows(which), rgb[half_rows(h), :], NT)

    def give_sum(h, kind):
        return remote(
            dout.at[h, kind], din.at[h, kind], dsums.at[2 * h + kind], dsumr.at[2 * h + kind],
            (t, partner),
        )

    def to_far_heads(h, s):
        j = lax.rem(i + s, 4)
        return remote(
            cross.at[h, j], gq.at[1, i, :, lanes(h)], csend.at[4 * h + s], crecv.at[4 * h + i],
            (base + j, far),
        )

    def to_near_heads(h, s):
        j = lax.rem(i + s, 4)
        return remote(
            near.at[j, :, lanes(h)], gq.at[0, i, :, lanes(h)], gsend.at[4 * h + s],
            grecv.at[4 * h + i], (base + j, hd),
        )

    for h in range(2):
        rows = half_rows(h)
        for c in stat_copies2[h]:
            c.wait_recv()
        there = stats2[0, :, rows] + stats2[1, :, rows] + stats2[2, :, rows] + stats2[3, :, rows]
        sums = turned_back(there, 128)
        grad = cote[16 + 128 * h : 144 + 128 * h, :] + inv_ref[rows, 0:1] * (
            ng[rows, :] * gain - sums[:, 0:1] / D - standard[rows, :] * (sums[:, 1:2] / D)
        )
        rgb[rows, :] = grad.astype(BF16)
        dout[h, 0] = partial(3, h)
        give_sum(h, 0).start()
        dhalf[...] = partial(2, h)
        give_sum(h, 0).wait_recv()
        cross[h] = (dhalf[...] + din[h, 0]).astype(BF16).reshape(4, DH, 128)
        for s in (1, 2, 3, 0):
            to_far_heads(h, s).start()
        dout[h, 1] = partial(1, h)
        give_sum(h, 1).start()

    for h in range(2):
        rows = half_rows(h)
        dhalf[...] = partial(0, h)
        give_sum(h, 1).wait_recv()
        near[:, :, rows] = (dhalf[...] + din[h, 1]).astype(BF16).reshape(4, DH, 128)
        for s in (1, 2, 3):
            to_near_heads(h, s).start()
        gq[0, pl.ds(i, 1), :, rows] = near[pl.ds(i, 1), :, rows]

    rg_ref[...] = rgb[...]
    blk_ref[...] = (mixed[...] + silu[16 : 16 + GROUP, :]).astype(BF16)
    kernel_sums()
    exchange(*z_parts)
    rz[pl.ds(z, 1)] = kpart[pl.ds(pl.multiple_of(z * 16, 16), 16), :][None]
    def both_halves(half):
        return jnp.concatenate([half, half], axis=1)

    def weights(j, w):
        s = dot(qnat[j], win[w, 0], NN)
        inside = lax.broadcasted_iota(jnp.int32, s.shape, 1) < block_limit(
            gm_ref, gl_ref, base, w, j
        )
        return jnp.exp2(jnp.where(inside, s * SCALE2, NEG) - both_halves(lse_wide[j]))

    for j in range(4):
        pfirst[j] = weights(j, 4 + i)
    finish(*z_parts)
    rx[pl.ds(x, 1)] = sum((rz[a] for a in range(1, RUN)), rz[0])[None]
    exchange(*x_parts)
    def arrive_half(h):
        for s in (1, 2, 3):
            j = lax.rem(i + 4 - s, 4)
            remote(
                cross.at[0, 0], gq.at[0, j, :, lanes(h)], gsend.at[4 * h + s], grecv.at[4 * h + j],
                (following, hd),
            ).wait_recv()
        for s in (1, 2, 3, 0):
            j = lax.rem(i + 4 - s, 4)
            remote(
                cross.at[0, 0], gq.at[1, j, :, lanes(h)], csend.at[4 * h + s], crecv.at[4 * h + j],
                (following, hd),
            ).wait_recv()
        rows = half_rows(h)
        for j in range(4):
            both = gq[0, j, :, rows].astype(F32) + gq[1, j, :, rows].astype(F32)
            rounded = both.astype(BF16)
            gnat[j, rows, :] = both.T.astype(BF16)
            gq[0, j, :, rows] = rounded
            delta[j, :, rows] = jnp.sum(
                rounded.astype(F32) * mine[j, :, rows].astype(F32), axis=0, keepdims=True
            )
        turn[0:4, 0:128] = delta[:, :, rows].reshape(4, 128)
        back = turn[:, 0:128].T
        for j in range(4):
            delta_wide[j, rows, :] = jnp.broadcast_to(back[:, j : j + 1], (128, 128))

    part[...] = jnp.zeros(part.shape, F32)
    first_values, first_turned = win[4 + i, 1], knat[4 + i]
    for h in range(2):
        arrive_half(h)
        rows = half_rows(h)
        for j in range(4):
            p = pfirst[j, rows, :]
            dp = dot(gnat[j, rows, :], first_values, NN)
            ds = (p * (dp - both_halves(delta_wide[j, rows, :]))).astype(BF16)
            dq[j, rows, :] = dq[j, rows, :] + dot(ds, first_turned, NN)
            part[0, 0] = part[0, 0] + dot(qb[j, :, rows], ds, NN)
            part[0, 1] = part[0, 1] + dot(gq[0, j, :, rows], p.astype(BF16), NN)
    part[:, 0] = part[:, 0] * SCALE

    def terms(group_for, place_for):
        part[...] = jnp.zeros(part.shape, F32)
        for j in range(4):
            w, place = group_for(j), place_for(j)
            p = weights(j, w)
            ds = (p * (dot(gnat[j], win[w, 1], NN) - both_halves(delta_wide[j]))).astype(BF16)
            dq[j] = dq[j] + dot(ds, knat[w], NN)
            part[place, 0] = part[place, 0] + dot(qb[j], ds, NN)
            part[place, 1] = part[place, 1] + dot(gq[0, j], p.astype(BF16), NN)
        part[:, 0] = part[:, 0] * SCALE

    def to_before(j):
        return remote(out.at[4 + j], rnext.at[i], nsend.at[j], nrecv.at[i], (earlier + j, hd))

    def send_before(j):
        out[4 + j] = part[0].astype(BF16)
        to_before(j).start()

    def before_step(s, carry):
        j = lax.rem(i + s, 4)
        terms(lambda _: 4 + j, lambda _: 0)
        send_before(j)
        return carry

    send_before(i)
    lax.fori_loop(1, 2, before_step, 0)
    finish(*x_parts)
    ry[pl.ds(y, 1)] = (rx[0] + rx[1] + rx[2] + rx[3])[None]
    exchange(*y_parts)
    lax.fori_loop(2, 4, before_step, 0)
    finish(*y_parts)
    kg_ref[pl.ds(z, 1)] = (ry[0] + ry[1] + ry[2] + ry[3])[None]
    exchange(*g_parts)

    def to_across(w):
        return remote(
            out.at[w], racross.at[w], xsend.at[w], xrecv.at[w], (lax.rem(t + n - RUN, n), hd)
        )

    def own_step(s, carry):
        m = 3 - s
        terms(lambda j: jnp.where(j >= m, 8 + m, m), lambda j: jnp.where(j >= m, 0, 1))
        ownp[m] = part[0]

        @pl.when(m >= 1)
        def _():
            out[m] = part[1].astype(BF16)
            to_across(m).start()

        return carry

    lax.fori_loop(0, 4, own_step, 0)

    def give(s):
        j = lax.rem(i + s, 4)
        return remote(dqs.at[j], rq.at[i], qsend.at[s], qrecv.at[i], (base + j, hd))

    for j in range(4):
        dqs[j] = (dq[j] * SCALE).T.astype(BF16)
    for s in range(1, 4):
        give(s).start()
    rq[pl.ds(i, 1)] = dqs[pl.ds(i, 1)]

    def to_own(j):
        return remote(out.at[8 + j], rown.at[i], osend.at[j], orecv.at[i], (base + j, hd))

    for j in (0, 3, 2, 1):
        if j:
            to_across(j).wait_recv()
            out[8 + j] = (ownp[j] + racross[j].astype(F32)).astype(BF16)
        else:
            out[8 + j] = ownp[j].astype(BF16)

        @pl.when(j != i)
        def _(j=j):
            to_own(j).start()

    rown[pl.ds(i, 1)] = out[pl.ds(8 + i, 1)]
    for s in range(1, 4):
        j = lax.rem(i + 4 - s, 4)
        remote(dqs.at[0], rq.at[j], qsend.at[s], qrecv.at[j], (following, hd)).wait_recv()
    dq_ref[...] = rq[...].reshape(COLS, GROUP).T
    finish(*g_parts)
    for c in own_kv + own_q + next_kv + [cot_up, cot_down, weight] + halos:
        c.wait_send()
    for c in stat_copies + stat_copies2[0] + stat_copies2[1]:
        c.wait_send()

    @pl.when(sends_weights)
    def _():
        for a in range(4):
            to_far_core(a, 0).wait_send()
            to_far_core(a, 1).wait_send()

    for a in range(4):
        @pl.when(x != a)
        def _(a=a):
            over_x(a).wait_send()

        @pl.when(y != a)
        def _(a=a):
            over_y(a).wait_send()

        to_partner(0, a).wait_send()
        to_partner(1, a).wait_send()
        give_att_far(a).wait_send()
        to_far_heads(0, a).wait_send()
        to_far_heads(1, a).wait_send()
        give_sum(a // 2, a % 2).wait_send()
    for s in range(1, 4):
        onward(s).wait_send()
        give_att(s).wait_send()
        to_near_heads(0, s).wait_send()
        to_near_heads(1, s).wait_send()
        give(s).wait_send()
        to_across(s).wait_send()
    for s in range(1, 4):
        j = lax.rem(i + 4 - s, 4)
        remote(out.at[8], rown.at[j], osend.at[0], orecv.at[j], (following, hd)).wait_recv()
    for j in range(4):
        remote(out.at[4], rnext.at[j], nsend.at[0], nrecv.at[j], (following, hd)).wait_recv()
    for j in range(4):
        to_before(j).wait_send()

        @pl.when(j != i)
        def _(j=j):
            to_own(j).wait_send()


def finals(
    blk, rg, dq, kg, rown, rnext,
    block_out, residual_grad, query_grad, key_grad, value_grad, gain_grad, kernel_grad,
):
    block_out[...] = blk[...]
    residual_grad[...] = rg[...]
    query_grad[...] = dq[...]
    for a, ref in enumerate((key_grad, value_grad)):
        both = rown[:, a].astype(F32) + rnext[:, a].astype(F32)
        ref[...] = both.astype(BF16).reshape(COLS, GROUP).T
    flat = kg[...].reshape(128, 128)
    for cb in range(3):
        cols = slice(cb * 128, cb * 128 + 128)
        kernel_grad[:, cols] = flat[cb * 40 : cb * 40 + TAPS]
        gain_grad[cols] = flat[cb * 40 + TAPS]


VM = pl.BlockSpec(memory_space=pltpu.VMEM)
SM = pl.BlockSpec(memory_space=pltpu.SMEM)
HB = pl.BlockSpec(memory_space=pltpu.HBM)
DMA = pltpu.SemaphoreType.DMA


def shape(dims, kind=BF16):
    return jax.ShapeDtypeStruct(dims, kind)


def body(
    queries, key_input, value_input, residual, out_weight, norm_gain, conv_kernel, cotangent,
    group_mask, group_len,
):
    turned = (4, DH, GROUP)
    block = (GROUP, COLS)
    row = (4, 1, GROUP)
    window = (12, 2, DH, GROUP)
    pieces = (4, 2, DH, GROUP)
    longer = (GROUP + 32, COLS)
    across = (4, 16, 128)
    results = pl.pallas_call(
        conformer,
        out_shape=[
            shape(block), shape(block), shape(block), shape((8, 16, 128), F32),
            shape(pieces), shape(pieces),
        ],
        in_specs=[HB] * 6 + [VM, VM, SM, SM],
        out_specs=[VM] * 6,
        scratch_shapes=[
            pltpu.VMEM(dims, kind)
            for dims, kind in (
                ((3,) + block, BF16), (pieces, BF16), (turned, BF16), (window, BF16),
                (turned, BF16), ((12, GROUP, DH), BF16), ((4, GROUP, DH), BF16), ((4, GROUP, DH), BF16),
                ((4, GROUP, 128), F32), ((4, GROUP, 128), F32), (turned, BF16),
                (turned, F32), (row, F32), (row, F32), (row, F32), ((4,) + turned, BF16),
                ((COLS, D), BF16), ((COLS, COLS), BF16), ((16, 48, COLS), BF16),
                (block, BF16), (block, BF16), ((2, 16, COLS), BF16),
                (block, F32), (block, F32), ((GROUP, 128), F32),
                ((4, 8, GROUP), F32), ((4, 8, GROUP), F32), ((2, 4, 8, 128), F32),
                ((2, 32, COLS), F32), ((128, GROUP), F32),
                ((GROUP + 64, COLS), F32), (longer, F32), (longer, F32), (longer, F32),
                (block, F32), ((40, 8, COLS), F32), ((128, 128), F32),
                (block, BF16), ((2, 2, COLS, 128), F32), ((2, 2, COLS, 128), F32),
                ((COLS, 128), F32), (turned, BF16), ((2, 4, DH, 128), BF16),
                ((8, 16, 128), F32), (across, F32), (across, F32), ((2,) + turned, BF16),
                ((4, GROUP, GROUP), F32), (row, F32), ((4, GROUP, DH), F32), (turned, BF16), (turned, BF16),
                ((2, 2, DH, GROUP), F32), (pieces, F32), (window, BF16), (pieces, BF16),
            )
        ]
        + [DMA((6,))]
        + [DMA((4,))] * 28
        + [DMA((8,))] * 15
        + [DMA((4,))] * 4
        + [DMA((9,))] * 2,
        compiler_params=pltpu.CompilerParams(
            collective_id=0, has_side_effects=True, vmem_limit_bytes=VMEM_LIMIT
        ),
        name="conformer",
    )(
        queries, key_input, value_input, out_weight, residual, cotangent,
        norm_gain, conv_kernel, group_mask.T, group_len,
    )
    return pl.pallas_call(
        finals,
        out_shape=[shape(block)] * 5 + [shape((COLS,), F32), shape((TAPS, COLS), F32)],
        in_specs=[VM] * 6,
        out_specs=[VM] * 7,
        compiler_params=pltpu.CompilerParams(vmem_limit_bytes=VMEM_LIMIT),
        name="finals",
    )(*results)


def solution(mesh):
    rows = P("tm", "heads")
    in_specs = (
        rows, rows, rows, rows, P("heads", None), P("heads"), P(None, "heads"), rows, P(), P(),
    )
    out_specs = (rows, rows, rows, rows, rows, P("heads"), P(None, "heads"))
    return jax.shard_map(body, mesh=mesh, in_specs=in_specs, out_specs=out_specs, check_vma=False)
```
